32 devices in a mesh: videos: 4 (over z), mp: 8 (over y, x, core).
Axes of the slice: x: 2, y: 2, z: 4, core: 2. Of those that a mesh axis runs over, the one named last changes fastest.
Arguments:
- frames: bfloat16 [192, 197, 768], P(('videos', 'mp')), may hold values from -8 to 8
- cotangent: bfloat16 [192, 197, 768], P(('videos', 'mp')), may hold values from -6 to 6
- frame_video: int32 [192], P('videos'), may hold values from 0 to 11, as said below
- group_ids: int32 [12], replicated, may hold values from 0 to 5, as said below
- message_fc: bfloat16 [768, 768], P('mp'), may hold values from -0.21875 to 0.21875
- message_gain: bfloat16 [768], P('mp'), may hold values from 0.5 to 1.5
- message_shift: bfloat16 [768], P('mp'), may hold values from -1 to 1
- message_qkv: bfloat16 [768, 2304], P('mp'), may hold values from -0.3125 to 0.3125
- message_out: bfloat16 [768, 768], P('mp'), may hold values from -0.4375 to 0.4375
- pre_gain: bfloat16 [768], P('mp'), may hold values from 0.5 to 1.5
- pre_shift: bfloat16 [768], P('mp'), may hold values from -1 to 1
- attn_qkv: bfloat16 [768, 2304], P('mp'), may hold values from -0.3125 to 0.3125
- attn_out: bfloat16 [768, 768], P('mp'), may hold values from -0.625 to 0.625
- mlp_gain: bfloat16 [768], P('mp'), may hold values from 0.5 to 1.5
- mlp_shift: bfloat16 [768], P('mp'), may hold values from -1 to 1
- fc_in: bfloat16 [768, 3072], P('mp'), may hold values from -0.21875 to 0.21875
- fc_out: bfloat16 [3072, 768], P('mp'), may hold values from -0.109375 to 0.109375
Outputs:
- out_frames: bfloat16 [192, 197, 768], P(('videos', 'mp'))
- clip_loss: float32 [], replicated
- frames_grad: bfloat16 [192, 197, 768], P(('videos', 'mp'))
- grad_message_fc: bfloat16 [768, 768], P('mp')
- grad_message_gain: bfloat16 [768], P('mp')
- grad_message_shift: bfloat16 [768], P('mp')
- grad_message_qkv: bfloat16 [768, 2304], P('mp')
- grad_message_out: bfloat16 [768, 768], P('mp')
- grad_pre_gain: bfloat16 [768], P('mp')
- grad_pre_shift: bfloat16 [768], P('mp')
- grad_attn_qkv: bfloat16 [768, 2304], P('mp')
- grad_attn_out: bfloat16 [768, 768], P('mp')
- grad_mlp_gain: bfloat16 [768], P('mp')
- grad_mlp_shift: bfloat16 [768], P('mp')
- grad_fc_in: bfloat16 [768, 3072], P('mp')
- grad_fc_out: bfloat16 [3072, 768], P('mp')
The draws below stay inside these ranges and needn't reach their ends.
Inputs may be any that keep to these rules, and one draw needn't show every extreme that they name: `frame_video`: frames of index block g (frames 48 * g to 48 * (g + 1) - 1) belong to videos 3 * g to 3 * (g + 1) - 1, each video having exactly 16 frames. `group_ids`: each value names exactly two videos.
All inputs are finite; a program needn't handle non-finite values.
Results may differ from the reference program's by a relative error of at most 0.029.
Values may be sent and summed in bfloat16 or wider, within the bound.
No kernel may reach another device: no remote copies, remote signals or barrier semaphores. Data moves between devices by JAX's collectives and lax.ppermute only.
A program may use at most 192 MiB of HBM per device.

```python
import jax
import jax.numpy as jnp
from jax import lax

D = 768
HEADS = 12
FF = 3072
TPF = 197
FPV = 16
FRAMES_GRP = 48
VID_GRP = 3
VIDEOS = 12
FRAMES = 192


def draw_frames(key, part):
    noise_key, offset_key = jax.random.split(key)
    noise = jax.random.normal(noise_key, (FRAMES, TPF, D), jnp.float32)
    offset = jax.random.normal(offset_key, (FRAMES, 1, D), jnp.float32)
    return jnp.clip(noise + offset, -8.0, 8.0).astype(jnp.bfloat16)


def draw_frame_video(key, part):
    groups = VIDEOS // VID_GRP
    group_keys = jax.random.split(key, groups)
    orders = jax.vmap(lambda group_key: jax.random.permutation(group_key, FRAMES_GRP))(group_keys)
    local_ids = orders // FPV
    return (local_ids + jnp.arange(groups)[:, None] * VID_GRP).reshape(-1).astype(jnp.int32)


def draw_group_ids(key, part):
    return (jax.random.permutation(key, VIDEOS) // 2).astype(jnp.int32)


def level_of(rng, extent, shards, smallest, high):
    gain = 1.0
    for position, shards_of in shards:
        draws = jax.random.uniform(jax.random.fold_in(jax.random.fold_in(rng, 6), position), (shards_of,), jnp.float32, smallest / len(shards), high / len(shards))
        gain = gain * jnp.repeat(jnp.exp(draws), extent[position] // shards_of).reshape((-1,) + (1,) * (len(extent) - 1 - position))
    return gain


def scatter_about(rng, extent, width, limit, cuts=(), kind=jnp.bfloat16):
    values = width * jax.random.normal(rng, extent, jnp.float32)
    if cuts:
        values = values * level_of(rng, extent, cuts, -0.22, 0.18)
    return jnp.clip(values, -limit, limit).astype(kind)


def setup_inputs(seed: int = 0) -> dict:
    seeds = jax.random.split(jax.random.key(seed), 18)
    frames = draw_frames(jax.random.fold_in(seeds[17], 71), 0)
    cotangent = scatter_about(seeds[1], (FRAMES, TPF, D), 1.0, 6.0, ((0, 32),))
    frame_video = draw_frame_video(jax.random.fold_in(seeds[17], 71), 0)
    group_ids = draw_group_ids(jax.random.fold_in(seeds[17], 71), 0)
    message_fc = scatter_about(seeds[4], (D, D), D ** -0.5, 0.21875, ((0, 8),))
    message_gain = jnp.clip(1.0 + 0.1 * jax.random.normal(seeds[5], (D,), jnp.float32), 0.5, 1.5).astype(jnp.bfloat16)
    message_shift = scatter_about(seeds[6], (D,), 0.2, 1.0, ((0, 8),))
    message_qkv = scatter_about(seeds[7], (D, 3 * D), (D // 2) ** -0.5, 0.3125, ((0, 8),))
    message_out = scatter_about(seeds[8], (D, D), (D // 4) ** -0.5, 0.4375, ((0, 8),))
    pre_gain = jnp.clip(1.0 + 0.1 * jax.random.normal(seeds[9], (D,), jnp.float32), 0.5, 1.5).astype(jnp.bfloat16)
    pre_shift = scatter_about(seeds[10], (D,), 0.2, 1.0, ((0, 8),))
    attn_qkv = scatter_about(seeds[11], (D, 3 * D), (D // 2) ** -0.5, 0.3125, ((0, 8),))
    attn_out = scatter_about(seeds[12], (D, D), (D // 8) ** -0.5, 0.625, ((0, 8),))
    mlp_gain = jnp.clip(1.0 + 0.1 * jax.random.normal(seeds[13], (D,), jnp.float32), 0.5, 1.5).astype(jnp.bfloat16)
    mlp_shift = scatter_about(seeds[14], (D,), 0.2, 1.0, ((0, 8),))
    fc_in = scatter_about(seeds[15], (D, FF), D ** -0.5, 0.21875, ((0, 8),))
    fc_out = scatter_about(seeds[16], (FF, D), FF ** -0.5, 0.109375, ((0, 8),))
    return dict(frames=frames, cotangent=cotangent, frame_video=frame_video, group_ids=group_ids, message_fc=message_fc, message_gain=message_gain, message_shift=message_shift, message_qkv=message_qkv, message_out=message_out, pre_gain=pre_gain, pre_shift=pre_shift, attn_qkv=attn_qkv, attn_out=attn_out, mlp_gain=mlp_gain, mlp_shift=mlp_shift, fc_in=fc_in, fc_out=fc_out)


@jax.custom_vjp
def low(v):
    return lax.optimization_barrier(v.astype(jnp.bfloat16)).astype(jnp.float32)

@jax.custom_vjp
def low_back(v):
    return v

def low_keep(v):
    return (low(v), None)

def low_pass(kept, grad):
    return (grad,)

def back_keep(v):
    return (v, None)

def back_low(kept, grad):
    return (low(grad),)
low.defvjp(low_keep, low_pass)
low_back.defvjp(back_keep, back_low)
EPS = 1e-05
LOGIT_SCALE = 50.0

def matmul(left, right):
    return jnp.dot(left, right, precision=lax.Precision.HIGHEST, preferred_element_type=jnp.float32)

def layer_norm(values_in, gain_in, shift_in):
    row_mean = lax.optimization_barrier(jnp.mean(values_in, axis=-1, keepdims=True))
    centred = values_in - row_mean
    row_var = lax.optimization_barrier(jnp.mean(centred * centred, axis=-1, keepdims=True))
    return centred * lax.rsqrt(row_var + EPS) * gain_in + shift_in

def quick_gelu(values_in):
    return values_in * jax.nn.sigmoid(1.702 * values_in)

def contrast(pooled, group_ids):
    centred = pooled - lax.optimization_barrier(jnp.mean(pooled, axis=0, keepdims=True))
    embed = centred * lax.rsqrt(lax.optimization_barrier(jnp.sum(centred * centred, axis=1, keepdims=True)) + 1e-06)
    logits = LOGIT_SCALE * jnp.dot(embed, embed.T, precision=lax.Precision.HIGHEST)
    count_videos = pooled.shape[0]
    diagonal = jnp.arange(count_videos)[:, None] == jnp.arange(count_videos)[None, :]
    others = jnp.where(diagonal, -1e+30, logits)
    log_total = jax.nn.logsumexp(others, axis=1)
    positive = jnp.logical_and(group_ids[:, None] == group_ids[None, :], jnp.logical_not(diagonal))
    pos_count = lax.optimization_barrier(jnp.sum(positive.astype(jnp.float32), axis=1))
    pos_mean = lax.optimization_barrier(jnp.sum(jnp.where(positive, logits, 0.0), axis=1)) / pos_count
    return jnp.mean(log_total - pos_mean)

def forward(frames, frame_video, group_ids, message_fc, message_gain, message_shift, message_qkv, message_out, pre_gain, pre_shift, attn_qkv, attn_out, mlp_gain, mlp_shift, fc_in, fc_out):
    total_frames, patches, features = frames.shape
    head_dim = features // HEADS
    score_scale = head_dim ** (-0.5)
    message = low_back(matmul(frames[:, 0, :], message_fc))
    msg_act = low(layer_norm(message, message_gain, message_shift))
    msg_proj = low(low_back(matmul(msg_act, message_qkv)))
    groups = total_frames // FRAMES_GRP
    proj_groups = msg_proj.reshape(groups, FRAMES_GRP, 3 * features)
    video_groups = frame_video.reshape(groups, FRAMES_GRP)

    def message_attend(inputs):
        group_proj, video_ids = inputs
        msg_query = group_proj[:, :features].reshape(FRAMES_GRP, HEADS, head_dim)
        msg_key = group_proj[:, features:2 * features].reshape(FRAMES_GRP, HEADS, head_dim)
        msg_value = group_proj[:, 2 * features:].reshape(FRAMES_GRP, HEADS, head_dim)
        msg_scores = low_back(jnp.einsum('fhd,ghd->hfg', msg_query, msg_key, precision=lax.Precision.HIGHEST) * score_scale)
        same_video = video_ids[:, None] == video_ids[None, :]
        msg_probs = low(jax.nn.softmax(jnp.where(same_video[None], msg_scores, -1e+30), axis=-1))
        msg_mix = jnp.einsum('hfg,ghd->fhd', msg_probs, msg_value, precision=lax.Precision.HIGHEST)
        return low(low_back(msg_mix.reshape(FRAMES_GRP, features)))
    msg_mix = lax.map(jax.checkpoint(message_attend), (proj_groups, video_groups)).reshape(total_frames, features)
    msg_total = message + low_back(matmul(msg_mix, message_out))
    blocks = total_frames // FPV
    frame_blocks = frames.reshape(blocks, FPV, patches, features)
    msg_blocks = msg_total.reshape(blocks, FPV, features)

    def frame_layer(inputs):
        frame_block, msg_rows = inputs
        stacked = jnp.concatenate([frame_block, msg_rows[:, None, :]], axis=1)
        pre_act = low(layer_norm(stacked, pre_gain, pre_shift))
        qkv_all = low(low_back(matmul(pre_act.reshape(-1, features), attn_qkv))).reshape(FPV, patches + 1, 3 * features)
        frame_query = qkv_all[:, :patches, :features].reshape(FPV, patches, HEADS, head_dim)
        frame_key = qkv_all[:, :, features:2 * features].reshape(FPV, patches + 1, HEADS, head_dim)
        frame_value = qkv_all[:, :, 2 * features:].reshape(FPV, patches + 1, HEADS, head_dim)
        frame_scores = low_back(jnp.einsum('fqhd,fkhd->fhqk', frame_query, frame_key, precision=lax.Precision.HIGHEST) * score_scale)
        frame_probs = low(jax.nn.softmax(frame_scores, axis=-1))
        frame_mixed = jnp.einsum('fhqk,fkhd->fqhd', frame_probs, frame_value, precision=lax.Precision.HIGHEST)
        frame_mixed = low(low_back(frame_mixed.reshape(-1, features)))
        residual = frame_block.reshape(-1, features) + low_back(matmul(frame_mixed, attn_out))
        mlp_act = low(layer_norm(residual, mlp_gain, mlp_shift))
        hidden = low(quick_gelu(low_back(matmul(mlp_act, fc_in))))
        output = residual + low_back(matmul(hidden, fc_out))
        return output.reshape(FPV, patches, features)
    outputs = lax.map(jax.checkpoint(frame_layer), (frame_blocks, msg_blocks)).reshape(total_frames, patches, features)
    frame_mean = lax.optimization_barrier(jnp.mean(outputs, axis=1))
    pooled = jax.ops.segment_sum(frame_mean, frame_video, num_segments=VIDEOS) / FPV
    return (outputs, contrast(pooled, group_ids))

def reference(frames, cotangent, frame_video, group_ids, message_fc, message_gain, message_shift, message_qkv, message_out, pre_gain, pre_shift, attn_qkv, attn_out, mlp_gain, mlp_shift, fc_in, fc_out):
    weights = tuple((weight.astype(jnp.float32) for weight in (message_fc, message_gain, message_shift, message_qkv, message_out, pre_gain, pre_shift, attn_qkv, attn_out, mlp_gain, mlp_shift, fc_in, fc_out)))

    def objective(inputs, *params):
        return forward(inputs, frame_video, group_ids, *params)
    (outputs, clip_loss), back = jax.vjp(objective, frames.astype(jnp.float32), *weights)
    loss_weight = jnp.full_like(clip_loss, float(VIDEOS * FPV * TPF))
    grads = back((cotangent.astype(outputs.dtype), loss_weight))
    low_grads = tuple((grad_piece.astype(jnp.bfloat16) for grad_piece in grads[1:]))
    return (outputs.astype(jnp.bfloat16), clip_loss, grads[0].astype(jnp.bfloat16), low_grads[0], low_grads[1], low_grads[2], low_grads[3], low_grads[4], low_grads[5], low_grads[6], low_grads[7], low_grads[8], low_grads[9], low_grads[10], low_grads[11], low_grads[12])
```

```python
import functools

import jax
import jax.numpy as jnp
from jax import lax
from jax.experimental import pallas as pl
from jax.experimental.pallas import tpu as pltpu
from jax.sharding import PartitionSpec as P

HEADS = 12
FPV = 16
EPS = 1e-05
LOGIT_SCALE = 50.0
ROWS = 208
PACK = 128
VMEM = 60 * 1024 * 1024

f32 = jnp.float32
bf16 = jnp.bfloat16
HIGH = lax.Precision.HIGHEST


def nn(a, b, precision=None):
    return jnp.dot(a, b, preferred_element_type=f32, precision=precision)


def nt(a, b, precision=None):
    return lax.dot_general(
        a, b, (((1,), (1,)), ((), ())), preferred_element_type=f32, precision=precision
    )


def norm_parts(x):
    mean = jnp.mean(x, axis=-1, keepdims=True)
    centred = x - mean
    var = jnp.mean(centred * centred, axis=-1, keepdims=True)
    rstd = lax.rsqrt(var + EPS)
    return centred * rstd, rstd


def norm_back(grad, xhat, rstd, gain):
    gy = grad * gain
    return rstd * (
        gy
        - jnp.mean(gy, axis=-1, keepdims=True)
        - xhat * jnp.mean(gy * xhat, axis=-1, keepdims=True)
    )


def sigmoid(x):
    return 0.5 * jnp.tanh(0.5 * x) + 0.5


def lane_masks(dtype):
    lane = lax.broadcasted_iota(jnp.int32, (1, 128), 1)
    low = (lane < 64).astype(f32)
    return low.astype(dtype), (1.0 - low).astype(dtype)


def transpose(x):
    return jnp.transpose(x.astype(f32)).astype(x.dtype)


def pair_probs(q2, k2, valid):
    m0, m1 = lane_masks(bf16)
    qs = q2 * jnp.asarray(0.125, bf16)
    keys = jnp.concatenate([k2 * m0, k2 * m1], axis=0)
    scores = nt(keys, qs)
    count = k2.shape[0]
    out = []
    for j in range(2):
        s = jnp.where(valid, scores[j * count : (j + 1) * count], -1e30)
        e = jnp.exp(s - jnp.max(s, axis=0, keepdims=True))
        out.append(e * (1.0 / jnp.sum(e, axis=0, keepdims=True)))
    return out


def pair_mix(v2, p0, p1):
    vt = transpose(v2)
    mixed = jnp.concatenate([nn(vt[:64], p0), nn(vt[64:], p1)], axis=0)
    return jnp.transpose(mixed)


def pair_back(q2, k2, v2, dm2, p0, p1):
    m0, m1 = lane_masks(bf16)
    count = k2.shape[0]
    lane = lax.broadcasted_iota(jnp.int32, (1, 128), 1) < 64
    eighth = jnp.asarray(0.125, bf16)
    dps = nt(jnp.concatenate([v2 * m0, v2 * m1], axis=0), dm2)
    lows, grads = [], []
    for j, p in enumerate((p0, p1)):
        dp = dps[j * count : (j + 1) * count]
        p_full = p.astype(f32)
        row = jnp.sum(dp * p_full, axis=0, keepdims=True)
        grads.append((p_full * (dp - row)).astype(bf16))
        lows.append(p.astype(bf16))
    dv = nn(jnp.concatenate(lows, axis=0), dm2)
    dk = nn(jnp.concatenate(grads, axis=0), q2 * eighth)
    kt = transpose(k2 * eighth)
    dq = jnp.transpose(
        jnp.concatenate([nn(kt[:64], grads[0]), nn(kt[64:], grads[1])], axis=0)
    )
    return dq, jnp.where(lane, dk[:count], dk[count:]), jnp.where(lane, dv[:count], dv[count:])


def call(body, out_shape, grid, in_specs, out_specs, scratch, flops, bytes_accessed):
    return pl.pallas_call(
        body,
        out_shape=out_shape,
        grid_spec=pltpu.PrefetchScalarGridSpec(
            num_scalar_prefetch=1,
            grid=grid,
            in_specs=in_specs,
            out_specs=out_specs,
            scratch_shapes=scratch,
        ),
        compiler_params=pltpu.CompilerParams(
            dimension_semantics=("arbitrary",) * len(grid), vmem_limit_bytes=VMEM
        ),
        cost_estimate=pl.CostEstimate(
            flops=flops, bytes_accessed=bytes_accessed, transcendentals=0
        ),
    )


ANY = pl.BlockSpec(memory_space=pl.ANY)


def whole(shape):
    return pl.BlockSpec(shape, lambda i, s: (0,) * len(shape))


def per_step(shape):
    return pl.BlockSpec((1,) + shape, lambda i, s: (i,) + (0,) * len(shape))


def sds(shape, dtype):
    return jax.ShapeDtypeStruct(shape, dtype)


class Weights:
    def __init__(self, arrays, places, rows):
        self.arrays = arrays
        self.places = places
        self.rows = rows

    def copies(self, refs, me, sems, first, columns, dst):
        out = []
        for number, (ref, (slot, start, count)) in enumerate(zip(refs, self.places)):
            if slot is None:
                target = dst
            else:
                offset = jnp.bitwise_xor(me, slot) * self.rows + start
                target = dst.at[pl.ds(pl.multiple_of(offset, 16), count), :]
            out.append(
                pltpu.make_async_copy(
                    ref.at[:, pl.ds(first, columns)], target, sems.at[number]
                )
            )
        return out


def run_copies(copies):
    for copy in copies:
        copy.start()
    for copy in copies:
        copy.wait()


def swap(x, axis, size, bit):
    return lax.ppermute(x, axis, [(i, i ^ bit) for i in range(size)])


def gather_weights(x, fast, mp):
    rows = x.shape[0]
    if not fast:
        full = lax.all_gather(x, "mp", axis=0, tiled=True)
        return Weights([full], [(None, 0, rows * mp)], rows)
    half = rows // 2
    own_c = swap(x, "mp", mp, 1)
    from_x = swap(x, "mp", mp, 2)
    from_y = swap(x, "mp", mp, 4)
    diag_a = swap(from_x[:half], "mp", mp, 4)
    diag_b = swap(from_y[half:], "mp", mp, 2)
    arrays = [x, own_c, from_x, from_y, diag_a, diag_b]
    places = [(0, 0, rows), (1, 0, rows), (2, 0, rows), (4, 0, rows), (6, 0, half), (6, half, half)]
    for number in (2, 3, 4, 5):
        slot, start, count = places[number]
        arrays.append(swap(arrays[number], "mp", mp, 1))
        places.append((slot ^ 1, start, count))
    return Weights(arrays, places, rows)


def gather_small(x, fast, videos, mp):
    if not fast:
        return lax.all_gather(x, ("videos", "mp"), axis=0, tiled=True)
    z = lax.axis_index("videos")
    me = lax.axis_index("mp")
    shape = x.shape
    x = x.reshape((1,) * 5 + shape)
    steps = (
        ("videos", videos, 1, z & 1, 1),
        ("videos", videos, 3, (z >> 1) & 1, 0),
        ("mp", mp, 2, (me >> 1) & 1, 3),
        ("mp", mp, 4, (me >> 2) & 1, 2),
        ("mp", mp, 1, me & 1, 4),
    )
    for axis, size, bit, own_bit, place in steps:
        other = swap(x, axis, size, bit)
        first = jnp.where(own_bit == 0, x, other)
        second = jnp.where(own_bit == 0, other, x)
        x = jnp.concatenate([first, second], axis=place)
    return x.reshape((videos * mp * shape[0],) + shape[1:])


def sum_small(x, fast, mp):
    if not fast:
        return lax.psum(x, "mp")
    for bit in (1, 2, 4):
        x = x + swap(x, "mp", mp, bit)
    return x


def gather_videos(x, fast, videos):
    if not fast:
        return lax.all_gather(x, "videos", axis=0, tiled=True)
    z = lax.axis_index("videos")
    for bit, own_bit in ((1, z & 1), (3, (z >> 1) & 1)):
        other = swap(x, "videos", videos, bit)
        x = jnp.concatenate(
            [jnp.where(own_bit == 0, x, other), jnp.where(own_bit == 0, other, x)], axis=0
        )
    return x


def reduce_grad(parts, fast, videos, mp, x_first):
    if not fast:
        share = lax.psum_scatter(parts[0], "mp", scatter_dimension=0, tiled=False)
        return lax.psum(share, "videos").astype(f32)
    keep, send = parts
    other = swap(send, "mp", mp, 1)
    if x_first:
        bits, pick = (2, 4), lambda a, far: a[:, far]
        zbits = (1, 3)
    else:
        bits, pick = (4, 2), lambda a, far: a[far]
        zbits = (3, 1)
    far = (pick(keep, 1).astype(f32) + pick(other, 1).astype(f32)).astype(bf16)
    far = swap(far, "mp", mp, bits[0])
    near = pick(keep, 0).astype(f32) + pick(other, 0).astype(f32) + far.astype(f32)
    far = swap(near[1].astype(bf16), "mp", mp, bits[1])
    total = (near[0] + far.astype(f32)).astype(bf16)
    for bit in zbits:
        other = swap(total, "videos", videos, bit)
        summed = total.astype(f32) + other.astype(f32)
        total = summed.astype(bf16)
    return summed


def message_forward(meta, cls, weights, features):
    rows = cls.shape[0]
    chunk = min(rows, 256)
    count = len(weights.arrays)

    def body(s, cls_ref, *rest):
        pieces, rest = rest[:count], rest[count:]
        act_ref, proj_ref, mix_ref, message_ref, total_ref, params_ref = rest[:6]
        fc_w, qkv_w, out_w, pack_w, sems = rest[6:]

        @pl.when(pl.program_id(0) == 0)
        def _():
            copies = []
            for number, (first, columns, dst) in enumerate(
                (
                    (0, features, fc_w),
                    (features, 3 * features, qkv_w),
                    (4 * features, features, out_w),
                    (5 * features, PACK, pack_w),
                )
            ):
                copies += weights.copies(pieces, s[0], sems.at[number], first, columns, dst)
            run_copies(copies)
            params_ref[...] = jnp.transpose(pack_w[...].astype(f32))[:16]

        ids = cls_ref[:, features:].astype(f32)
        same = ids[:, :1] == jnp.transpose(ids)[:1, :]
        message = nn(cls_ref[:, :features], fc_w[...])
        message_ref[...] = message
        xhat, _ = norm_parts(message)
        act_ref[...] = (xhat * params_ref[0:1] + params_ref[1:2]).astype(bf16)
        proj_ref[...] = nn(act_ref[...], qkv_w[...]).astype(bf16)
        for p in range(HEADS // 2):
            q2, k2, v2 = (
                proj_ref[:, part * features + p * 128 : part * features + (p + 1) * 128]
                for part in range(3)
            )
            p0, p1 = pair_probs(q2, k2, same)
            mix_ref[:, p * 128 : (p + 1) * 128] = pair_mix(
                v2, p0.astype(bf16), p1.astype(bf16)
            ).astype(bf16)
        total_ref[...] = message_ref[...] + nn(mix_ref[...], out_w[...])

    def block(columns):
        return pl.BlockSpec((chunk, columns), lambda i, s: (i, 0))

    return call(
        body,
        [
            sds((rows, features), bf16),
            sds((rows, 3 * features), bf16),
            sds((rows, features), bf16),
            sds((rows, features), f32),
            sds((rows, features), f32),
            sds((16, features), f32),
        ],
        (rows // chunk,),
        [block(features + PACK)] + [ANY] * count,
        [
            block(features),
            block(3 * features),
            block(features),
            block(features),
            block(features),
            whole((16, features)),
        ],
        [
            pltpu.VMEM((features, features), bf16),
            pltpu.VMEM((features, 3 * features), bf16),
            pltpu.VMEM((features, features), bf16),
            pltpu.VMEM((features, PACK), bf16),
            pltpu.SemaphoreType.DMA((4, count)),
        ],
        2 * rows * 5 * features * features,
        12 * features * features,
    )(meta, cls, *weights.arrays)


def attention_forward(meta, frames, total, params, weights):
    number_frames, patches, features = frames.shape
    count = len(weights.arrays)

    def body(s, frames_ref, total_ref, params_ref, *rest):
        pieces, rest = rest[:count], rest[count:]
        act_ref, qkv_ref, probs_ref, mixed_ref, residual_ref = rest[:5]
        qkv_w, out_w, stacked, sems = rest[5:]
        f = pl.program_id(0)

        @pl.when(f == 0)
        def _():
            copies = weights.copies(pieces, s[0], sems.at[0], 0, 3 * features, qkv_w)
            copies += weights.copies(pieces, s[0], sems.at[1], 3 * features, features, out_w)
            run_copies(copies)
            stacked[...] = jnp.zeros_like(stacked)

        stacked[0:patches] = frames_ref[0].astype(f32)
        stacked[patches : patches + 1] = total_ref[pl.ds(f, 1), :]
        xhat, _ = norm_parts(stacked[...])
        act_ref[0] = (xhat * params_ref[2:3] + params_ref[3:4]).astype(bf16)
        qkv_ref[0] = nn(act_ref[0], qkv_w[...]).astype(bf16)
        valid = lax.broadcasted_iota(jnp.int32, (ROWS, 1), 0) < patches + 1
        for p in range(HEADS // 2):
            q2, k2, v2 = (
                qkv_ref[0, :, part * features + p * 128 : part * features + (p + 1) * 128]
                for part in range(3)
            )
            p0, p1 = pair_probs(q2, k2, valid)
            p0, p1 = p0.astype(bf16), p1.astype(bf16)
            probs_ref[0, p, 0] = p0
            probs_ref[0, p, 1] = p1
            mixed_ref[0, :, p * 128 : (p + 1) * 128] = pair_mix(v2, p0, p1).astype(bf16)
        residual_ref[0] = stacked[...] + nn(mixed_ref[0], out_w[...])

    n = number_frames
    return call(
        body,
        [
            sds((n, ROWS, features), bf16),
            sds((n, ROWS, 3 * features), bf16),
            sds((n, HEADS // 2, 2, ROWS, ROWS), bf16),
            sds((n, ROWS, features), bf16),
            sds((n, ROWS, features), f32),
        ],
        (n,),
        [per_step((patches, features)), whole((8, features)), whole((16, features))]
        + [ANY] * count,
        [
            per_step((ROWS, features)),
            per_step((ROWS, 3 * features)),
            per_step((HEADS // 2, 2, ROWS, ROWS)),
            per_step((ROWS, features)),
            per_step((ROWS, features)),
        ],
        [
            pltpu.VMEM((features, 3 * features), bf16),
            pltpu.VMEM((features, features), bf16),
            pltpu.VMEM((ROWS, features), f32),
            pltpu.SemaphoreType.DMA((2, count)),
        ],
        2 * n * ROWS * (4 * features * features + 2 * ROWS * features),
        24 * 1024 * 1024,
    )(meta, frames, total, params, *weights.arrays)


def mlp_forward(meta, residual, params, onehot, win, wout, patches):
    n, _, features = residual.shape
    hidden_units = win.arrays[0].shape[1]
    count_in, count_out = len(win.arrays), len(wout.arrays)
    chunks = hidden_units // features
    videos = onehot.shape[0]

    def body(s, residual_ref, params_ref, onehot_ref, *rest):
        in_pieces, rest = rest[:count_in], rest[count_in:]
        out_pieces, rest = rest[:count_out], rest[count_out:]
        act_ref, pre_ref, hidden_ref, out_ref, sum_ref = rest[:5]
        in_w, out_w, means, in_sems, out_sems = rest[5:]
        f = pl.program_id(0)

        @pl.when(f == 0)
        def _():
            run_copies(
                win.copies(in_pieces, s[0], in_sems, 0, hidden_units, in_w)
                + wout.copies(out_pieces, s[0], out_sems, 0, features, out_w)
            )
            means[...] = jnp.zeros_like(means)

        residual_in = residual_ref[0]
        xhat, _ = norm_parts(residual_in)
        act_ref[0] = (xhat * params_ref[4:5] + params_ref[5:6]).astype(bf16)
        output = residual_in
        for c in range(chunks):
            columns = slice(c * features, (c + 1) * features)
            pre = nn(act_ref[0], in_w[:, columns])
            pre_ref[0, :, columns] = pre.astype(bf16)
            hidden = (pre * sigmoid(1.702 * pre)).astype(bf16)
            hidden_ref[0, :, columns] = hidden
            output = output + nn(hidden, out_w[columns, :])
        out_ref[0] = output[:patches].astype(bf16)
        valid = lax.broadcasted_iota(jnp.int32, (ROWS, 1), 0) < patches
        means[pl.ds(f, 1), :] = jnp.sum(
            jnp.where(valid, output, 0.0), axis=0, keepdims=True
        ) * (1.0 / patches)

        @pl.when(f == n - 1)
        def _():
            sum_ref[...] = nn(onehot_ref[...], means[...], HIGH) * (1.0 / FPV)

    return call(
        body,
        [
            sds((n, ROWS, features), bf16),
            sds((n, ROWS, hidden_units), bf16),
            sds((n, ROWS, hidden_units), bf16),
            sds((n, patches, features), bf16),
            sds((videos, features), f32),
        ],
        (n,),
        [per_step((ROWS, features)), whole((16, features)), whole((videos, 8))]
        + [ANY] * (count_in + count_out),
        [
            per_step((ROWS, features)),
            per_step((ROWS, hidden_units)),
            per_step((ROWS, hidden_units)),
            per_step((patches, features)),
            whole((videos, features)),
        ],
        [
            pltpu.VMEM((features, hidden_units), bf16),
            pltpu.VMEM((hidden_units, features), bf16),
            pltpu.VMEM((8, features), f32),
            pltpu.SemaphoreType.DMA((count_in,)),
            pltpu.SemaphoreType.DMA((count_out,)),
        ],
        4 * n * ROWS * features * hidden_units,
        32 * 1024 * 1024,
    )(meta, residual, params, onehot, *win.arrays, *wout.arrays)


def contrast(meta, pooled, ids_column, ids_row, onehot, group_videos, patches):
    total, features = pooled.shape
    pad = onehot.shape[0]
    videos = total // pad * group_videos
    weight = float(videos * FPV * patches)

    def body(s, pooled_ref, column_ref, row_ref, onehot_ref, loss_ref, grad_ref, back):
        rows = lax.broadcasted_iota(jnp.int32, (total, 1), 0)
        lanes = lax.broadcasted_iota(jnp.int32, (1, total), 1)
        row_valid = lax.rem(rows, pad) < group_videos
        lane_valid = lax.rem(lanes, pad) < group_videos
        row_one = row_valid.astype(f32)
        values = jnp.where(row_valid, pooled_ref[...], 0.0)
        centred = (values - jnp.sum(values, axis=0, keepdims=True) / videos) * row_one
        scale = lax.rsqrt(jnp.sum(centred * centred, axis=1, keepdims=True) + 1e-06)
        embed = centred * scale
        logits = LOGIT_SCALE * nt(embed, embed, HIGH)
        other = jnp.logical_and(rows != lanes, jnp.logical_and(row_valid, lane_valid))
        masked = jnp.where(other, logits, -1e30)
        top = jnp.max(masked, axis=1, keepdims=True)
        e = jnp.where(other, jnp.exp(masked - top), 0.0)
        e_sum = jnp.sum(e, axis=1, keepdims=True)
        e_sum = jnp.where(row_valid, e_sum, 1.0)
        positive = jnp.logical_and(column_ref[:, :1] == row_ref[:1, :], other).astype(f32)
        counts = jnp.sum(positive, axis=1, keepdims=True)
        counts = jnp.where(row_valid, counts, 1.0)
        means = jnp.sum(positive * logits, axis=1, keepdims=True) / counts
        terms = jnp.where(row_valid, top + jnp.log(e_sum) - means, 0.0)
        loss_ref[...] = jnp.broadcast_to(
            jnp.sum(terms, axis=0, keepdims=True) / videos, loss_ref.shape
        )
        logit_grad = (e / e_sum - positive / counts) * (weight / videos)
        embed_grad = LOGIT_SCALE * (
            nn(logit_grad, embed, HIGH)
            + lax.dot_general(
                logit_grad, embed, (((0,), (0,)), ((), ())),
                preferred_element_type=f32, precision=HIGH,
            )
        )
        along = jnp.sum(embed_grad * embed, axis=1, keepdims=True)
        centred_grad = scale * (embed_grad - embed * along) * row_one
        back[...] = (
            centred_grad - jnp.sum(centred_grad, axis=0, keepdims=True) / videos
        ) * row_one
        own = back[pl.ds(pl.multiple_of(s[1] * pad, 8), pad), :]
        grad_ref[...] = lax.dot_general(
            onehot_ref[...], own, (((0,), (0,)), ((), ())),
            preferred_element_type=f32, precision=HIGH,
        ) * (1.0 / (FPV * patches))

    return call(
        body,
        [sds((8, 128), f32), sds((8, features), f32)],
        (1,),
        [whole(pooled.shape), whole(ids_column.shape), whole(ids_row.shape), whole(onehot.shape)],
        [whole((8, 128)), whole((8, features))],
        [pltpu.VMEM(pooled.shape, f32)],
        10**6,
        10**6,
    )(meta, pooled, ids_column, ids_row, onehot)


def mlp_backward(meta, cotangent, frame_grad, pre, residual, params, win, wout):
    n, patches, features = cotangent.shape
    hidden_units = pre.shape[2]
    count_in, count_out = len(win.arrays), len(wout.arrays)
    chunks = hidden_units // features

    def body(s, cot_ref, fg_ref, pre_ref, residual_ref, params_ref, *rest):
        in_pieces, rest = rest[:count_in], rest[count_in:]
        out_pieces, rest = rest[:count_out], rest[count_out:]
        branch_ref, pre_grad_ref, residual_grad_ref, low_ref, norm_ref = rest[:5]
        in_w, out_w, output_grad, in_sems, out_sems = rest[5:]
        f = pl.program_id(0)

        @pl.when(f == 0)
        def _():
            run_copies(
                win.copies(in_pieces, s[0], in_sems, 0, hidden_units, in_w)
                + wout.copies(out_pieces, s[0], out_sems, 0, features, out_w)
            )
            output_grad[...] = jnp.zeros_like(output_grad)
            norm_ref[...] = jnp.zeros_like(norm_ref)

        output_grad[0:patches] = cot_ref[0].astype(f32) + fg_ref[pl.ds(f, 1), :]
        branch_ref[0] = output_grad[...].astype(bf16)
        normed = jnp.zeros((ROWS, features), f32)
        for c in range(chunks):
            columns = slice(c * features, (c + 1) * features)
            hidden_grad = nt(branch_ref[0], out_w[columns, :])
            u = pre_ref[0, :, columns].astype(f32)
            sig = sigmoid(1.702 * u)
            slope = sig * (1.0 + 1.702 * u * (1.0 - sig))
            pre_grad = (hidden_grad * slope).astype(bf16)
            pre_grad_ref[0, :, columns] = pre_grad
            normed = normed + nt(pre_grad, in_w[:, columns])
        xhat, rstd = norm_parts(residual_ref[0])
        norm_ref[0:1] += jnp.sum(normed * xhat, axis=0, keepdims=True)
        norm_ref[1:2] += jnp.sum(normed, axis=0, keepdims=True)
        residual_grad = output_grad[...] + norm_back(normed, xhat, rstd, params_ref[4:5])
        residual_grad_ref[0] = residual_grad
        low_ref[0] = residual_grad.astype(bf16)

    return call(
        body,
        [
            sds((n, ROWS, features), bf16),
            sds((n, ROWS, hidden_units), bf16),
            sds((n, ROWS, features), f32),
            sds((n, ROWS, features), bf16),
            sds((8, features), f32),
        ],
        (n,),
        [
            per_step((patches, features)),
            whole((8, features)),
            per_step((ROWS, hidden_units)),
            per_step((ROWS, features)),
            whole((16, features)),
        ]
        + [ANY] * (count_in + count_out),
        [
            per_step((ROWS, features)),
            per_step((ROWS, hidden_units)),
            per_step((ROWS, features)),
            per_step((ROWS, features)),
            whole((8, features)),
        ],
        [
            pltpu.VMEM((features, hidden_units), bf16),
            pltpu.VMEM((hidden_units, features), bf16),
            pltpu.VMEM((ROWS, features), f32),
            pltpu.SemaphoreType.DMA((count_in,)),
            pltpu.SemaphoreType.DMA((count_out,)),
        ],
        4 * n * ROWS * features * hidden_units,
        36 * 1024 * 1024,
    )(meta, cotangent, frame_grad, pre, residual, params, *win.arrays, *wout.arrays)


def attention_backward(meta, low, qkv, probs, weights, patches):
    n, _, features = low.shape
    count = len(weights.arrays)

    def body(s, low_ref, qkv_ref, probs_ref, *rest):
        pieces, rest = rest[:count], rest[count:]
        grad_ref, out_w, mixed_grad, sems = rest

        @pl.when(pl.program_id(0) == 0)
        def _():
            run_copies(weights.copies(pieces, s[0], sems, 3 * features, features, out_w))

        mixed_grad[...] = nt(low_ref[0], out_w[...]).astype(bf16)
        for p in range(HEADS // 2):
            q2, k2, v2 = (
                qkv_ref[0, :, part * features + p * 128 : part * features + (p + 1) * 128]
                for part in range(3)
            )
            grads = pair_back(
                q2, k2, v2, mixed_grad[:, p * 128 : (p + 1) * 128],
                probs_ref[0, p, 0], probs_ref[0, p, 1],
            )
            for part, grad in enumerate(grads):
                grad_ref[0, :, part * features + p * 128 : part * features + (p + 1) * 128] = (
                    grad.astype(bf16)
                )

    return call(
        body,
        sds((n, ROWS, 3 * features), bf16),
        (n,),
        [
            per_step((ROWS, features)),
            per_step((ROWS, 3 * features)),
            per_step((HEADS // 2, 2, ROWS, ROWS)),
        ]
        + [ANY] * count,
        per_step((ROWS, 3 * features)),
        [
            pltpu.VMEM((features, features), bf16),
            pltpu.VMEM((ROWS, features), bf16),
            pltpu.SemaphoreType.DMA((count,)),
        ],
        2 * n * ROWS * (features * features + 6 * ROWS * features),
        24 * 1024 * 1024,
    )(meta, low, qkv, probs, *weights.arrays)


def stacked_backward(meta, qkv_grad, frames, total, residual_grad, params, weights):
    n, patches, features = frames.shape
    count = len(weights.arrays)

    def body(s, grad_ref, frames_ref, total_ref, residual_grad_ref, params_ref, *rest):
        pieces, rest = rest[:count], rest[count:]
        frames_grad_ref, first_ref, total_grad_ref, norm_ref = rest[:4]
        qkv_w, stacked, sems = rest[4:]
        f = pl.program_id(0)

        @pl.when(f == 0)
        def _():
            run_copies(weights.copies(pieces, s[0], sems, 0, 3 * features, qkv_w))
            stacked[...] = jnp.zeros_like(stacked)
            norm_ref[...] = jnp.zeros_like(norm_ref)
            first_ref[...] = jnp.zeros_like(first_ref)
            total_grad_ref[...] = jnp.zeros_like(total_grad_ref)

        stacked[0:patches] = frames_ref[0].astype(f32)
        stacked[patches : patches + 1] = total_ref[pl.ds(f, 1), :]
        pre_grad = nt(grad_ref[0], qkv_w[...])
        xhat, rstd = norm_parts(stacked[...])
        norm_ref[0:1] += jnp.sum(pre_grad * xhat, axis=0, keepdims=True)
        norm_ref[1:2] += jnp.sum(pre_grad, axis=0, keepdims=True)
        stacked[...] = norm_back(pre_grad, xhat, rstd, params_ref[2:3]) + residual_grad_ref[0]
        frames_grad_ref[0] = stacked[0:patches].astype(bf16)
        first_ref[pl.ds(f, 1), :] = stacked[0:1]
        total_grad_ref[pl.ds(f, 1), :] = stacked[patches : patches + 1]
        stacked[patches : patches + 1] = jnp.zeros((1, features), f32)
        stacked[patches + 1 :] = jnp.zeros((ROWS - patches - 1, features), f32)

    return call(
        body,
        [
            sds((n, patches, features), bf16),
            sds((8, features), f32),
            sds((8, features), f32),
            sds((8, features), f32),
        ],
        (n,),
        [
            per_step((ROWS, 3 * features)),
            per_step((patches, features)),
            whole((8, features)),
            per_step((ROWS, features)),
            whole((16, features)),
        ]
        + [ANY] * count,
        [
            per_step((patches, features)),
            whole((8, features)),
            whole((8, features)),
            whole((8, features)),
        ],
        [
            pltpu.VMEM((features, 3 * features), bf16),
            pltpu.VMEM((ROWS, features), f32),
            pltpu.SemaphoreType.DMA((count,)),
        ],
        2 * n * ROWS * 3 * features * features,
        24 * 1024 * 1024,
    )(meta, qkv_grad, frames, total, residual_grad, params, *weights.arrays)


def message_backward(meta, total_grad, cls, act, proj, mix, message, params, weights, rows, own_chunk):
    total, features = act.shape
    chunk = min(total, 256)
    steps = total // chunk
    count = len(weights.arrays)

    def body(s, tg_ref, cls_ref, act_ref, proj_ref, mix_ref, message_ref, params_ref, *rest):
        pieces, rest = rest[:count], rest[count:]
        fc_ref, qkv_ref, out_ref, norm_ref, class_ref = rest[:5]
        fc_w, qkv_w, out_w, grads, low, fc_sum, qkv_sum, out_sum, sems = rest[5:]
        step = pl.program_id(0)

        @pl.when(step == 0)
        def _():
            copies = []
            for number, (first, columns, dst) in enumerate(
                (
                    (4 * features, features, out_w),
                    (features, 3 * features, qkv_w),
                    (0, features, fc_w),
                )
            ):
                copies += weights.copies(pieces, s[0], sems.at[number], first, columns, dst)
            run_copies(copies)
            norm_ref[...] = jnp.zeros_like(norm_ref)
            fc_sum[...] = jnp.zeros_like(fc_sum)
            qkv_sum[...] = jnp.zeros_like(qkv_sum)
            out_sum[...] = jnp.zeros_like(out_sum)

        pick = (
            lax.broadcasted_iota(jnp.int32, (features, 128), 0)
            == lax.broadcasted_iota(jnp.int32, (features, 128), 1) + s[0] * rows
        ).astype(f32).astype(bf16)

        def own_rows(values):
            return jnp.transpose(nn(values, pick)).astype(bf16)[:rows]

        ids = cls_ref[:, features:].astype(f32)
        same = ids[:, :1] == jnp.transpose(ids)[:1, :]
        tg = tg_ref[...]
        mix_grad = nt(tg, out_w[...]).astype(bf16)
        for p in range(HEADS // 2):
            q2, k2, v2 = (
                proj_ref[:, part * features + p * 128 : part * features + (p + 1) * 128]
                for part in range(3)
            )
            p0, p1 = pair_probs(q2, k2, same)
            parts = pair_back(q2, k2, v2, mix_grad[:, p * 128 : (p + 1) * 128], p0, p1)
            for part, grad in enumerate(parts):
                grads[:, part * features + p * 128 : part * features + (p + 1) * 128] = (
                    grad.astype(bf16)
                )
        out_sum[...] += nn(own_rows(mix_ref[...]), tg)
        qkv_sum[...] += nn(own_rows(act_ref[...]), grads[...])
        normed = nt(grads[...], qkv_w[...])
        xhat, rstd = norm_parts(message_ref[...])
        norm_ref[0:1] += jnp.sum(normed * xhat, axis=0, keepdims=True)
        norm_ref[1:2] += jnp.sum(normed, axis=0, keepdims=True)
        message_grad = tg.astype(f32) + norm_back(normed, xhat, rstd, params_ref[0:1])
        low[...] = message_grad
        fc_sum[...] += nn(own_rows(cls_ref[:, :features]), message_grad.astype(bf16))

        @pl.when(step == s[2])
        def _():
            own = low[pl.ds(pl.multiple_of(s[3], 8), 8), :].astype(bf16)
            class_ref[...] = nt(own, fc_w[...])

        @pl.when(step == steps - 1)
        def _():
            fc_ref[...] = fc_sum[...].astype(bf16)
            qkv_ref[...] = qkv_sum[...].astype(bf16)
            out_ref[...] = out_sum[...].astype(bf16)

    def block(columns):
        return pl.BlockSpec((chunk, columns), lambda i, s: (i, 0))

    return call(
        body,
        [
            sds((rows, features), bf16),
            sds((rows, 3 * features), bf16),
            sds((rows, features), bf16),
            sds((8, features), f32),
            sds((8, features), f32),
        ],
        (steps,),
        [
            block(features),
            block(features + PACK),
            block(features),
            block(3 * features),
            block(features),
            block(features),
            whole((16, features)),
        ]
        + [ANY] * count,
        [
            whole((rows, features)),
            whole((rows, 3 * features)),
            whole((rows, features)),
            whole((8, features)),
            whole((8, features)),
        ],
        [
            pltpu.VMEM((features, features), bf16),
            pltpu.VMEM((features, 3 * features), bf16),
            pltpu.VMEM((features, features), bf16),
            pltpu.VMEM((chunk, 3 * features), bf16),
            pltpu.VMEM((chunk, features), f32),
            pltpu.VMEM((rows, features), f32),
            pltpu.VMEM((rows, 3 * features), f32),
            pltpu.VMEM((rows, features), f32),
            pltpu.SemaphoreType.DMA((3, count)),
        ],
        4 * total * 5 * features * features,
        14 * features * features,
    )(meta, total_grad, cls, act, proj, mix, message, params, *weights.arrays)


def scatter_rows(s, product, rows, fast, mp, refs):
    if not fast:
        for d in range(mp):
            refs[0][d] = product[d * rows : (d + 1) * rows].astype(bf16)
        return
    even = (s[0] & 1) == 0
    for pair in range(mp // 2):
        low = product[2 * pair * rows : (2 * pair + 1) * rows].astype(bf16)
        high = product[(2 * pair + 1) * rows : (2 * pair + 2) * rows].astype(bf16)
        slot = jnp.bitwise_xor(s[0] >> 1, pair)
        refs[0][slot] = jnp.where(even, low, high)
        refs[1][slot] = jnp.where(even, high, low)


def weight_grad(meta, jobs, outs, rows, fast, mp):
    features = jobs[0][0].shape[1]
    tokens = jobs[0][0].shape[0]
    steps = len(jobs)
    copies = 2 if fast else 1
    lefts, rights = [], []
    for left, right, _, _, _ in jobs:
        if all(left is not x for x in lefts):
            lefts.append(left)
        if all(right is not x for x in rights):
            rights.append(right)
    left_of = [next(i for i, x in enumerate(lefts) if x is job[0]) for job in jobs]
    right_of = [next(i for i, x in enumerate(rights) if x is job[1]) for job in jobs]

    def body(s, *refs):
        left_refs, refs = refs[: len(lefts)], refs[len(lefts) :]
        right_refs, refs = refs[: len(rights)], refs[len(rights) :]
        out_refs, scratch = refs[: copies * len(outs)], refs[-1]
        step = pl.program_id(0)
        for number in range(len(lefts)):

            @pl.when(step == left_of.index(number))
            def _(number=number):
                scratch[...] = transpose(left_refs[number][...])

        for number in range(len(rights)):
            for target in range(len(outs)):
                mine = [
                    i for i in range(steps) if right_of[i] == number and jobs[i][3] == target
                ]
                if not mine:
                    continue

                @pl.when(jnp.logical_and(step >= mine[0], step <= mine[-1]))
                def _(number=number, target=target):
                    product = nn(scratch[...], right_refs[number][...])
                    scatter_rows(
                        s, product, rows, fast, mp,
                        out_refs[copies * target : copies * (target + 1)],
                    )

    def index_map(values, make):
        def pick(i, s):
            index = values[0]
            for number in range(1, steps):
                index = jnp.where(i >= number, values[number], index)
            return make(index)

        return pick

    def held(number, of, column):
        values, last = [], None
        for i in range(steps):
            if of[i] == number:
                last = jobs[i][column]
            values.append(last)
        first = next(v for v in values if v is not None)
        return [first if v is None else v for v in values]

    in_specs = [whole((tokens, features)) for _ in lefts]
    for number in range(len(rights)):
        in_specs.append(
            pl.BlockSpec(
                (tokens, features),
                index_map(held(number, right_of, 2), lambda index: (0, index)),
            )
        )
    out_of = [job[3] for job in jobs]
    out_specs, out_shape = [], []
    lead = mp // 2 if fast else mp
    for target, columns in enumerate(outs):
        spec = pl.BlockSpec(
            (lead, rows, features),
            index_map(held(target, out_of, 4), lambda index: (0, 0, index)),
        )
        for _ in range(copies):
            out_specs.append(spec)
            out_shape.append(sds((lead, rows, columns), bf16))
    results = call(
        body,
        out_shape,
        (steps,),
        in_specs,
        out_specs,
        [pltpu.VMEM((features, tokens), bf16)],
        2 * steps * tokens * features * features,
        (2 * steps + 1) * tokens * features * 2,
    )(meta, *lefts, *rights)
    grouped = [results[copies * t : copies * (t + 1)] for t in range(len(outs))]
    if not fast:
        return grouped
    return [[x.reshape((2, 2) + x.shape[1:]) for x in pair] for pair in grouped]


def hidden_weight_grad(meta, branch, hidden, rows, fast, mp):
    tokens, features = branch.shape
    copies = 2 if fast else 1
    width = 2 * rows if fast else features

    def body(s, branch_ref, hidden_ref, *refs):
        scratch = refs[-1]

        @pl.when(pl.program_id(0) == 0)
        def _():
            scratch[...] = transpose(branch_ref[...])

        product = nn(scratch[...], hidden_ref[...]).astype(bf16)
        if fast:
            low, high = product[:, :rows], product[:, rows:]
            even = (s[0] & 1) == 0
            refs[0][0] = jnp.where(even, low, high)
            refs[1][0] = jnp.where(even, high, low)
        else:
            refs[0][...] = product

    if fast:
        right_map = lambda i, s: (0, jnp.bitwise_xor(i, s[0] >> 1))
        out_spec = pl.BlockSpec((1, features, rows), lambda i, s: (i, 0, 0))
        out_shape = sds((mp // 2, features, rows), bf16)
    else:
        right_map = lambda i, s: (0, i)
        out_spec = pl.BlockSpec((features, width), lambda i, s: (0, i))
        out_shape = sds((features, hidden.shape[1]), bf16)
    results = call(
        body,
        [out_shape] * copies,
        (hidden.shape[1] // width,),
        [whole((tokens, features)), pl.BlockSpec((tokens, width), right_map)],
        [out_spec] * copies,
        [pltpu.VMEM((features, tokens), bf16)],
        2 * tokens * features * hidden.shape[1],
        (hidden.shape[1] + features) * tokens * 2,
    )(meta, branch, hidden)
    if not fast:
        return [results[0].reshape(features, mp, rows).transpose(1, 0, 2)]
    return [x.reshape((2, 2) + x.shape[1:]) for x in results]


def local(
    videos,
    mp,
    frames,
    cotangent,
    frame_video,
    group_ids,
    message_fc,
    message_gain,
    message_shift,
    message_qkv,
    message_out,
    pre_gain,
    pre_shift,
    attn_qkv,
    attn_out,
    mlp_gain,
    mlp_shift,
    fc_in,
    fc_out,
):
    n, patches, features = frames.shape
    rows = message_fc.shape[0]
    fast = (videos, mp) == (4, 8)
    z = lax.axis_index("videos")
    me = lax.axis_index("mp")
    group_videos = frame_video.shape[0] // FPV
    pad_videos = -(-group_videos // 8) * 8
    device_rows = 8 * (z * mp + me)
    meta = jnp.stack([me, z, device_rows // 256, lax.rem(device_rows, 256)]).astype(jnp.int32)

    own_video = lax.dynamic_slice_in_dim(frame_video, me * n, n)
    own_video = jnp.concatenate([own_video, jnp.full((8 - n,), -1, own_video.dtype)])
    onehot = (
        (own_video - z * group_videos)[None, :] == jnp.arange(pad_videos)[:, None]
    ).astype(f32)
    cls = jnp.concatenate(
        [
            jnp.pad(frames[:, 0, :], ((0, 8 - n), (0, 0))),
            jnp.broadcast_to(own_video.astype(bf16)[:, None], (8, PACK)),
        ],
        axis=1,
    )
    cls_all = gather_small(cls, fast, videos, mp)
    norms = jnp.stack(
        [message_gain, message_shift, pre_gain, pre_shift, mlp_gain, mlp_shift], axis=1
    )
    message_shard = jnp.concatenate(
        [message_fc, message_qkv, message_out, jnp.pad(norms, ((0, 0), (0, PACK - 6)))], axis=1
    )
    message_w = gather_weights(message_shard, fast, mp)
    attn_w = gather_weights(jnp.concatenate([attn_qkv, attn_out], axis=1), fast, mp)
    in_w = gather_weights(fc_in, fast, mp)
    out_w = gather_weights(fc_out, fast, mp)

    msg_act, msg_proj, msg_mix, message, msg_total, params = message_forward(
        meta, cls_all, message_w, features
    )
    own_total = lax.dynamic_slice_in_dim(msg_total, device_rows, 8)
    pre_act, qkv, probs, mixed, residual = attention_forward(
        meta, frames, own_total, params, attn_w
    )
    mlp_act, hidden_pre, hidden, out_frames, video_part = mlp_forward(
        meta, residual, params, onehot, in_w, out_w, patches
    )
    pooled = gather_videos(sum_small(video_part, fast, mp), fast, videos)
    ids = jnp.pad(group_ids.reshape(videos, group_videos), ((0, 0), (0, pad_videos - group_videos)))
    ids = ids.reshape(-1)
    loss, frame_grad = contrast(
        meta,
        pooled,
        jnp.broadcast_to(ids[:, None], (ids.shape[0], 128)),
        jnp.broadcast_to(ids[None, :], (8, ids.shape[0])),
        onehot,
        group_videos,
        patches,
    )
    branch, pre_grad, residual_grad, low, mlp_norm = mlp_backward(
        meta, cotangent, frame_grad, hidden_pre, residual, params, in_w, out_w
    )
    flat = lambda a: a.reshape(n * ROWS, a.shape[-1])
    out_parts = hidden_weight_grad(meta, flat(branch), flat(hidden), fc_out.shape[0], fast, mp)
    grad_fc_out = reduce_grad(out_parts, fast, videos, mp, True)
    act_flat, pre_flat = flat(mlp_act), flat(pre_grad)
    (in_parts,) = weight_grad(
        meta,
        [(act_flat, pre_flat, c, 0, c) for c in range(fc_in.shape[1] // features)],
        [fc_in.shape[1]],
        rows,
        fast,
        mp,
    )
    grad_fc_in = reduce_grad(in_parts, fast, videos, mp, False)

    qkv_grad = attention_backward(meta, low, qkv, probs, attn_w, patches)
    stacked_flat, qkv_flat, mixed_flat, low_flat = map(flat, (pre_act, qkv_grad, mixed, low))
    first_parts, second_parts = weight_grad(
        meta,
        [
            (stacked_flat, qkv_flat, 0, 0, 0),
            (stacked_flat, qkv_flat, 1, 0, 1),
            (stacked_flat, qkv_flat, 2, 1, 0),
            (mixed_flat, low_flat, 0, 1, 1),
        ],
        [2 * features, 2 * features],
        rows,
        fast,
        mp,
    )
    first_grad = reduce_grad(first_parts, fast, videos, mp, True)
    second_grad = reduce_grad(second_parts, fast, videos, mp, False)

    frames_grad, first_token, total_grad, pre_norm = stacked_backward(
        meta, qkv_grad, frames, own_total, residual_grad, params, attn_w
    )
    payload = jnp.concatenate(
        [total_grad, pre_norm[:2], mlp_norm[:2], jnp.zeros((4, features), f32)], axis=0
    ).astype(bf16)
    payload_all = gather_small(payload, fast, videos, mp).reshape(videos * mp, 16, features)
    total_grads = payload_all[:, :8].reshape(-1, features)
    norm_sums = payload_all[:, 8:12].astype(f32)
    while norm_sums.shape[0] > 1:
        half = norm_sums.shape[0] // 2
        norm_sums = norm_sums[:half] + norm_sums[half:]
    norm_sums = norm_sums[0]
    grad_message_fc, grad_message_qkv, grad_message_out, message_norm, class_grad = (
        message_backward(
            meta, total_grads, cls_all, msg_act, msg_proj, msg_mix, message, params, message_w,
            rows, None,
        )
    )
    tokens = (first_token + class_grad)[:n].astype(bf16)
    frames_grad = lax.dynamic_update_slice(frames_grad, tokens[:, None, :], (0, 0, 0))
    norm_all = jnp.concatenate([message_norm[:2], norm_sums], axis=0)
    norm_own = lax.dynamic_slice_in_dim(norm_all, me * rows, rows, 1).astype(bf16)
    return (
        out_frames,
        loss[0, 0],
        frames_grad,
        grad_message_fc,
        norm_own[0],
        norm_own[1],
        grad_message_qkv,
        grad_message_out,
        norm_own[2],
        norm_own[3],
        jnp.concatenate([first_grad, second_grad[:, :features]], axis=1).astype(bf16),
        second_grad[:, features:].astype(bf16),
        norm_own[4],
        norm_own[5],
        grad_fc_in.astype(bf16),
        grad_fc_out.T.astype(bf16),
    )


def solution(mesh):
    weight, norm = P("mp", None), P("mp")
    frame = P(("videos", "mp"), None, None)
    params = (
        weight, norm, norm, weight, weight, norm, norm, weight, weight, norm, norm, weight, weight,
    )
    return jax.shard_map(
        functools.partial(local, mesh.shape["videos"], mesh.shape["mp"]),
        mesh=mesh,
        in_specs=(frame, frame, P("videos"), P()) + params,
        out_specs=(frame, P(), frame) + params,
        check_vma=False,
    )
```

```python
import functools

import jax
import jax.numpy as jnp
from jax import lax
from jax.experimental import pallas as pl
from jax.experimental.pallas import tpu as pltpu
from jax.sharding import PartitionSpec as P

HEADS = 12
FPV = 16
EPS = 1e-05
LOGIT_SCALE = 50.0
ROWS = 208
PACK = 128
VMEM = 60 * 1024 * 1024

f32 = jnp.float32
bf16 = jnp.bfloat16
HIGH = lax.Precision.HIGHEST


def nn(a, b, precision=None):
    return jnp.dot(a, b, preferred_element_type=f32, precision=precision)


def nt(a, b, precision=None):
    return lax.dot_general(
        a, b, (((1,), (1,)), ((), ())), preferred_element_type=f32, precision=precision
    )


def norm_parts(x):
    mean = jnp.mean(x, axis=-1, keepdims=True)
    centred = x - mean
    var = jnp.mean(centred * centred, axis=-1, keepdims=True)
    rstd = lax.rsqrt(var + EPS)
    return centred * rstd, rstd


def norm_back(grad, xhat, rstd, gain):
    gy = grad * gain
    return rstd * (
        gy
        - jnp.mean(gy, axis=-1, keepdims=True)
        - xhat * jnp.mean(gy * xhat, axis=-1, keepdims=True)
    )


def sigmoid(x):
    return 0.5 * jnp.tanh(0.5 * x) + 0.5


def lane_masks(dtype):
    lane = lax.broadcasted_iota(jnp.int32, (1, 128), 1)
    low = (lane < 64).astype(f32)
    return low.astype(dtype), (1.0 - low).astype(dtype)


def transpose(x):
    return jnp.transpose(x.astype(f32)).astype(x.dtype)


def pair_probs(q2, k2, valid):
    m0, m1 = lane_masks(bf16)
    qs = q2 * jnp.asarray(0.125, bf16)
    keys = jnp.concatenate([k2 * m0, k2 * m1], axis=0)
    scores = nt(keys, qs)
    count = k2.shape[0]
    out = []
    for j in range(2):
        s = jnp.where(valid, scores[j * count : (j + 1) * count], -1e30)
        e = jnp.exp(s - jnp.max(s, axis=0, keepdims=True))
        out.append(e * (1.0 / jnp.sum(e, axis=0, keepdims=True)))
    return out


def pair_mix(v2, p0, p1):
    vt = transpose(v2)
    mixed = jnp.concatenate([nn(vt[:64], p0), nn(vt[64:], p1)], axis=0)
    return jnp.transpose(mixed)


def pair_back(q2, k2, v2, dm2, p0, p1):
    m0, m1 = lane_masks(bf16)
    count = k2.shape[0]
    lane = lax.broadcasted_iota(jnp.int32, (1, 128), 1) < 64
    eighth = jnp.asarray(0.125, bf16)
    dps = nt(jnp.concatenate([v2 * m0, v2 * m1], axis=0), dm2)
    lows, grads = [], []
    for j, p in enumerate((p0, p1)):
        dp = dps[j * count : (j + 1) * count]
        p_full = p.astype(f32)
        row = jnp.sum(dp * p_full, axis=0, keepdims=True)
        grads.append((p_full * (dp - row)).astype(bf16))
        lows.append(p.astype(bf16))
    dv = nn(jnp.concatenate(lows, axis=0), dm2)
    dk = nn(jnp.concatenate(grads, axis=0), q2 * eighth)
    kt = transpose(k2 * eighth)
    dq = jnp.transpose(
        jnp.concatenate([nn(kt[:64], grads[0]), nn(kt[64:], grads[1])], axis=0)
    )
    return dq, jnp.where(lane, dk[:count], dk[count:]), jnp.where(lane, dv[:count], dv[count:])


def call(body, out_shape, grid, in_specs, out_specs, scratch, flops, bytes_accessed, deps=()):
    count = 1 + len(in_specs)
    deps = tuple(deps)

    def run(*refs):
        return body(*refs[:count], *refs[count + len(deps) :])

    function = pl.pallas_call(
        run,
        out_shape=out_shape,
        grid_spec=pltpu.PrefetchScalarGridSpec(
            num_scalar_prefetch=1,
            grid=grid,
            in_specs=list(in_specs) + [ANY] * len(deps),
            out_specs=out_specs,
            scratch_shapes=scratch,
        ),
        compiler_params=pltpu.CompilerParams(
            dimension_semantics=("arbitrary",) * len(grid), vmem_limit_bytes=VMEM
        ),
        cost_estimate=pl.CostEstimate(
            flops=2 * flops, bytes_accessed=bytes_accessed, transcendentals=0
        ),
    )
    return lambda *arrays: function(*arrays, *deps)


ANY = pl.BlockSpec(memory_space=pl.ANY)


def whole(shape):
    return pl.BlockSpec(shape, lambda i, s: (0,) * len(shape))


def per_step(shape):
    return pl.BlockSpec((1,) + shape, lambda i, s: (i,) + (0,) * len(shape))


def sds(shape, dtype):
    return jax.ShapeDtypeStruct(shape, dtype)


def pack_columns(meta, groups):
    arrays = [x for group in groups for x in group]
    rows, count = arrays[0].shape[0], len(arrays)
    widths = [sum(x.shape[1] for x in group) for group in groups]

    def body(s, *refs):
        ins, outs = list(refs[:count]), refs[count:]
        for group, out in zip(groups, outs):
            first = 0
            for x in group:
                out[:, first : first + x.shape[1]] = ins.pop(0)[...]
                first += x.shape[1]

    return call(
        body,
        [sds((rows, width), bf16) for width in widths],
        (1,),
        [whole(x.shape) for x in arrays],
        [whole((rows, width)) for width in widths],
        [],
        0,
        4 * rows * sum(widths),
    )(meta, *arrays)


class Weights:
    def __init__(self, arrays, places, rows):
        self.arrays = arrays
        self.places = places
        self.rows = rows

    def copies(self, refs, me, sems, first, columns, dst):
        out = []
        for number, (ref, (slot, start, count)) in enumerate(zip(refs, self.places)):
            if slot is None:
                target = dst
            else:
                offset = jnp.bitwise_xor(me, slot) * self.rows + start
                target = dst.at[pl.ds(pl.multiple_of(offset, 16), count), :]
            out.append(
                pltpu.make_async_copy(
                    ref.at[:, pl.ds(first, columns)], target, sems.at[number]
                )
            )
        return out


def run_copies(copies):
    for copy in copies:
        copy.start()
    for copy in copies:
        copy.wait()


def swap(x, axis, size, bit):
    return lax.ppermute(x, axis, [(i, i ^ bit) for i in range(size)])


def tie(x, *arrays):
    return lax.optimization_barrier((x,) + arrays)[0]


def gather_weights(x, fast, mp, first=(), relay=(), swaps=(), late=()):
    rows = x.shape[0]
    if not fast:
        full = lax.all_gather(x, "mp", axis=0, tiled=True)
        return Weights([full], [(None, 0, rows * mp)], rows)
    half = rows // 2
    x = tie(x, *first)
    from_x = swap(x, "mp", mp, 2)
    from_y = swap(x, "mp", mp, 4)
    own_c = swap(tie(x, *swaps), "mp", mp, 1)
    arrays = [
        x,
        own_c,
        from_x,
        from_y,
        swap(tie(from_x, *relay)[:half], "mp", mp, 4),
        swap(tie(from_y, *relay)[half:], "mp", mp, 2),
    ]
    places = [(0, 0, rows), (1, 0, rows), (2, 0, rows), (4, 0, rows), (6, 0, half), (6, half, half)]
    for number in range(2, 6):
        slot, start, count = places[number]
        wait = late if number > 3 else swaps
        arrays.append(swap(tie(arrays[number], *wait), "mp", mp, 1))
        places.append((slot ^ 1, start, count))
    return Weights(arrays, places, rows)


def gather_whole(x, mp, first=()):
    rows = x.shape[0]
    full = lax.all_gather(tie(x, *first), "mp", axis=0, tiled=True)
    return Weights([full], [(None, 0, rows * mp)], rows)


def gather_small(x, fast, videos, mp):
    if not fast:
        for _ in range(3):
            yield x
        yield lax.all_gather(x, "mp", axis=0, tiled=False)
        whole_x = lax.all_gather(x, ("videos", "mp"), axis=0, tiled=True)
        while True:
            yield whole_x
    z = lax.axis_index("videos")
    me = lax.axis_index("mp")
    shape = x.shape
    x = x.reshape((1,) * 4 + shape)

    def ordered(own_first, own, other):
        return jnp.where(own_first, own, other), jnp.where(own_first, other, own)

    for bit, place in ((2, 2), (4, 1), (1, 3)):
        other = swap(x, "mp", mp, bit)
        yield other
        x = jnp.concatenate(ordered((me & bit) == 0, x, other), axis=place)
    after = yield x.reshape((-1,) + shape)
    x = tie(x, *after)
    other = swap(x, "videos", videos, 3)
    yield other
    x = jnp.concatenate(ordered(z < 2, x, other), axis=0)
    other = swap(x, "videos", videos, 1)
    yield other
    outer, inner = ordered(jnp.logical_or(z == 0, z == 3), x, other)
    x = jnp.concatenate([outer[:1], inner, outer[1:]], axis=0)
    yield x.reshape((videos * mp * shape[0],) + shape[1:])


def drain(steps, count=5):
    for _ in range(count):
        next(steps)
    return next(steps)


def sum_all(x, fast, videos, mp):
    if not fast:
        total = lax.psum(x, ("videos", "mp"))
        while True:
            yield total
    for axis, size, bit in (
        ("mp", mp, 1), ("mp", mp, 2), ("mp", mp, 4), ("videos", videos, 1), ("videos", videos, 3),
    ):
        other = swap(x, axis, size, bit)
        after = yield other
        x = x + (tie(other, *after) if after else other)
    yield x


def sum_small(x, fast, mp):
    if not fast:
        return lax.psum(x, "mp")
    for bit in (1, 2, 4):
        x = x + swap(x, "mp", mp, bit)
    return x


def gather_videos(x, fast, videos):
    if not fast:
        return lax.all_gather(x, "videos", axis=0, tiled=True)
    z = lax.axis_index("videos")
    for bit, own_bit in ((1, z & 1), (3, (z >> 1) & 1)):
        other = swap(x, "videos", videos, bit)
        x = jnp.concatenate(
            [jnp.where(own_bit == 0, x, other), jnp.where(own_bit == 0, other, x)], axis=0
        )
    return x


class Reduce:
    def __init__(self, parts, fast, videos, mp, x_first):
        self.parts, self.fast, self.videos, self.mp = parts, fast, videos, mp
        self.bits = (2, 4) if x_first else (4, 2)
        self.number = 0
        if not fast:
            share = lax.psum_scatter(parts[0], "mp", scatter_dimension=0, tiled=False)
            self.total = lax.psum(share, "videos").astype(f32)

    def step(self, after=()):
        if not self.fast:
            return self.total
        number, self.number = self.number, self.number + 1
        if number == 0:
            self.keep, send = self.parts
            self.other = swap(tie(send, *after), "mp", self.mp, 1)
            return self.other
        other = tie(self.other, *after)
        if number == 1:
            self.first = other
            far = self.keep[1].astype(f32) + other[1].astype(f32)
            self.other = swap(far.astype(bf16), "mp", self.mp, self.bits[0])
        elif number == 2:
            near = self.keep[0].astype(f32) + self.first[0].astype(f32) + other.astype(f32)
            self.near = near[0]
            self.other = swap(near[1].astype(bf16), "mp", self.mp, self.bits[1])
        else:
            if number == 3:
                self.total = (self.near + other.astype(f32)).astype(bf16)
            else:
                self.total = (self.total.astype(f32) + other.astype(f32)).astype(bf16)
            self.other = swap(self.total, "videos", self.videos, (1, 3)[number - 3])
        return self.other

    def result(self, after=()):
        if not self.fast:
            return self.total
        return self.total.astype(f32) + tie(self.other, *after).astype(f32)


def scatter_sum(x, after=()):
    return lax.psum_scatter(tie(x, *after), "mp", scatter_dimension=0, tiled=False)


class Along:
    def __init__(self, arrays, fast, videos):
        self.arrays, self.fast, self.videos = list(arrays), fast, videos
        self.number = 0
        if not fast:
            self.arrays = [lax.psum(x, "videos") for x in self.arrays]

    def add(self, after=()):
        self.arrays = [
            x.astype(f32) + tie(y, *after).astype(f32) for x, y in zip(self.arrays, self.others)
        ]

    def step(self, after=()):
        if not self.fast:
            return self.arrays
        if self.number:
            self.add(after)
        low = [x.astype(bf16) for x in self.arrays]
        order = ((1, 3), (3, 1))
        self.others = [
            swap(x, "videos", self.videos, order[i % 2][self.number]) for i, x in enumerate(low)
        ]
        self.arrays = low
        self.number += 1
        return self.others

    def result(self, after=()):
        if self.fast:
            self.add(after)
        return [x.astype(f32) for x in self.arrays]


def message_forward(meta, cls, params, weights, deps=()):
    rows = cls.shape[0]
    features = params.shape[1]
    chunk = min(rows, 256)
    count = len(weights.arrays)

    def body(s, cls_ref, params_ref, *rest):
        pieces, rest = rest[:count], rest[count:]
        act_ref, proj_ref, mix_ref, message_ref, total_ref = rest[:5]
        fc_w, qkv_w, out_w, sems = rest[5:]

        @pl.when(pl.program_id(0) == 0)
        def _():
            copies = []
            for number, (first, columns, dst) in enumerate(
                (
                    (features, features, fc_w),
                    (2 * features, 3 * features, qkv_w),
                    (5 * features, features, out_w),
                )
            ):
                copies += weights.copies(pieces, s[0], sems.at[number], first, columns, dst)
            run_copies(copies)

        ids = cls_ref[:, features:].astype(f32)
        same = ids[:, :1] == jnp.transpose(ids)[:1, :]
        message = nn(cls_ref[:, :features], fc_w[...])
        message_ref[...] = message
        xhat, _ = norm_parts(message)
        act_ref[...] = (xhat * params_ref[0:1] + params_ref[1:2]).astype(bf16)
        proj_ref[...] = nn(act_ref[...], qkv_w[...]).astype(bf16)
        for p in range(HEADS // 2):
            q2, k2, v2 = (
                proj_ref[:, part * features + p * 128 : part * features + (p + 1) * 128]
                for part in range(3)
            )
            p0, p1 = pair_probs(q2, k2, same)
            mix_ref[:, p * 128 : (p + 1) * 128] = pair_mix(
                v2, p0.astype(bf16), p1.astype(bf16)
            ).astype(bf16)
        total_ref[...] = message_ref[...] + nn(mix_ref[...], out_w[...])

    def block(columns):
        return pl.BlockSpec((chunk, columns), lambda i, s: (i, 0))

    return call(
        body,
        [
            sds((rows, features), bf16),
            sds((rows, 3 * features), bf16),
            sds((rows, features), bf16),
            sds((rows, features), f32),
            sds((rows, features), f32),
        ],
        (rows // chunk,),
        [block(features + PACK), whole((16, features))] + [ANY] * count,
        [
            block(features),
            block(3 * features),
            block(features),
            block(features),
            block(features),
        ],
        [
            pltpu.VMEM((features, features), bf16),
            pltpu.VMEM((features, 3 * features), bf16),
            pltpu.VMEM((features, features), bf16),
            pltpu.SemaphoreType.DMA((3, count)),
        ],
        2 * rows * 5 * features * features,
        12 * features * features,
        deps,
    )(meta, cls, params, *weights.arrays)


def frame_projection(meta, frames, params, weights, deps=()):
    n, patches, features = frames.shape
    count = len(weights.arrays)

    def body(s, frames_ref, params_ref, *rest):
        pieces, rest = rest[:count], rest[count:]
        act_ref, qkv_ref, qkv_w, stacked, sems = rest

        @pl.when(pl.program_id(0) == 0)
        def _():
            run_copies(weights.copies(pieces, s[0], sems, 0, 3 * features, qkv_w))
            stacked[...] = jnp.zeros_like(stacked)

        stacked[0:patches] = frames_ref[0].astype(f32)
        xhat, _ = norm_parts(stacked[...])
        act_ref[0] = (xhat * params_ref[2:3] + params_ref[3:4]).astype(bf16)
        qkv_ref[0] = nn(act_ref[0], qkv_w[...]).astype(bf16)

    return call(
        body,
        [
            sds((n, ROWS, features), bf16),
            sds((n, ROWS, 3 * features), bf16),
        ],
        (n,),
        [per_step((patches, features)), whole((16, features))] + [ANY] * count,
        [per_step((ROWS, features)), per_step((ROWS, 3 * features))],
        [
            pltpu.VMEM((features, 3 * features), bf16),
            pltpu.VMEM((ROWS, features), f32),
            pltpu.SemaphoreType.DMA((count,)),
        ],
        2 * n * ROWS * 3 * features * features,
        16 * 1024 * 1024,
        deps,
    )(meta, frames, params, *weights.arrays)


def attention_forward(meta, frames, total, params, act, qkv, weights, out_weights, deps=()):
    n, patches, features = frames.shape
    count, count_out = len(weights.arrays), len(out_weights.arrays)

    def body(s, frames_ref, total_ref, params_ref, act_in, qkv_in, *rest):
        pieces, rest = rest[:count], rest[count:]
        out_pieces, rest = rest[:count_out], rest[count_out:]
        act_ref, qkv_ref, probs_ref, mixed_ref, residual_ref = rest[:5]
        qkv_w, out_w, stacked, act_rows, qkv_rows, sems = rest[5:]
        f = pl.program_id(0)

        @pl.when(f == 0)
        def _():
            copies = weights.copies(pieces, s[0], sems.at[0], 0, 3 * features, qkv_w)
            copies += out_weights.copies(out_pieces, s[0], sems.at[1], 0, features, out_w)
            run_copies(copies)
            stacked[...] = jnp.zeros_like(stacked)
            xhat, _ = norm_parts(total_ref[...])
            rows = xhat * params_ref[2:3] + params_ref[3:4]
            act_rows[...] = rows
            qkv_rows[...] = nn(rows.astype(bf16), qkv_w[...])

        stacked[0:patches] = frames_ref[0].astype(f32)
        message_row = lax.broadcasted_iota(jnp.int32, (ROWS, 1), 0) == patches
        act_ref[0] = jnp.where(
            message_row, act_rows[pl.ds(f, 1), :], act_in[0].astype(f32)
        ).astype(bf16)
        qkv_ref[0] = jnp.where(
            message_row, qkv_rows[pl.ds(f, 1), :], qkv_in[0].astype(f32)
        ).astype(bf16)
        valid = lax.broadcasted_iota(jnp.int32, (ROWS, 1), 0) < patches + 1
        for p in range(HEADS // 2):
            q2, k2, v2 = (
                qkv_ref[0, :, part * features + p * 128 : part * features + (p + 1) * 128]
                for part in range(3)
            )
            p0, p1 = pair_probs(q2, k2, valid)
            p0, p1 = p0.astype(bf16), p1.astype(bf16)
            probs_ref[0, p, 0] = p0
            probs_ref[0, p, 1] = p1
            mixed_ref[0, :, p * 128 : (p + 1) * 128] = pair_mix(v2, p0, p1).astype(bf16)
        residual_ref[0] = stacked[...] + nn(mixed_ref[0], out_w[...])

    return call(
        body,
        [
            sds((n, ROWS, features), bf16),
            sds((n, ROWS, 3 * features), bf16),
            sds((n, HEADS // 2, 2, ROWS, ROWS), bf16),
            sds((n, ROWS, features), bf16),
            sds((n, ROWS, features), f32),
        ],
        (n,),
        [
            per_step((patches, features)),
            whole((8, features)),
            whole((16, features)),
            per_step((ROWS, features)),
            per_step((ROWS, 3 * features)),
        ]
        + [ANY] * (count + count_out),
        [
            per_step((ROWS, features)),
            per_step((ROWS, 3 * features)),
            per_step((HEADS // 2, 2, ROWS, ROWS)),
            per_step((ROWS, features)),
            per_step((ROWS, features)),
        ],
        [
            pltpu.VMEM((features, 3 * features), bf16),
            pltpu.VMEM((features, features), bf16),
            pltpu.VMEM((ROWS, features), f32),
            pltpu.VMEM((8, features), f32),
            pltpu.VMEM((8, 3 * features), f32),
            pltpu.SemaphoreType.DMA((2, count)),
        ],
        2 * n * ROWS * (features * features + 2 * ROWS * features),
        32 * 1024 * 1024,
        deps,
    )(meta, frames, total, params, act, qkv, *weights.arrays, *out_weights.arrays)


def mlp_in(meta, residual, params, win, deps=()):
    n, _, features = residual.shape
    hidden_units = win.arrays[0].shape[1]
    count = len(win.arrays)
    chunks = hidden_units // features

    def body(s, residual_ref, params_ref, *rest):
        pieces, rest = rest[:count], rest[count:]
        act_ref, pre_ref, hidden_ref, in_w, sems = rest

        @pl.when(pl.program_id(0) == 0)
        def _():
            run_copies(win.copies(pieces, s[0], sems, 0, hidden_units, in_w))

        xhat, _ = norm_parts(residual_ref[0])
        act_ref[0] = (xhat * params_ref[4:5] + params_ref[5:6]).astype(bf16)
        for c in range(chunks):
            columns = slice(c * features, (c + 1) * features)
            pre = nn(act_ref[0], in_w[:, columns])
            pre_ref[0, :, columns] = pre.astype(bf16)
            hidden_ref[0, :, columns] = (pre * sigmoid(1.702 * pre)).astype(bf16)

    return call(
        body,
        [
            sds((n, ROWS, features), bf16),
            sds((n, ROWS, hidden_units), bf16),
            sds((n, ROWS, hidden_units), bf16),
        ],
        (n,),
        [per_step((ROWS, features)), whole((16, features))] + [ANY] * count,
        [
            per_step((ROWS, features)),
            per_step((ROWS, hidden_units)),
            per_step((ROWS, hidden_units)),
        ],
        [pltpu.VMEM((features, hidden_units), bf16), pltpu.SemaphoreType.DMA((count,))],
        2 * n * ROWS * features * hidden_units,
        24 * 1024 * 1024,
        deps,
    )(meta, residual, params, *win.arrays)


def mlp_out(meta, residual, hidden, onehot, wout, patches, deps=()):
    n, _, features = residual.shape
    hidden_units = hidden.shape[2]
    count = len(wout.arrays)
    videos = onehot.shape[0]

    def body(s, residual_ref, hidden_ref, onehot_ref, *rest):
        pieces, rest = rest[:count], rest[count:]
        out_ref, sum_ref, out_w, means, sems = rest
        f = pl.program_id(0)

        @pl.when(f == 0)
        def _():
            run_copies(wout.copies(pieces, s[0], sems, 0, features, out_w))
            means[...] = jnp.zeros_like(means)

        output = residual_ref[0] + nn(hidden_ref[0], out_w[...])
        out_ref[0] = output[:patches].astype(bf16)
        valid = lax.broadcasted_iota(jnp.int32, (ROWS, 1), 0) < patches
        means[pl.ds(f, 1), :] = jnp.sum(
            jnp.where(valid, output, 0.0), axis=0, keepdims=True
        ) * (1.0 / patches)

        @pl.when(f == n - 1)
        def _():
            sum_ref[...] = nn(onehot_ref[...], means[...], HIGH) * (1.0 / FPV)

    return call(
        body,
        [sds((n, patches, features), bf16), sds((videos, features), f32)],
        (n,),
        [per_step((ROWS, features)), per_step((ROWS, hidden_units)), whole((videos, 8))]
        + [ANY] * count,
        [per_step((patches, features)), whole((videos, features))],
        [
            pltpu.VMEM((hidden_units, features), bf16),
            pltpu.VMEM((8, features), f32),
            pltpu.SemaphoreType.DMA((count,)),
        ],
        2 * n * ROWS * features * hidden_units,
        20 * 1024 * 1024,
        deps,
    )(meta, residual, hidden, onehot, *wout.arrays)


def contrast(meta, pooled, ids_column, ids_row, onehot, group_videos, patches, deps=()):
    total, features = pooled.shape
    pad = onehot.shape[0]
    videos = total // pad * group_videos
    weight = float(videos * FPV * patches)

    def body(s, pooled_ref, column_ref, row_ref, onehot_ref, loss_ref, grad_ref, all_ref, back):
        rows = lax.broadcasted_iota(jnp.int32, (total, 1), 0)
        lanes = lax.broadcasted_iota(jnp.int32, (1, total), 1)
        row_valid = lax.rem(rows, pad) < group_videos
        lane_valid = lax.rem(lanes, pad) < group_videos
        row_one = row_valid.astype(f32)
        values = jnp.where(row_valid, pooled_ref[...], 0.0)
        centred = (values - jnp.sum(values, axis=0, keepdims=True) / videos) * row_one
        scale = lax.rsqrt(jnp.sum(centred * centred, axis=1, keepdims=True) + 1e-06)
        embed = centred * scale
        logits = LOGIT_SCALE * nt(embed, embed, HIGH)
        other = jnp.logical_and(rows != lanes, jnp.logical_and(row_valid, lane_valid))
        masked = jnp.where(other, logits, -1e30)
        top = jnp.max(masked, axis=1, keepdims=True)
        e = jnp.where(other, jnp.exp(masked - top), 0.0)
        e_sum = jnp.sum(e, axis=1, keepdims=True)
        e_sum = jnp.where(row_valid, e_sum, 1.0)
        positive = jnp.logical_and(column_ref[:, :1] == row_ref[:1, :], other).astype(f32)
        counts = jnp.sum(positive, axis=1, keepdims=True)
        counts = jnp.where(row_valid, counts, 1.0)
        means = jnp.sum(positive * logits, axis=1, keepdims=True) / counts
        terms = jnp.where(row_valid, top + jnp.log(e_sum) - means, 0.0)
        loss_ref[...] = jnp.broadcast_to(
            jnp.sum(terms, axis=0, keepdims=True) / videos, loss_ref.shape
        )
        logit_grad = (e / e_sum - positive / counts) * (weight / videos)
        embed_grad = LOGIT_SCALE * (
            nn(logit_grad, embed, HIGH)
            + lax.dot_general(
                logit_grad, embed, (((0,), (0,)), ((), ())),
                preferred_element_type=f32, precision=HIGH,
            )
        )
        along = jnp.sum(embed_grad * embed, axis=1, keepdims=True)
        centred_grad = scale * (embed_grad - embed * along) * row_one
        back[...] = (
            centred_grad - jnp.sum(centred_grad, axis=0, keepdims=True) / videos
        ) * row_one
        own = back[pl.ds(pl.multiple_of(s[1] * pad, 8), pad), :]
        grad_ref[...] = lax.dot_general(
            onehot_ref[...], own, (((0,), (0,)), ((), ())),
            preferred_element_type=f32, precision=HIGH,
        ) * (1.0 / (FPV * patches))
        all_ref[...] = back[...] * (1.0 / (FPV * patches))

    return call(
        body,
        [sds((8, 128), f32), sds((8, features), f32), sds(pooled.shape, f32)],
        (1,),
        [whole(pooled.shape), whole(ids_column.shape), whole(ids_row.shape), whole(onehot.shape)],
        [whole((8, 128)), whole((8, features)), whole(pooled.shape)],
        [pltpu.VMEM(pooled.shape, f32)],
        10**6,
        10**6,
        deps,
    )(meta, pooled, ids_column, ids_row, onehot)


def mlp_backward(meta, cotangent, frame_grad, pre, residual, params, win, wout, deps=()):
    n, patches, features = cotangent.shape
    hidden_units = pre.shape[2]
    count_in, count_out = len(win.arrays), len(wout.arrays)
    chunks = hidden_units // features

    def body(s, cot_ref, fg_ref, pre_ref, residual_ref, params_ref, *rest):
        in_pieces, rest = rest[:count_in], rest[count_in:]
        out_pieces, rest = rest[:count_out], rest[count_out:]
        pre_grad_ref, residual_grad_ref, low_ref, norm_ref = rest[:4]
        in_w, out_w, output_grad, in_sems, out_sems = rest[4:]
        f = pl.program_id(0)

        @pl.when(f == 0)
        def _():
            run_copies(
                win.copies(in_pieces, s[0], in_sems, 0, hidden_units, in_w)
                + wout.copies(out_pieces, s[0], out_sems, 0, features, out_w)
            )
            output_grad[...] = jnp.zeros_like(output_grad)
            norm_ref[...] = jnp.zeros_like(norm_ref)

        output_grad[0:patches] = cot_ref[0].astype(f32) + fg_ref[pl.ds(f, 1), :]
        branch = output_grad[...].astype(bf16)
        normed = jnp.zeros((ROWS, features), f32)
        for c in range(chunks):
            columns = slice(c * features, (c + 1) * features)
            hidden_grad = nt(branch, out_w[columns, :])
            u = pre_ref[0, :, columns].astype(f32)
            sig = sigmoid(1.702 * u)
            slope = sig * (1.0 + 1.702 * u * (1.0 - sig))
            pre_grad = (hidden_grad * slope).astype(bf16)
            pre_grad_ref[0, :, columns] = pre_grad
            normed = normed + nt(pre_grad, in_w[:, columns])
        xhat, rstd = norm_parts(residual_ref[0])
        norm_ref[0:1] += jnp.sum(normed * xhat, axis=0, keepdims=True)
        norm_ref[1:2] += jnp.sum(normed, axis=0, keepdims=True)
        residual_grad = output_grad[...] + norm_back(normed, xhat, rstd, params_ref[4:5])
        residual_grad_ref[0] = residual_grad
        low_ref[0] = residual_grad.astype(bf16)

    return call(
        body,
        [
            sds((n, ROWS, hidden_units), bf16),
            sds((n, ROWS, features), f32),
            sds((n, ROWS, features), bf16),
            sds((8, features), f32),
        ],
        (n,),
        [
            per_step((patches, features)),
            whole((8, features)),
            per_step((ROWS, hidden_units)),
            per_step((ROWS, features)),
            whole((16, features)),
        ]
        + [ANY] * (count_in + count_out),
        [
            per_step((ROWS, hidden_units)),
            per_step((ROWS, features)),
            per_step((ROWS, features)),
            whole((8, features)),
        ],
        [
            pltpu.VMEM((features, hidden_units), bf16),
            pltpu.VMEM((hidden_units, features), bf16),
            pltpu.VMEM((ROWS, features), f32),
            pltpu.SemaphoreType.DMA((count_in,)),
            pltpu.SemaphoreType.DMA((count_out,)),
        ],
        4 * n * ROWS * features * hidden_units,
        36 * 1024 * 1024,
        deps,
    )(meta, cotangent, frame_grad, pre, residual, params, *win.arrays, *wout.arrays)


def message_token_backward(
    meta, low, mixed, qkv, probs, total, params, weights, out_weights, patches, deps=()
):
    n, _, features = low.shape
    count, count_out = len(weights.arrays), len(out_weights.arrays)
    base = patches // 16 * 16

    def body(s, low_ref, mixed_ref, qkv_ref, probs_ref, total_ref, params_ref, *rest):
        pieces, rest = rest[:count], rest[count:]
        out_pieces, rest = rest[:count_out], rest[count_out:]
        grad_ref, total_grad_ref, kv_w, out_w, heads, rows, table, sems = rest
        f = pl.program_id(0)

        @pl.when(f == 0)
        def _():
            run_copies(out_weights.copies(out_pieces, s[0], sems.at[0], 0, features, out_w))
            for copy in weights.copies(pieces, s[0], sems.at[1], features, 2 * features, kv_w):
                copy.start()
            rows[...] = jnp.zeros_like(rows)
            table[...] = jnp.zeros_like(table)
            head = lax.broadcasted_iota(jnp.int32, (features, 128), 0) // (features // HEADS)
            lane = lax.broadcasted_iota(jnp.int32, (features, 128), 1)
            heads[...] = (head == lane).astype(f32).astype(bf16)

        mixed_grad = nt(low_ref[0], out_w[...]).astype(bf16)
        grad_ref[0] = mixed_grad
        mixed_grad = mixed_grad.astype(f32)
        dots = nn((mixed_grad * mixed_ref[0].astype(f32)).astype(bf16), heads[...])
        here = slice(patches - base, patches - base + 1)
        value = qkv_ref[0, base : base + 16, 2 * features :].astype(f32)[here]
        prob_grad = nn((mixed_grad * value).astype(bf16), heads[...])
        for p in range(HEADS // 2):
            for j in range(2):
                table[2 * p + j : 2 * p + j + 1] = probs_ref[0, p, j].astype(f32)[here]
        probs = jnp.transpose(table[...])
        score_grad = (probs * (prob_grad - dots)).astype(bf16)
        queries = qkv_ref[0, :, :features].astype(f32) * 0.125
        key_grad = jnp.sum(nt(score_grad, heads[...]) * queries, axis=0, keepdims=True)
        value_grad = jnp.sum(
            nt(probs.astype(bf16), heads[...]) * mixed_grad, axis=0, keepdims=True
        )
        rows[pl.ds(f, 1), :] = jnp.concatenate([key_grad, value_grad], axis=1)

        @pl.when(f == n - 1)
        def _():
            for copy in weights.copies(pieces, s[0], sems.at[1], features, 2 * features, kv_w):
                copy.wait()
            pre_grad = nt(rows[...].astype(bf16), kv_w[...])
            xhat, rstd = norm_parts(total_ref[...])
            total_grad_ref[...] = norm_back(pre_grad, xhat, rstd, params_ref[2:3]).astype(bf16)

    return call(
        body,
        [sds((n, ROWS, features), bf16), sds((8, features), bf16)],
        (n,),
        [
            per_step((ROWS, features)),
            per_step((ROWS, features)),
            per_step((ROWS, 3 * features)),
            pl.BlockSpec(
                (1, HEADS // 2, 2, 16, ROWS), lambda i, s: (i, 0, 0, base // 16, 0)
            ),
            whole((8, features)),
            whole((16, features)),
        ]
        + [ANY] * (count + count_out),
        [per_step((ROWS, features)), whole((8, features))],
        [
            pltpu.VMEM((features, 2 * features), bf16),
            pltpu.VMEM((features, features), bf16),
            pltpu.VMEM((features, 128), bf16),
            pltpu.VMEM((8, 2 * features), f32),
            pltpu.VMEM((128, ROWS), f32),
            pltpu.SemaphoreType.DMA((2, max(count, count_out))),
        ],
        2 * n * ROWS * features * (features + 512),
        16 * 1024 * 1024,
        deps,
    )(meta, low, mixed, qkv, probs, total, params, *weights.arrays, *out_weights.arrays)


def attention_backward(meta, mixed_grad, qkv, probs, deps=()):
    n, _, features = mixed_grad.shape

    def body(s, mixed_grad_ref, qkv_ref, probs_ref, grad_ref):
        for p in range(HEADS // 2):
            q2, k2, v2 = (
                qkv_ref[0, :, part * features + p * 128 : part * features + (p + 1) * 128]
                for part in range(3)
            )
            grads = pair_back(
                q2, k2, v2, mixed_grad_ref[0, :, p * 128 : (p + 1) * 128],
                probs_ref[0, p, 0], probs_ref[0, p, 1],
            )
            for part, grad in enumerate(grads):
                columns = slice(part * features + p * 128, part * features + (p + 1) * 128)
                grad_ref[0, :, columns] = grad.astype(bf16)

    return call(
        body,
        sds((n, ROWS, 3 * features), bf16),
        (n,),
        [
            per_step((ROWS, features)),
            per_step((ROWS, 3 * features)),
            per_step((HEADS // 2, 2, ROWS, ROWS)),
        ],
        per_step((ROWS, 3 * features)),
        [],
        2 * n * ROWS * 6 * ROWS * features,
        24 * 1024 * 1024,
        deps,
    )(meta, mixed_grad, qkv, probs)


def stacked_backward(meta, qkv_grad, frames, total, residual_grad, params, weights, deps=()):
    n, patches, features = frames.shape
    count = len(weights.arrays)

    def body(s, grad_ref, frames_ref, total_ref, residual_grad_ref, params_ref, *rest):
        pieces, rest = rest[:count], rest[count:]
        frames_grad_ref, first_ref, norm_ref, qkv_w, stacked, sems = rest
        f = pl.program_id(0)

        @pl.when(f == 0)
        def _():
            run_copies(weights.copies(pieces, s[0], sems, 0, 3 * features, qkv_w))
            stacked[...] = jnp.zeros_like(stacked)
            norm_ref[...] = jnp.zeros_like(norm_ref)
            first_ref[...] = jnp.zeros_like(first_ref)

        stacked[0:patches] = frames_ref[0].astype(f32)
        stacked[patches : patches + 1] = total_ref[pl.ds(f, 1), :]
        pre_grad = nt(grad_ref[0], qkv_w[...])
        xhat, rstd = norm_parts(stacked[...])
        norm_ref[0:1] += jnp.sum(pre_grad * xhat, axis=0, keepdims=True)
        norm_ref[1:2] += jnp.sum(pre_grad, axis=0, keepdims=True)
        stacked[...] = norm_back(pre_grad, xhat, rstd, params_ref[2:3]) + residual_grad_ref[0]
        frames_grad_ref[0] = stacked[0:patches].astype(bf16)
        first_ref[pl.ds(f, 1), :] = stacked[0:1]
        stacked[patches : patches + 1] = jnp.zeros((1, features), f32)
        stacked[patches + 1 :] = jnp.zeros((ROWS - patches - 1, features), f32)

    return call(
        body,
        [
            sds((n, patches, features), bf16),
            sds((8, features), f32),
            sds((8, features), f32),
        ],
        (n,),
        [
            per_step((ROWS, 3 * features)),
            per_step((patches, features)),
            whole((8, features)),
            per_step((ROWS, features)),
            whole((16, features)),
        ]
        + [ANY] * count,
        [
            per_step((patches, features)),
            whole((8, features)),
            whole((8, features)),
        ],
        [
            pltpu.VMEM((features, 3 * features), bf16),
            pltpu.VMEM((ROWS, features), f32),
            pltpu.SemaphoreType.DMA((count,)),
        ],
        2 * n * ROWS * 3 * features * features,
        24 * 1024 * 1024,
        deps,
    )(meta, qkv_grad, frames, total, residual_grad, params, *weights.arrays)


def message_backward(meta, total_grad, cls, act, proj, mix, message, params, weights, rows, deps=()):
    total, features = act.shape
    chunk = min(total, 256)
    steps = total // chunk
    count = len(weights.arrays)

    def body(s, tg_ref, cls_ref, act_ref, proj_ref, mix_ref, message_ref, params_ref, *rest):
        pieces, rest = rest[:count], rest[count:]
        fc_ref, qkv_ref, out_ref, norm_ref, class_ref = rest[:5]
        fc_w, qkv_w, out_w, grads, low, fc_sum, qkv_sum, out_sum, sems = rest[5:]
        step = pl.program_id(0)

        @pl.when(step == 0)
        def _():
            copies = []
            for number, (first, columns, dst) in enumerate(
                (
                    (5 * features, features, out_w),
                    (2 * features, 3 * features, qkv_w),
                    (features, features, fc_w),
                )
            ):
                copies += weights.copies(pieces, s[0], sems.at[number], first, columns, dst)
            run_copies(copies)
            norm_ref[...] = jnp.zeros_like(norm_ref)
            fc_sum[...] = jnp.zeros_like(fc_sum)
            qkv_sum[...] = jnp.zeros_like(qkv_sum)
            out_sum[...] = jnp.zeros_like(out_sum)

        pick = (
            lax.broadcasted_iota(jnp.int32, (features, 128), 0)
            == lax.broadcasted_iota(jnp.int32, (features, 128), 1) + s[0] * rows
        ).astype(f32).astype(bf16)

        def own_rows(values):
            return jnp.transpose(nn(values, pick)).astype(bf16)[:rows]

        ids = cls_ref[:, features:].astype(f32)
        same = ids[:, :1] == jnp.transpose(ids)[:1, :]
        tg = tg_ref[...]
        mix_grad = nt(tg, out_w[...]).astype(bf16)
        for p in range(HEADS // 2):
            q2, k2, v2 = (
                proj_ref[:, part * features + p * 128 : part * features + (p + 1) * 128]
                for part in range(3)
            )
            p0, p1 = pair_probs(q2, k2, same)
            parts = pair_back(q2, k2, v2, mix_grad[:, p * 128 : (p + 1) * 128], p0, p1)
            for part, grad in enumerate(parts):
                grads[:, part * features + p * 128 : part * features + (p + 1) * 128] = (
                    grad.astype(bf16)
                )
        out_sum[...] += nn(own_rows(mix_ref[...]), tg)
        qkv_sum[...] += nn(own_rows(act_ref[...]), grads[...])
        normed = nt(grads[...], qkv_w[...])
        xhat, rstd = norm_parts(message_ref[...])
        norm_ref[0:1] += jnp.sum(normed * xhat, axis=0, keepdims=True)
        norm_ref[1:2] += jnp.sum(normed, axis=0, keepdims=True)
        message_grad = tg.astype(f32) + norm_back(normed, xhat, rstd, params_ref[0:1])
        low[...] = message_grad
        fc_sum[...] += nn(own_rows(cls_ref[:, :features]), message_grad.astype(bf16))

        @pl.when(step == s[2])
        def _():
            own = low[pl.ds(pl.multiple_of(s[3], 8), 8), :].astype(bf16)
            class_ref[...] = nt(own, fc_w[...])

        @pl.when(step == steps - 1)
        def _():
            fc_ref[...] = fc_sum[...].astype(bf16)
            qkv_ref[...] = qkv_sum[...].astype(bf16)
            out_ref[...] = out_sum[...].astype(bf16)

    def block(columns):
        return pl.BlockSpec((chunk, columns), lambda i, s: (i, 0))

    return call(
        body,
        [
            sds((rows, features), bf16),
            sds((rows, 3 * features), bf16),
            sds((rows, features), bf16),
            sds((8, features), f32),
            sds((8, features), f32),
        ],
        (steps,),
        [
            block(features),
            block(features + PACK),
            block(features),
            block(3 * features),
            block(features),
            block(features),
            whole((16, features)),
        ]
        + [ANY] * count,
        [
            whole((rows, features)),
            whole((rows, 3 * features)),
            whole((rows, features)),
            whole((8, features)),
            whole((8, features)),
        ],
        [
            pltpu.VMEM((features, features), bf16),
            pltpu.VMEM((features, 3 * features), bf16),
            pltpu.VMEM((features, features), bf16),
            pltpu.VMEM((chunk, 3 * features), bf16),
            pltpu.VMEM((chunk, features), f32),
            pltpu.VMEM((rows, features), f32),
            pltpu.VMEM((rows, 3 * features), f32),
            pltpu.VMEM((rows, features), f32),
            pltpu.SemaphoreType.DMA((3, count)),
        ],
        4 * total * 5 * features * features,
        14 * features * features,
        deps,
    )(meta, total_grad, cls, act, proj, mix, message, params, *weights.arrays)


def chip_slot(chip, x_first):
    if not x_first:
        return chip
    return ((chip & 1) << 1) | (chip >> 1)


def scatter_rows(s, product, rows, fast, mp, refs, x_first):
    if not fast:
        for d in range(mp):
            refs[0][d] = product[d * rows : (d + 1) * rows].astype(bf16)
        return
    even = (s[0] & 1) == 0
    for pair in range(mp // 2):
        low = product[2 * pair * rows : (2 * pair + 1) * rows].astype(bf16)
        high = product[(2 * pair + 1) * rows : (2 * pair + 2) * rows].astype(bf16)
        slot = chip_slot(jnp.bitwise_xor(s[0] >> 1, pair), x_first)
        refs[0][slot] = jnp.where(even, low, high)
        refs[1][slot] = jnp.where(even, high, low)


def weight_grad(meta, jobs, outs, rows, fast, mp, x_first, deps=()):
    features = jobs[0][0].shape[1]
    tokens = jobs[0][0].shape[0]
    steps = len(jobs)
    copies = 2 if fast else 1
    lefts, rights = [], []
    for left, right, _, _, _ in jobs:
        if all(left is not x for x in lefts):
            lefts.append(left)
        if all(right is not x for x in rights):
            rights.append(right)
    left_of = [next(i for i, x in enumerate(lefts) if x is job[0]) for job in jobs]
    right_of = [next(i for i, x in enumerate(rights) if x is job[1]) for job in jobs]

    def body(s, *refs):
        left_refs, refs = refs[: len(lefts)], refs[len(lefts) :]
        right_refs, refs = refs[: len(rights)], refs[len(rights) :]
        out_refs, scratch = refs[: copies * len(outs)], refs[-1]
        step = pl.program_id(0)
        for number in range(len(lefts)):

            @pl.when(step == left_of.index(number))
            def _(number=number):
                scratch[...] = transpose(left_refs[number][...])

        for number in range(len(rights)):
            for target in range(len(outs)):
                mine = [
                    i for i in range(steps) if right_of[i] == number and jobs[i][3] == target
                ]
                if not mine:
                    continue

                @pl.when(jnp.logical_and(step >= mine[0], step <= mine[-1]))
                def _(number=number, target=target):
                    product = nn(scratch[...], right_refs[number][...])
                    scatter_rows(
                        s, product, rows, fast, mp,
                        out_refs[copies * target : copies * (target + 1)], x_first,
                    )

    def index_map(values, make):
        def pick(i, s):
            index = values[0]
            for number in range(1, steps):
                index = jnp.where(i >= number, values[number], index)
            return make(index)

        return pick

    def held(number, of, column):
        values, last = [], None
        for i in range(steps):
            if of[i] == number:
                last = jobs[i][column]
            values.append(last)
        first = next(v for v in values if v is not None)
        return [first if v is None else v for v in values]

    in_specs = [whole((tokens, features)) for _ in lefts]
    for number in range(len(rights)):
        in_specs.append(
            pl.BlockSpec(
                (tokens, features),
                index_map(held(number, right_of, 2), lambda index: (0, index)),
            )
        )
    out_of = [job[3] for job in jobs]
    out_specs, out_shape = [], []
    lead = mp // 2 if fast else mp
    for target, columns in enumerate(outs):
        spec = pl.BlockSpec(
            (lead, rows, features),
            index_map(held(target, out_of, 4), lambda index: (0, 0, index)),
        )
        for _ in range(copies):
            out_specs.append(spec)
            out_shape.append(sds((lead, rows, columns), bf16))
    results = call(
        body,
        out_shape,
        (steps,),
        in_specs,
        out_specs,
        [pltpu.VMEM((features, tokens), bf16)],
        2 * steps * tokens * features * features,
        (2 * steps + 1) * tokens * features * 2,
        deps,
    )(meta, *lefts, *rights)
    grouped = [results[copies * t : copies * (t + 1)] for t in range(len(outs))]
    if not fast:
        return grouped
    return [[x.reshape((2, 2) + x.shape[1:]) for x in pair] for pair in grouped]


def hidden_weight_grad(meta, cotangent, hidden, ids, all_videos, rows, mp, deps=()):
    n, patches, features = cotangent.shape
    tokens = n * ROWS
    count = features + all_videos
    wide = features + -(-all_videos // 128) * 128
    blocks = features // rows if rows % 128 == 0 else 0
    width = features

    def body(s, cot_ref, ids_ref, hidden_ref, *refs):
        left, scratch = refs[-2:]

        @pl.when(pl.program_id(0) == 0)
        def _():
            lane = lax.broadcasted_iota(jnp.int32, (patches, wide - features), 1)
            left[...] = jnp.zeros_like(left)
            for f in range(n):
                here = slice(f * ROWS, f * ROWS + patches)
                left[here, :features] = cot_ref[f].astype(f32)
                left[here, features:] = (lane == ids_ref[f : f + 1, :1]).astype(f32)
            scratch[...] = jnp.transpose(left[...]).astype(bf16)

        product = nn(scratch[...], hidden_ref[...]).astype(bf16)[:count]
        for d in range(blocks):
            refs[0][d] = product[:, d * rows : (d + 1) * rows]
        if not blocks:
            refs[0][...] = product

    if blocks:
        out_spec = pl.BlockSpec((blocks, count, rows), lambda i, s: (i, 0, 0))
        out_shape = sds((mp, count, rows), bf16)
    else:
        out_spec = pl.BlockSpec((count, width), lambda i, s: (0, i))
        out_shape = sds((count, hidden.shape[1]), bf16)
    results = call(
        body,
        [out_shape],
        (hidden.shape[1] // width,),
        [
            whole((n, patches, features)),
            whole((8, 128)),
            pl.BlockSpec((tokens, width), lambda i, s: (0, i)),
        ],
        [out_spec],
        [pltpu.VMEM((tokens, wide), f32), pltpu.VMEM((wide, tokens), bf16)],
        2 * tokens * features * hidden.shape[1],
        (hidden.shape[1] + features) * tokens * 2,
        deps,
    )(meta, cotangent, ids, hidden)
    if blocks:
        return results[0]
    return results[0].reshape(count, mp, rows).transpose(1, 0, 2)


def local(
    videos,
    mp,
    frames,
    cotangent,
    frame_video,
    group_ids,
    message_fc,
    message_gain,
    message_shift,
    message_qkv,
    message_out,
    pre_gain,
    pre_shift,
    attn_qkv,
    attn_out,
    mlp_gain,
    mlp_shift,
    fc_in,
    fc_out,
):
    n, patches, features = frames.shape
    rows = message_fc.shape[0]
    fast = (videos, mp) == (4, 8)
    z = lax.axis_index("videos")
    me = lax.axis_index("mp")
    group_videos = frame_video.shape[0] // FPV
    pad_videos = -(-group_videos // 8) * 8
    device_rows = 8 * (z * mp + me)
    meta = jnp.stack([me, z, device_rows // 256, lax.rem(device_rows, 256)]).astype(jnp.int32)

    own_video = lax.dynamic_slice_in_dim(frame_video, me * n, n)
    own_video = jnp.concatenate([own_video, jnp.full((8 - n,), -1, own_video.dtype)])
    onehot = (
        (own_video - z * group_videos)[None, :] == jnp.arange(pad_videos)[:, None]
    ).astype(f32)
    norms = jnp.concatenate(
        [message_gain, message_shift, pre_gain, pre_shift, mlp_gain, mlp_shift]
    )
    cls = jnp.concatenate(
        [
            jnp.concatenate(
                [
                    frames[:, 0, :],
                    jnp.pad(norms, (0, features - 6 * rows))[None, :],
                    jnp.zeros((7 - n, features), bf16),
                ]
            ),
            jnp.broadcast_to(own_video.astype(bf16)[:, None], (8, PACK)),
        ],
        axis=1,
    )
    qkv_w = gather_weights(attn_qkv, fast, mp)
    cls_steps = gather_small(tie(cls, *qkv_w.arrays[2:4]), fast, videos, mp)
    next(cls_steps)
    small = next(cls_steps)
    next(cls_steps)
    norms = next(cls_steps)[:, n, : 6 * rows].reshape(mp, 6, rows).transpose(1, 0, 2)
    params = jnp.pad(norms.reshape(6, features).astype(f32), ((0, 10), (0, 0)))
    pre_act, qkv = frame_projection(meta, frames, params, qkv_w)
    early = qkv_w.arrays[4:6] + [small] if fast else ()
    message_w = gather_weights(
        pack_columns(meta, [[attn_out, message_fc, message_qkv, message_out]])[0],
        fast, mp, first=early, relay=[qkv],
    )
    in_w = gather_whole(fc_in, mp, early)
    out_w = gather_whole(fc_out, mp, early)
    cls_steps.send([qkv])
    next(cls_steps)
    cls_all = next(cls_steps)
    msg_act, msg_proj, msg_mix, message, msg_total = message_forward(
        meta, cls_all, params, message_w
    )
    own_total = lax.dynamic_slice_in_dim(msg_total, device_rows, 8)
    attn_act, attn_proj, probs, mixed, residual = attention_forward(
        meta, frames, own_total, params, pre_act, qkv, qkv_w, message_w
    )
    pre_act, qkv = attn_act, attn_proj
    mlp_act, hidden_pre, hidden = mlp_in(meta, residual, params, in_w)
    out_frames, video_part = mlp_out(meta, residual, hidden, onehot, out_w, patches)
    all_videos = videos * pad_videos
    own_place = jnp.where(own_video < 0, -1, own_video - z * group_videos + z * pad_videos)
    out_parts = hidden_weight_grad(
        meta, cotangent, hidden.reshape(n * ROWS, -1),
        jnp.broadcast_to(own_place.astype(jnp.int32)[:, None], (8, 128)),
        all_videos, fc_out.shape[0], mp,
    )
    out_share = scatter_sum(out_parts)
    pooled = gather_videos(sum_small(video_part, fast, mp), fast, videos)
    ids = jnp.pad(group_ids.reshape(videos, group_videos), ((0, 0), (0, pad_videos - group_videos)))
    ids = ids.reshape(-1)
    loss, frame_grad, video_grad = contrast(
        meta,
        pooled,
        jnp.broadcast_to(ids[:, None], (ids.shape[0], 128)),
        jnp.broadcast_to(ids[None, :], (8, ids.shape[0])),
        onehot,
        group_videos,
        patches,
    )
    pre_grad, residual_grad, low, mlp_norm = mlp_backward(
        meta, cotangent, frame_grad, hidden_pre, residual, params, in_w, out_w
    )
    flat = lambda a: a.reshape(n * ROWS, a.shape[-1])
    act_flat, pre_flat = flat(mlp_act), flat(pre_grad)
    mixed_grad, total_grad = message_token_backward(
        meta, low, mixed, qkv, probs, own_total, params, qkv_w, message_w, patches
    )
    gathered = lax.all_gather(
        jnp.pad(total_grad, ((0, 16), (0, 0))), ("videos", "mp"), axis=0, tiled=True
    )
    (in_parts,) = weight_grad(
        meta,
        [(act_flat, pre_flat, c, 0, c) for c in range(fc_in.shape[1] // features)],
        [fc_in.shape[1]], rows, fast, mp, True, [mixed_grad],
    )
    in_red = Reduce(in_parts, fast, videos, mp, True)
    in_1, in_2 = in_red.step(), in_red.step()
    out_along = Along([tie(out_share, in_parts[0])], fast, videos)
    out_1 = out_along.step()
    qkv_grad = attention_backward(meta, mixed_grad, qkv, probs, [in_1])
    in_3 = in_red.step([qkv_grad])
    out_2 = out_along.step([qkv_grad])
    stacked_flat, qkv_flat, mixed_flat, low_flat = map(flat, (pre_act, qkv_grad, mixed, low))
    ((attn_parts,),) = weight_grad(
        meta,
        [(stacked_flat, qkv_flat, c, 0, c) for c in range(3)] + [(mixed_flat, low_flat, 0, 0, 3)],
        [4 * features], rows, False, mp, True, [in_2] + out_1,
    )
    attn_share = scatter_sum(attn_parts)
    in_4 = in_red.step([attn_parts])
    frames_grad, first_token, pre_norm = stacked_backward(
        meta, qkv_grad, frames, own_total, residual_grad, params, qkv_w, [in_3] + out_2
    )
    in_5 = in_red.step([frames_grad])
    norms_all = sum_all(
        jnp.concatenate([pre_norm[:2], mlp_norm[:2], jnp.zeros((4, features), f32)], axis=0),
        fast, videos, mp,
    )
    norms_1, norms_2 = next(norms_all), next(norms_all)
    total_grads = tie(gathered, frames_grad).reshape(-1, 24, features)[:, :8].reshape(-1, features)
    grad_message_fc, grad_message_qkv, grad_message_out, message_norm, class_grad = (
        message_backward(
            meta, total_grads, cls_all, msg_act, msg_proj, msg_mix, message, params, message_w,
            rows, [in_4, norms_1],
        )
    )
    norms_all.send([class_grad])
    norm_sums = drain(norms_all, 2)[:4]
    grad_fc_in = in_red.result([class_grad])
    (grad_fc_out,) = out_along.result([class_grad])
    attn_share = tie(attn_share, class_grad)
    attn_along = Along([attn_share[:, : 2 * features], attn_share[:, 2 * features :]], fast, videos)
    attn_along.step(), attn_along.step()
    first_grad, second_grad = attn_along.result()
    grad_fc_out = grad_fc_out[:features] + lax.dot_general(
        video_grad, grad_fc_out[features:], (((0,), (0,)), ((), ())), precision=HIGH
    )
    tokens = (first_token + class_grad)[:n].astype(bf16)
    frames_grad = lax.dynamic_update_slice(frames_grad, tokens[:, None, :], (0, 0, 0))
    norm_all = jnp.concatenate([message_norm[:2], norm_sums], axis=0)
    norm_own = lax.dynamic_slice_in_dim(norm_all, me * rows, rows, 1).astype(bf16)
    return (
        out_frames,
        loss[0, 0],
        frames_grad,
        grad_message_fc,
        norm_own[0],
        norm_own[1],
        grad_message_qkv,
        grad_message_out,
        norm_own[2],
        norm_own[3],
        jnp.concatenate([first_grad, second_grad[:, :features]], axis=1).astype(bf16),
        second_grad[:, features:].astype(bf16),
        norm_own[4],
        norm_own[5],
        grad_fc_in.astype(bf16),
        grad_fc_out.T.astype(bf16),
    )


def solution(mesh):
    weight, norm = P("mp", None), P("mp")
    frame = P(("videos", "mp"), None, None)
    params = (
        weight, norm, norm, weight, weight, norm, norm, weight, weight, norm, norm, weight, weight,
    )
    return jax.shard_map(
        functools.partial(local, mesh.shape["videos"], mesh.shape["mp"]),
        mesh=mesh,
        in_specs=(frame, frame, P("videos"), P()) + params,
        out_specs=(frame, P(), frame) + params,
        check_vma=False,
    )
```

```python
import functools

import jax
import jax.numpy as jnp
from jax import lax
from jax.experimental import pallas as pl
from jax.experimental.pallas import tpu as pltpu
from jax.sharding import PartitionSpec as P

HEADS = 12
FPV = 16
EPS = 1e-05
LOGIT_SCALE = 50.0
ROWS = 208
PACK = 128
VMEM = 60 * 1024 * 1024

f32 = jnp.float32
bf16 = jnp.bfloat16
HIGH = lax.Precision.HIGHEST


def nn(a, b, precision=None):
    return jnp.dot(a, b, preferred_element_type=f32, precision=precision)


def nt(a, b, precision=None):
    return lax.dot_general(
        a, b, (((1,), (1,)), ((), ())), preferred_element_type=f32, precision=precision
    )


def norm_parts(x):
    mean = jnp.mean(x, axis=-1, keepdims=True)
    centred = x - mean
    var = jnp.mean(centred * centred, axis=-1, keepdims=True)
    rstd = lax.rsqrt(var + EPS)
    return centred * rstd, rstd


def norm_back(grad, xhat, rstd, gain):
    gy = grad * gain
    return rstd * (
        gy
        - jnp.mean(gy, axis=-1, keepdims=True)
        - xhat * jnp.mean(gy * xhat, axis=-1, keepdims=True)
    )


def sigmoid(x):
    return 0.5 * jnp.tanh(0.5 * x) + 0.5


def lane_masks(dtype):
    lane = lax.broadcasted_iota(jnp.int32, (1, 128), 1)
    low = (lane < 64).astype(f32)
    return low.astype(dtype), (1.0 - low).astype(dtype)


def transpose(x):
    return jnp.transpose(x.astype(f32)).astype(x.dtype)


def pair_probs(q2, k2, valid):
    m0, m1 = lane_masks(bf16)
    qs = q2 * jnp.asarray(0.125, bf16)
    keys = jnp.concatenate([k2 * m0, k2 * m1], axis=0)
    scores = nt(keys, qs)
    count = k2.shape[0]
    out = []
    for j in range(2):
        s = jnp.where(valid, scores[j * count : (j + 1) * count], -1e30)
        e = jnp.exp(s - jnp.max(s, axis=0, keepdims=True))
        out.append(e * (1.0 / jnp.sum(e, axis=0, keepdims=True)))
    return out


def pair_mix(v2, p0, p1):
    vt = transpose(v2)
    mixed = jnp.concatenate([nn(vt[:64], p0), nn(vt[64:], p1)], axis=0)
    return jnp.transpose(mixed)


def pair_back(q2, k2, v2, dm2, p0, p1):
    m0, m1 = lane_masks(bf16)
    count = k2.shape[0]
    lane = lax.broadcasted_iota(jnp.int32, (1, 128), 1) < 64
    eighth = jnp.asarray(0.125, bf16)
    dps = nt(jnp.concatenate([v2 * m0, v2 * m1], axis=0), dm2)
    lows, grads = [], []
    for j, p in enumerate((p0, p1)):
        dp = dps[j * count : (j + 1) * count]
        p_full = p.astype(f32)
        row = jnp.sum(dp * p_full, axis=0, keepdims=True)
        grads.append((p_full * (dp - row)).astype(bf16))
        lows.append(p.astype(bf16))
    dv = nn(jnp.concatenate(lows, axis=0), dm2)
    dk = nn(jnp.concatenate(grads, axis=0), q2 * eighth)
    kt = transpose(k2 * eighth)
    dq = jnp.transpose(
        jnp.concatenate([nn(kt[:64], grads[0]), nn(kt[64:], grads[1])], axis=0)
    )
    return dq, jnp.where(lane, dk[:count], dk[count:]), jnp.where(lane, dv[:count], dv[count:])


def call(body, out_shape, grid, in_specs, out_specs, scratch, flops, bytes_accessed, deps=()):
    count = 1 + len(in_specs)
    deps = tuple(deps)

    def run(*refs):
        return body(*refs[:count], *refs[count + len(deps) :])

    function = pl.pallas_call(
        run,
        out_shape=out_shape,
        grid_spec=pltpu.PrefetchScalarGridSpec(
            num_scalar_prefetch=1,
            grid=grid,
            in_specs=list(in_specs) + [ANY] * len(deps),
            out_specs=out_specs,
            scratch_shapes=scratch,
        ),
        compiler_params=pltpu.CompilerParams(
            dimension_semantics=("arbitrary",) * len(grid), vmem_limit_bytes=VMEM
        ),
        cost_estimate=pl.CostEstimate(
            flops=int(2 * flops), bytes_accessed=bytes_accessed, transcendentals=0
        ),
    )
    return lambda *arrays: function(*arrays, *deps)


ANY = pl.BlockSpec(memory_space=pl.ANY)


def whole(shape):
    return pl.BlockSpec(shape, lambda i, s: (0,) * len(shape))


def per_step(shape):
    return pl.BlockSpec((1,) + shape, lambda i, s: (i,) + (0,) * len(shape))


def sds(shape, dtype):
    return jax.ShapeDtypeStruct(shape, dtype)


def pack_columns(meta, groups):
    arrays = [x for group in groups for x in group]
    rows, count = arrays[0].shape[0], len(arrays)
    widths = [sum(x.shape[1] for x in group) for group in groups]

    def body(s, *refs):
        ins, outs = list(refs[:count]), refs[count:]
        for group, out in zip(groups, outs):
            first = 0
            for x in group:
                out[:, first : first + x.shape[1]] = ins.pop(0)[...]
                first += x.shape[1]

    return call(
        body,
        [sds((rows, width), bf16) for width in widths],
        (1,),
        [whole(x.shape) for x in arrays],
        [whole((rows, width)) for width in widths],
        [],
        0,
        4 * rows * sum(widths),
    )(meta, *arrays)


class Weights:
    def __init__(self, arrays, places, rows):
        self.arrays = arrays
        self.places = places
        self.rows = rows

    def copies(self, refs, me, sems, first, columns, dst):
        out = []
        for number, (ref, (slot, start, count)) in enumerate(zip(refs, self.places)):
            if slot is None:
                target = dst
            else:
                offset = jnp.bitwise_xor(me, slot) * self.rows + start
                target = dst.at[pl.ds(pl.multiple_of(offset, 16), count), :]
            out.append(
                pltpu.make_async_copy(
                    ref.at[:, pl.ds(first, columns)], target, sems.at[number]
                )
            )
        return out


def run_copies(copies):
    for copy in copies:
        copy.start()
    for copy in copies:
        copy.wait()


def swap(x, axis, size, bit):
    return lax.ppermute(x, axis, [(i, i ^ bit) for i in range(size)])


def tie(x, *arrays):
    return lax.optimization_barrier((x,) + arrays)[0]


def gather_weights(x, fast, mp, first=(), relay=(), swaps=(), late=()):
    rows = x.shape[0]
    if not fast:
        full = lax.all_gather(x, "mp", axis=0, tiled=True)
        return Weights([full], [(None, 0, rows * mp)], rows)
    half = rows // 2
    x = tie(x, *first)
    from_x = swap(x, "mp", mp, 2)
    from_y = swap(x, "mp", mp, 4)
    own_c = swap(tie(x, *swaps), "mp", mp, 1)
    arrays = [
        x,
        own_c,
        from_x,
        from_y,
        swap(tie(from_x, *relay)[:half], "mp", mp, 4),
        swap(tie(from_y, *relay)[half:], "mp", mp, 2),
    ]
    places = [(0, 0, rows), (1, 0, rows), (2, 0, rows), (4, 0, rows), (6, 0, half), (6, half, half)]
    for number in range(2, 6):
        slot, start, count = places[number]
        wait = late if number > 3 else swaps
        arrays.append(swap(tie(arrays[number], *wait), "mp", mp, 1))
        places.append((slot ^ 1, start, count))
    return Weights(arrays, places, rows)


def gather_whole(x, mp, first=()):
    rows = x.shape[0]
    full = lax.all_gather(tie(x, *first), "mp", axis=0, tiled=True)
    return Weights([full], [(None, 0, rows * mp)], rows)


def gather_small(x, fast, videos, mp):
    if not fast:
        for _ in range(3):
            yield x
        yield lax.all_gather(x, "mp", axis=0, tiled=False)
        whole_x = lax.all_gather(x, ("videos", "mp"), axis=0, tiled=True)
        while True:
            yield whole_x
    z = lax.axis_index("videos")
    me = lax.axis_index("mp")
    shape = x.shape
    x = x.reshape((1,) * 4 + shape)

    def ordered(own_first, own, other):
        return jnp.where(own_first, own, other), jnp.where(own_first, other, own)

    for bit, place in ((2, 2), (4, 1), (1, 3)):
        other = swap(x, "mp", mp, bit)
        yield other
        x = jnp.concatenate(ordered((me & bit) == 0, x, other), axis=place)
    after = yield x.reshape((-1,) + shape)
    x = tie(x, *after)
    other = swap(x, "videos", videos, 3)
    yield other
    x = jnp.concatenate(ordered(z < 2, x, other), axis=0)
    other = swap(x, "videos", videos, 1)
    yield other
    outer, inner = ordered(jnp.logical_or(z == 0, z == 3), x, other)
    x = jnp.concatenate([outer[:1], inner, outer[1:]], axis=0)
    yield x.reshape((videos * mp * shape[0],) + shape[1:])


def gather_along(x, fast, videos):
    if not fast:
        whole_x = lax.all_gather(x, "videos", axis=0, tiled=True)
        yield x
        while True:
            yield whole_x
    z = lax.axis_index("videos")
    yield x
    x = x[None]
    other = swap(x, "videos", videos, 3)
    after = yield other
    other = tie(other, *after)
    x = jnp.concatenate([jnp.where(z < 2, x, other), jnp.where(z < 2, other, x)])
    other = swap(x, "videos", videos, 1)
    after = yield other
    other = tie(other, *after)
    own_outer = jnp.logical_or(z == 0, z == 3)
    outer, inner = jnp.where(own_outer, x, other), jnp.where(own_outer, other, x)
    x = jnp.concatenate([outer[:1], inner, outer[1:]])
    yield x.reshape((-1,) + x.shape[2:])


def drain(steps, count=5):
    for _ in range(count):
        next(steps)
    return next(steps)


def sum_all(x, fast, videos, mp):
    if not fast:
        total = lax.psum(x, ("videos", "mp"))
        while True:
            yield total
    other = swap(x, "mp", mp, 1)
    yield other
    x = x + other
    others = plane_sum(x, mp)
    after = yield others[0]
    x = add_four(x, tuple(tie(y, *after) for y in others))
    others = along_all(x, videos)
    yield others[0]
    yield add_four(x, others)


def plane_sum(x, mp):
    return swap(x, "mp", mp, 2), swap(x, "mp", mp, 4), swap(x, "mp", mp, 6)


def add_four(x, others):
    return (x + others[0]) + (others[1] + others[2])


def along_all(x, videos):
    return tuple(swap(x, "videos", videos, bit) for bit in (1, 2, 3))


def sum_small(x, fast, mp):
    if not fast:
        return lax.psum(x, "mp")
    x = x + swap(x, "mp", mp, 1)
    return add_four(x, plane_sum(x, mp))


def gather_videos(x, fast, videos):
    if not fast:
        return lax.all_gather(x, "videos", axis=0, tiled=True)
    z = lax.axis_index("videos")
    parts = (x,) + along_all(x, videos)
    for bit in (1, 2):
        flip = (z & bit) != 0
        parts = tuple(jnp.where(flip, parts[i ^ bit], parts[i]) for i in range(4))
    return jnp.concatenate(parts, axis=0)


class Reduce:
    def __init__(self, parts, fast, videos, mp, x_first):
        self.parts, self.fast, self.videos, self.mp = parts, fast, videos, mp
        self.bits, self.zbits = ((2, 4), (1, 3)) if x_first else ((4, 2), (3, 1))
        self.number = 0
        if not fast:
            share = lax.psum_scatter(parts[0], "mp", scatter_dimension=0, tiled=False)
            self.total = lax.psum(share, "videos").astype(f32)

    def step(self, after=()):
        if not self.fast:
            return self.total
        number, self.number = self.number, self.number + 1
        if number == 0:
            self.keep, send = self.parts
            self.other = swap(tie(send, *after), "mp", self.mp, 1)
            return self.other
        other = tie(self.other, *after)
        if number == 1:
            self.first = other
            far = self.keep[1].astype(f32) + other[1].astype(f32)
            self.sent = far.astype(bf16)
            self.other = swap(self.sent, "mp", self.mp, self.bits[0])
        elif number == 2:
            near = self.keep[0].astype(f32) + self.first[0].astype(f32) + other.astype(f32)
            self.near = near[0]
            self.other = swap(near[1].astype(bf16), "mp", self.mp, self.bits[1])
        else:
            if number == 3:
                self.total = (self.near + other.astype(f32)).astype(bf16)
            else:
                self.total = (self.total.astype(f32) + other.astype(f32)).astype(bf16)
            self.other = swap(self.total, "videos", self.videos, self.zbits[number - 3])
        return self.other

    def result(self, after=()):
        if not self.fast:
            return self.total
        return self.total.astype(f32) + tie(self.other, *after).astype(f32)


def scatter_sum(x, after=()):
    return lax.psum_scatter(tie(x, *after), "mp", scatter_dimension=0, tiled=False)


class Along:
    def __init__(self, arrays, fast, videos):
        self.arrays, self.fast, self.videos = list(arrays), fast, videos
        self.number = 0
        if not fast:
            self.arrays = [lax.psum(x, "videos") for x in self.arrays]

    def add(self, after=()):
        self.arrays = [
            x.astype(f32) + tie(y, *after).astype(f32) for x, y in zip(self.arrays, self.others)
        ]

    def step(self, after=()):
        if not self.fast:
            return self.arrays
        if self.number:
            self.add(after)
        low = [x.astype(bf16) for x in self.arrays]
        order = ((3, 1), (1, 3))
        self.others = [
            swap(x, "videos", self.videos, order[i % 2][self.number]) for i, x in enumerate(low)
        ]
        self.arrays = low
        self.number += 1
        return self.others

    def result(self, after=()):
        if self.fast:
            self.add(after)
        return [x.astype(f32) for x in self.arrays]


def message_forward(meta, cls, params, weights, deps=()):
    rows = cls.shape[0]
    features = params.shape[1]
    chunk = min(rows, 256)
    count = len(weights.arrays)

    def body(s, cls_ref, params_ref, *rest):
        pieces, rest = rest[:count], rest[count:]
        act_ref, proj_ref, mix_ref, message_ref, total_ref = rest[:5]
        fc_w, qkv_w, out_w, sems = rest[5:]

        @pl.when(pl.program_id(0) == 0)
        def _():
            copies = []
            for number, (first, columns, dst) in enumerate(
                (
                    (features, features, fc_w),
                    (2 * features, 3 * features, qkv_w),
                    (5 * features, features, out_w),
                )
            ):
                copies += weights.copies(pieces, s[0], sems.at[number], first, columns, dst)
            run_copies(copies)

        ids = cls_ref[:, features:].astype(f32)
        same = ids[:, :1] == jnp.transpose(ids)[:1, :]
        message = nn(cls_ref[:, :features], fc_w[...])
        message_ref[...] = message
        xhat, _ = norm_parts(message)
        act_ref[...] = (xhat * params_ref[0:1] + params_ref[1:2]).astype(bf16)
        proj_ref[...] = nn(act_ref[...], qkv_w[...]).astype(bf16)
        for p in range(HEADS // 2):
            q2, k2, v2 = (
                proj_ref[:, part * features + p * 128 : part * features + (p + 1) * 128]
                for part in range(3)
            )
            p0, p1 = pair_probs(q2, k2, same)
            mix_ref[:, p * 128 : (p + 1) * 128] = pair_mix(
                v2, p0.astype(bf16), p1.astype(bf16)
            ).astype(bf16)
        total_ref[...] = message_ref[...] + nn(mix_ref[...], out_w[...])

    def block(columns):
        return pl.BlockSpec((chunk, columns), lambda i, s: (i, 0))

    return call(
        body,
        [
            sds((rows, features), bf16),
            sds((rows, 3 * features), bf16),
            sds((rows, features), bf16),
            sds((rows, features), f32),
            sds((rows, features), f32),
        ],
        (rows // chunk,),
        [block(features + PACK), whole((16, features))] + [ANY] * count,
        [
            block(features),
            block(3 * features),
            block(features),
            block(features),
            block(features),
        ],
        [
            pltpu.VMEM((features, features), bf16),
            pltpu.VMEM((features, 3 * features), bf16),
            pltpu.VMEM((features, features), bf16),
            pltpu.SemaphoreType.DMA((3, count)),
        ],
        2 * rows * 5 * features * features,
        12 * features * features,
        deps,
    )(meta, cls, params, *weights.arrays)


def frame_projection(meta, frames, params, weights, deps=()):
    n, patches, features = frames.shape
    count = len(weights.arrays)

    def body(s, frames_ref, params_ref, *rest):
        pieces, rest = rest[:count], rest[count:]
        act_ref, qkv_ref, qkv_w, stacked, sems = rest

        @pl.when(pl.program_id(0) == 0)
        def _():
            run_copies(weights.copies(pieces, s[0], sems, 0, 3 * features, qkv_w))
            stacked[...] = jnp.zeros_like(stacked)

        stacked[0:patches] = frames_ref[0].astype(f32)
        xhat, _ = norm_parts(stacked[...])
        act_ref[0] = (xhat * params_ref[2:3] + params_ref[3:4]).astype(bf16)
        qkv_ref[0] = nn(act_ref[0], qkv_w[...]).astype(bf16)

    return call(
        body,
        [
            sds((n, ROWS, features), bf16),
            sds((n, ROWS, 3 * features), bf16),
        ],
        (n,),
        [per_step((patches, features)), whole((16, features))] + [ANY] * count,
        [per_step((ROWS, features)), per_step((ROWS, 3 * features))],
        [
            pltpu.VMEM((features, 3 * features), bf16),
            pltpu.VMEM((ROWS, features), f32),
            pltpu.SemaphoreType.DMA((count,)),
        ],
        2 * n * ROWS * 3 * features * features,
        16 * 1024 * 1024,
        deps,
    )(meta, frames, params, *weights.arrays)


def attention_forward(meta, frames, total, params, act, qkv, weights, out_weights, deps=()):
    n, patches, features = frames.shape
    count, count_out = len(weights.arrays), len(out_weights.arrays)

    def body(s, frames_ref, total_ref, params_ref, act_in, qkv_in, *rest):
        pieces, rest = rest[:count], rest[count:]
        out_pieces, rest = rest[:count_out], rest[count_out:]
        act_ref, qkv_ref, probs_ref, mixed_ref, residual_ref = rest[:5]
        qkv_w, out_w, stacked, act_rows, qkv_rows, sems = rest[5:]
        f = pl.program_id(0)

        @pl.when(f == 0)
        def _():
            copies = weights.copies(pieces, s[0], sems.at[0], 0, 3 * features, qkv_w)
            copies += out_weights.copies(out_pieces, s[0], sems.at[1], 0, features, out_w)
            run_copies(copies)
            stacked[...] = jnp.zeros_like(stacked)
            xhat, _ = norm_parts(total_ref[...])
            rows = xhat * params_ref[2:3] + params_ref[3:4]
            act_rows[...] = rows
            qkv_rows[...] = nn(rows.astype(bf16), qkv_w[...])

        stacked[0:patches] = frames_ref[0].astype(f32)
        message_row = lax.broadcasted_iota(jnp.int32, (ROWS, 1), 0) == patches
        act_ref[0] = jnp.where(
            message_row, act_rows[pl.ds(f, 1), :], act_in[0].astype(f32)
        ).astype(bf16)
        qkv_ref[0] = jnp.where(
            message_row, qkv_rows[pl.ds(f, 1), :], qkv_in[0].astype(f32)
        ).astype(bf16)
        valid = lax.broadcasted_iota(jnp.int32, (ROWS, 1), 0) < patches + 1
        for p in range(HEADS // 2):
            q2, k2, v2 = (
                qkv_ref[0, :, part * features + p * 128 : part * features + (p + 1) * 128]
                for part in range(3)
            )
            p0, p1 = pair_probs(q2, k2, valid)
            p0, p1 = p0.astype(bf16), p1.astype(bf16)
            probs_ref[0, p, 0] = p0
            probs_ref[0, p, 1] = p1
            mixed_ref[0, :, p * 128 : (p + 1) * 128] = pair_mix(v2, p0, p1).astype(bf16)
        residual_ref[0] = stacked[...] + nn(mixed_ref[0], out_w[...])

    return call(
        body,
        [
            sds((n, ROWS, features), bf16),
            sds((n, ROWS, 3 * features), bf16),
            sds((n, HEADS // 2, 2, ROWS, ROWS), bf16),
            sds((n, ROWS, features), bf16),
            sds((n, ROWS, features), f32),
        ],
        (n,),
        [
            per_step((patches, features)),
            whole((8, features)),
            whole((16, features)),
            per_step((ROWS, features)),
            per_step((ROWS, 3 * features)),
        ]
        + [ANY] * (count + count_out),
        [
            per_step((ROWS, features)),
            per_step((ROWS, 3 * features)),
            per_step((HEADS // 2, 2, ROWS, ROWS)),
            per_step((ROWS, features)),
            per_step((ROWS, features)),
        ],
        [
            pltpu.VMEM((features, 3 * features), bf16),
            pltpu.VMEM((features, features), bf16),
            pltpu.VMEM((ROWS, features), f32),
            pltpu.VMEM((8, features), f32),
            pltpu.VMEM((8, 3 * features), f32),
            pltpu.SemaphoreType.DMA((2, count)),
        ],
        2 * n * ROWS * (features * features + 2 * ROWS * features),
        32 * 1024 * 1024,
        deps,
    )(meta, frames, total, params, act, qkv, *weights.arrays, *out_weights.arrays)


def mlp_in(meta, residual, params, win, deps=()):
    n, _, features = residual.shape
    hidden_units = win.arrays[0].shape[1]
    count = len(win.arrays)
    chunks = hidden_units // features

    def body(s, residual_ref, params_ref, *rest):
        pieces, rest = rest[:count], rest[count:]
        act_ref, pre_ref, hidden_ref, in_w, sems = rest

        @pl.when(pl.program_id(0) == 0)
        def _():
            run_copies(win.copies(pieces, s[0], sems, 0, hidden_units, in_w))

        xhat, _ = norm_parts(residual_ref[0])
        act_ref[0] = (xhat * params_ref[4:5] + params_ref[5:6]).astype(bf16)
        for c in range(chunks):
            columns = slice(c * features, (c + 1) * features)
            pre = nn(act_ref[0], in_w[:, columns])
            pre_ref[0, :, columns] = pre.astype(bf16)
            hidden_ref[0, :, columns] = (pre * sigmoid(1.702 * pre)).astype(bf16)

    return call(
        body,
        [
            sds((n, ROWS, features), bf16),
            sds((n, ROWS, hidden_units), bf16),
            sds((n, ROWS, hidden_units), bf16),
        ],
        (n,),
        [per_step((ROWS, features)), whole((16, features))] + [ANY] * count,
        [
            per_step((ROWS, features)),
            per_step((ROWS, hidden_units)),
            per_step((ROWS, hidden_units)),
        ],
        [pltpu.VMEM((features, hidden_units), bf16), pltpu.SemaphoreType.DMA((count,))],
        2 * n * ROWS * features * hidden_units,
        24 * 1024 * 1024,
        deps,
    )(meta, residual, params, *win.arrays)


def mlp_out(meta, residual, hidden, onehot, wout, patches, deps=()):
    n, _, features = residual.shape
    hidden_units = hidden.shape[2]
    count = len(wout.arrays)
    videos = onehot.shape[0]

    def body(s, residual_ref, hidden_ref, onehot_ref, *rest):
        pieces, rest = rest[:count], rest[count:]
        out_ref, sum_ref, out_w, means, sems = rest
        f = pl.program_id(0)

        @pl.when(f == 0)
        def _():
            run_copies(wout.copies(pieces, s[0], sems, 0, features, out_w))
            means[...] = jnp.zeros_like(means)

        output = residual_ref[0] + nn(hidden_ref[0], out_w[...])
        out_ref[0] = output[:patches].astype(bf16)
        valid = lax.broadcasted_iota(jnp.int32, (ROWS, 1), 0) < patches
        means[pl.ds(f, 1), :] = jnp.sum(
            jnp.where(valid, output, 0.0), axis=0, keepdims=True
        ) * (1.0 / patches)

        @pl.when(f == n - 1)
        def _():
            sum_ref[...] = nn(onehot_ref[...], means[...], HIGH) * (1.0 / FPV)

    return call(
        body,
        [sds((n, patches, features), bf16), sds((videos, features), f32)],
        (n,),
        [per_step((ROWS, features)), per_step((ROWS, hidden_units)), whole((videos, 8))]
        + [ANY] * count,
        [per_step((patches, features)), whole((videos, features))],
        [
            pltpu.VMEM((hidden_units, features), bf16),
            pltpu.VMEM((8, features), f32),
            pltpu.SemaphoreType.DMA((count,)),
        ],
        2 * n * ROWS * features * hidden_units,
        20 * 1024 * 1024,
        deps,
    )(meta, residual, hidden, onehot, *wout.arrays)


def contrast(meta, pooled, ids_column, ids_row, onehot, group_videos, patches, deps=()):
    total, features = pooled.shape
    pad = onehot.shape[0]
    videos = total // pad * group_videos
    weight = float(videos * FPV * patches)

    def body(s, pooled_ref, column_ref, row_ref, onehot_ref, loss_ref, grad_ref, all_ref, back):
        rows = lax.broadcasted_iota(jnp.int32, (total, 1), 0)
        lanes = lax.broadcasted_iota(jnp.int32, (1, total), 1)
        row_valid = lax.rem(rows, pad) < group_videos
        lane_valid = lax.rem(lanes, pad) < group_videos
        row_one = row_valid.astype(f32)
        values = jnp.where(row_valid, pooled_ref[...], 0.0)
        centred = (values - jnp.sum(values, axis=0, keepdims=True) / videos) * row_one
        scale = lax.rsqrt(jnp.sum(centred * centred, axis=1, keepdims=True) + 1e-06)
        embed = centred * scale
        logits = LOGIT_SCALE * nt(embed, embed, HIGH)
        other = jnp.logical_and(rows != lanes, jnp.logical_and(row_valid, lane_valid))
        masked = jnp.where(other, logits, -1e30)
        top = jnp.max(masked, axis=1, keepdims=True)
        e = jnp.where(other, jnp.exp(masked - top), 0.0)
        e_sum = jnp.sum(e, axis=1, keepdims=True)
        e_sum = jnp.where(row_valid, e_sum, 1.0)
        positive = jnp.logical_and(column_ref[:, :1] == row_ref[:1, :], other).astype(f32)
        counts = jnp.sum(positive, axis=1, keepdims=True)
        counts = jnp.where(row_valid, counts, 1.0)
        means = jnp.sum(positive * logits, axis=1, keepdims=True) / counts
        terms = jnp.where(row_valid, top + jnp.log(e_sum) - means, 0.0)
        loss_ref[...] = jnp.broadcast_to(
            jnp.sum(terms, axis=0, keepdims=True) / videos, loss_ref.shape
        )
        logit_grad = (e / e_sum - positive / counts) * (weight / videos)
        embed_grad = LOGIT_SCALE * (
            nn(logit_grad, embed, HIGH)
            + lax.dot_general(
                logit_grad, embed, (((0,), (0,)), ((), ())),
                preferred_element_type=f32, precision=HIGH,
            )
        )
        along = jnp.sum(embed_grad * embed, axis=1, keepdims=True)
        centred_grad = scale * (embed_grad - embed * along) * row_one
        back[...] = (
            centred_grad - jnp.sum(centred_grad, axis=0, keepdims=True) / videos
        ) * row_one
        own = back[pl.ds(pl.multiple_of(s[1] * pad, 8), pad), :]
        grad_ref[...] = lax.dot_general(
            onehot_ref[...], own, (((0,), (0,)), ((), ())),
            preferred_element_type=f32, precision=HIGH,
        ) * (1.0 / (FPV * patches))
        all_ref[...] = back[...] * (1.0 / (FPV * patches))

    return call(
        body,
        [sds((8, 128), f32), sds((8, features), f32), sds(pooled.shape, f32)],
        (1,),
        [whole(pooled.shape), whole(ids_column.shape), whole(ids_row.shape), whole(onehot.shape)],
        [whole((8, 128)), whole((8, features)), whole(pooled.shape)],
        [pltpu.VMEM(pooled.shape, f32)],
        10**6,
        10**6,
        deps,
    )(meta, pooled, ids_column, ids_row, onehot)


def mlp_backward(meta, cotangent, frame_grad, pre, residual, params, win, wout, deps=()):
    n, patches, features = cotangent.shape
    hidden_units = pre.shape[2]
    count_in, count_out = len(win.arrays), len(wout.arrays)
    chunks = hidden_units // features

    def body(s, cot_ref, fg_ref, pre_ref, residual_ref, params_ref, *rest):
        in_pieces, rest = rest[:count_in], rest[count_in:]
        out_pieces, rest = rest[:count_out], rest[count_out:]
        pre_grad_ref, residual_grad_ref, low_ref, norm_ref = rest[:4]
        in_w, out_w, output_grad, in_sems, out_sems = rest[4:]
        f = pl.program_id(0)

        @pl.when(f == 0)
        def _():
            run_copies(
                win.copies(in_pieces, s[0], in_sems, 0, hidden_units, in_w)
                + wout.copies(out_pieces, s[0], out_sems, 0, features, out_w)
            )
            output_grad[...] = jnp.zeros_like(output_grad)
            norm_ref[...] = jnp.zeros_like(norm_ref)

        output_grad[0:patches] = cot_ref[0].astype(f32) + fg_ref[pl.ds(f, 1), :]
        branch = output_grad[...].astype(bf16)
        normed = jnp.zeros((ROWS, features), f32)
        for c in range(chunks):
            columns = slice(c * features, (c + 1) * features)
            hidden_grad = nt(branch, out_w[columns, :])
            u = pre_ref[0, :, columns].astype(f32)
            sig = sigmoid(1.702 * u)
            slope = sig * (1.0 + 1.702 * u * (1.0 - sig))
            pre_grad = (hidden_grad * slope).astype(bf16)
            pre_grad_ref[0, :, columns] = pre_grad
            normed = normed + nt(pre_grad, in_w[:, columns])
        xhat, rstd = norm_parts(residual_ref[0])
        norm_ref[0:1] += jnp.sum(normed * xhat, axis=0, keepdims=True)
        norm_ref[1:2] += jnp.sum(normed, axis=0, keepdims=True)
        residual_grad = output_grad[...] + norm_back(normed, xhat, rstd, params_ref[4:5])
        residual_grad_ref[0] = residual_grad
        low_ref[0] = residual_grad.astype(bf16)

    return call(
        body,
        [
            sds((n, ROWS, hidden_units), bf16),
            sds((n, ROWS, features), f32),
            sds((n, ROWS, features), bf16),
            sds((8, features), f32),
        ],
        (n,),
        [
            per_step((patches, features)),
            whole((8, features)),
            per_step((ROWS, hidden_units)),
            per_step((ROWS, features)),
            whole((16, features)),
        ]
        + [ANY] * (count_in + count_out),
        [
            per_step((ROWS, hidden_units)),
            per_step((ROWS, features)),
            per_step((ROWS, features)),
            whole((8, features)),
        ],
        [
            pltpu.VMEM((features, hidden_units), bf16),
            pltpu.VMEM((hidden_units, features), bf16),
            pltpu.VMEM((ROWS, features), f32),
            pltpu.SemaphoreType.DMA((count_in,)),
            pltpu.SemaphoreType.DMA((count_out,)),
        ],
        4 * n * ROWS * features * hidden_units,
        36 * 1024 * 1024,
        deps,
    )(meta, cotangent, frame_grad, pre, residual, params, *win.arrays, *wout.arrays)


def message_token_backward(
    meta, low, mixed, qkv, probs, total, params, weights, out_weights, patches, deps=()
):
    n, _, features = low.shape
    count, count_out = len(weights.arrays), len(out_weights.arrays)
    base = patches // 16 * 16

    def body(s, low_ref, mixed_ref, qkv_ref, probs_ref, total_ref, params_ref, *rest):
        pieces, rest = rest[:count], rest[count:]
        out_pieces, rest = rest[:count_out], rest[count_out:]
        grad_ref, total_grad_ref, kv_w, out_w, heads, rows, table, sems = rest
        f = pl.program_id(0)

        @pl.when(f == 0)
        def _():
            run_copies(out_weights.copies(out_pieces, s[0], sems.at[0], 0, features, out_w))
            for copy in weights.copies(pieces, s[0], sems.at[1], features, 2 * features, kv_w):
                copy.start()
            rows[...] = jnp.zeros_like(rows)
            table[...] = jnp.zeros_like(table)
            head = lax.broadcasted_iota(jnp.int32, (features, 128), 0) // (features // HEADS)
            lane = lax.broadcasted_iota(jnp.int32, (features, 128), 1)
            heads[...] = (head == lane).astype(f32).astype(bf16)

        mixed_grad = nt(low_ref[0], out_w[...]).astype(bf16)
        grad_ref[0] = mixed_grad
        mixed_grad = mixed_grad.astype(f32)
        dots = nn((mixed_grad * mixed_ref[0].astype(f32)).astype(bf16), heads[...])
        here = slice(patches - base, patches - base + 1)
        value = qkv_ref[0, base : base + 16, 2 * features :].astype(f32)[here]
        prob_grad = nn((mixed_grad * value).astype(bf16), heads[...])
        for p in range(HEADS // 2):
            for j in range(2):
                table[2 * p + j : 2 * p + j + 1] = probs_ref[0, p, j].astype(f32)[here]
        probs = jnp.transpose(table[...])
        score_grad = (probs * (prob_grad - dots)).astype(bf16)
        queries = qkv_ref[0, :, :features].astype(f32) * 0.125
        key_grad = jnp.sum(nt(score_grad, heads[...]) * queries, axis=0, keepdims=True)
        value_grad = jnp.sum(
            nt(probs.astype(bf16), heads[...]) * mixed_grad, axis=0, keepdims=True
        )
        rows[pl.ds(f, 1), :] = jnp.concatenate([key_grad, value_grad], axis=1)

        @pl.when(f == n - 1)
        def _():
            for copy in weights.copies(pieces, s[0], sems.at[1], features, 2 * features, kv_w):
                copy.wait()
            pre_grad = nt(rows[...].astype(bf16), kv_w[...])
            xhat, rstd = norm_parts(total_ref[...])
            total_grad_ref[...] = norm_back(pre_grad, xhat, rstd, params_ref[2:3]).astype(bf16)

    return call(
        body,
        [sds((n, ROWS, features), bf16), sds((8, features), bf16)],
        (n,),
        [
            per_step((ROWS, features)),
            per_step((ROWS, features)),
            per_step((ROWS, 3 * features)),
            pl.BlockSpec(
                (1, HEADS // 2, 2, 16, ROWS), lambda i, s: (i, 0, 0, base // 16, 0)
            ),
            whole((8, features)),
            whole((16, features)),
        ]
        + [ANY] * (count + count_out),
        [per_step((ROWS, features)), whole((8, features))],
        [
            pltpu.VMEM((features, 2 * features), bf16),
            pltpu.VMEM((features, features), bf16),
            pltpu.VMEM((features, 128), bf16),
            pltpu.VMEM((8, 2 * features), f32),
            pltpu.VMEM((128, ROWS), f32),
            pltpu.SemaphoreType.DMA((2, max(count, count_out))),
        ],
        2 * n * ROWS * features * (features + 512),
        16 * 1024 * 1024,
        deps,
    )(meta, low, mixed, qkv, probs, total, params, *weights.arrays, *out_weights.arrays)


def attention_backward(meta, mixed_grad, qkv, probs, deps=()):
    n, _, features = mixed_grad.shape

    def body(s, mixed_grad_ref, qkv_ref, probs_ref, grad_ref):
        for p in range(HEADS // 2):
            q2, k2, v2 = (
                qkv_ref[0, :, part * features + p * 128 : part * features + (p + 1) * 128]
                for part in range(3)
            )
            grads = pair_back(
                q2, k2, v2, mixed_grad_ref[0, :, p * 128 : (p + 1) * 128],
                probs_ref[0, p, 0], probs_ref[0, p, 1],
            )
            for part, grad in enumerate(grads):
                columns = slice(part * features + p * 128, part * features + (p + 1) * 128)
                grad_ref[0, :, columns] = grad.astype(bf16)

    return call(
        body,
        sds((n, ROWS, 3 * features), bf16),
        (n,),
        [
            per_step((ROWS, features)),
            per_step((ROWS, 3 * features)),
            per_step((HEADS // 2, 2, ROWS, ROWS)),
        ],
        per_step((ROWS, 3 * features)),
        [],
        2 * n * ROWS * 6 * ROWS * features,
        24 * 1024 * 1024,
        deps,
    )(meta, mixed_grad, qkv, probs)


def stacked_backward(meta, qkv_grad, frames, total, residual_grad, params, weights, deps=()):
    n, patches, features = frames.shape
    count = len(weights.arrays)

    def body(s, grad_ref, frames_ref, total_ref, residual_grad_ref, params_ref, *rest):
        pieces, rest = rest[:count], rest[count:]
        frames_grad_ref, first_ref, norm_ref, qkv_w, stacked, sems = rest
        f = pl.program_id(0)

        @pl.when(f == 0)
        def _():
            run_copies(weights.copies(pieces, s[0], sems, 0, 3 * features, qkv_w))
            stacked[...] = jnp.zeros_like(stacked)
            norm_ref[...] = jnp.zeros_like(norm_ref)
            first_ref[...] = jnp.zeros_like(first_ref)

        stacked[0:patches] = frames_ref[0].astype(f32)
        stacked[patches : patches + 1] = total_ref[pl.ds(f, 1), :]
        pre_grad = nt(grad_ref[0], qkv_w[...])
        xhat, rstd = norm_parts(stacked[...])
        norm_ref[0:1] += jnp.sum(pre_grad * xhat, axis=0, keepdims=True)
        norm_ref[1:2] += jnp.sum(pre_grad, axis=0, keepdims=True)
        stacked[...] = norm_back(pre_grad, xhat, rstd, params_ref[2:3]) + residual_grad_ref[0]
        frames_grad_ref[0] = stacked[0:patches].astype(bf16)
        first_ref[pl.ds(f, 1), :] = stacked[0:1]
        stacked[patches : patches + 1] = jnp.zeros((1, features), f32)
        stacked[patches + 1 :] = jnp.zeros((ROWS - patches - 1, features), f32)

    return call(
        body,
        [
            sds((n, patches, features), bf16),
            sds((8, features), f32),
            sds((8, features), f32),
        ],
        (n,),
        [
            per_step((ROWS, 3 * features)),
            per_step((patches, features)),
            whole((8, features)),
            per_step((ROWS, features)),
            whole((16, features)),
        ]
        + [ANY] * count,
        [
            per_step((patches, features)),
            whole((8, features)),
            whole((8, features)),
        ],
        [
            pltpu.VMEM((features, 3 * features), bf16),
            pltpu.VMEM((ROWS, features), f32),
            pltpu.SemaphoreType.DMA((count,)),
        ],
        1,
        1,
        deps,
    )(meta, qkv_grad, frames, total, residual_grad, params, *weights.arrays)


def message_backward(meta, total_grad, cls, act, proj, mix, message, params, weights, rows, deps=()):
    total, features = act.shape
    chunk = min(total, 256)
    steps = total // chunk
    count = len(weights.arrays)

    def body(s, tg_ref, cls_ref, act_ref, proj_ref, mix_ref, message_ref, params_ref, *rest):
        pieces, rest = rest[:count], rest[count:]
        fc_ref, qkv_ref, out_ref, norm_ref, class_ref = rest[:5]
        fc_w, qkv_w, out_w, grads, low, fc_sum, qkv_sum, out_sum, sems = rest[5:]
        step = pl.program_id(0)

        @pl.when(step == 0)
        def _():
            copies = []
            for number, (first, columns, dst) in enumerate(
                (
                    (5 * features, features, out_w),
                    (2 * features, 3 * features, qkv_w),
                    (features, features, fc_w),
                )
            ):
                copies += weights.copies(pieces, s[0], sems.at[number], first, columns, dst)
            run_copies(copies)
            norm_ref[...] = jnp.zeros_like(norm_ref)
            fc_sum[...] = jnp.zeros_like(fc_sum)
            qkv_sum[...] = jnp.zeros_like(qkv_sum)
            out_sum[...] = jnp.zeros_like(out_sum)

        pick = (
            lax.broadcasted_iota(jnp.int32, (features, 128), 0)
            == lax.broadcasted_iota(jnp.int32, (features, 128), 1) + s[0] * rows
        ).astype(f32).astype(bf16)

        def own_rows(values):
            return jnp.transpose(nn(values, pick)).astype(bf16)[:rows]

        ids = cls_ref[:, features:].astype(f32)
        same = ids[:, :1] == jnp.transpose(ids)[:1, :]
        tg = tg_ref[...]
        mix_grad = nt(tg, out_w[...]).astype(bf16)
        for p in range(HEADS // 2):
            q2, k2, v2 = (
                proj_ref[:, part * features + p * 128 : part * features + (p + 1) * 128]
                for part in range(3)
            )
            p0, p1 = pair_probs(q2, k2, same)
            parts = pair_back(q2, k2, v2, mix_grad[:, p * 128 : (p + 1) * 128], p0, p1)
            for part, grad in enumerate(parts):
                grads[:, part * features + p * 128 : part * features + (p + 1) * 128] = (
                    grad.astype(bf16)
                )
        out_sum[...] += nn(own_rows(mix_ref[...]), tg)
        qkv_sum[...] += nn(own_rows(act_ref[...]), grads[...])
        normed = nt(grads[...], qkv_w[...])
        xhat, rstd = norm_parts(message_ref[...])
        norm_ref[0:1] += jnp.sum(normed * xhat, axis=0, keepdims=True)
        norm_ref[1:2] += jnp.sum(normed, axis=0, keepdims=True)
        message_grad = tg.astype(f32) + norm_back(normed, xhat, rstd, params_ref[0:1])
        low[...] = message_grad
        fc_sum[...] += nn(own_rows(cls_ref[:, :features]), message_grad.astype(bf16))

        @pl.when(step == s[2])
        def _():
            own = low[pl.ds(pl.multiple_of(s[3], 8), 8), :].astype(bf16)
            class_ref[...] = nt(own, fc_w[...])

        @pl.when(step == steps - 1)
        def _():
            fc_ref[...] = fc_sum[...].astype(bf16)
            qkv_ref[...] = qkv_sum[...].astype(bf16)
            out_ref[...] = out_sum[...].astype(bf16)

    def block(columns):
        return pl.BlockSpec((chunk, columns), lambda i, s: (i, 0))

    return call(
        body,
        [
            sds((rows, features), bf16),
            sds((rows, 3 * features), bf16),
            sds((rows, features), bf16),
            sds((8, features), f32),
            sds((8, features), f32),
        ],
        (steps,),
        [
            block(features),
            block(features + PACK),
            block(features),
            block(3 * features),
            block(features),
            block(features),
            whole((16, features)),
        ]
        + [ANY] * count,
        [
            whole((rows, features)),
            whole((rows, 3 * features)),
            whole((rows, features)),
            whole((8, features)),
            whole((8, features)),
        ],
        [
            pltpu.VMEM((features, features), bf16),
            pltpu.VMEM((features, 3 * features), bf16),
            pltpu.VMEM((features, features), bf16),
            pltpu.VMEM((chunk, 3 * features), bf16),
            pltpu.VMEM((chunk, features), f32),
            pltpu.VMEM((rows, features), f32),
            pltpu.VMEM((rows, 3 * features), f32),
            pltpu.VMEM((rows, features), f32),
            pltpu.SemaphoreType.DMA((3, count)),
        ],
        1,
        1,
        deps,
    )(meta, total_grad, cls, act, proj, mix, message, params, *weights.arrays)


def chip_slot(chip, x_first):
    if not x_first:
        return chip
    return ((chip & 1) << 1) | (chip >> 1)


def scatter_rows(s, product, rows, fast, mp, refs, x_first):
    if not fast:
        for d in range(mp):
            refs[0][d] = product[d * rows : (d + 1) * rows].astype(bf16)
        return
    even = (s[0] & 1) == 0
    for pair in range(mp // 2):
        low = product[2 * pair * rows : (2 * pair + 1) * rows].astype(bf16)
        high = product[(2 * pair + 1) * rows : (2 * pair + 2) * rows].astype(bf16)
        slot = chip_slot(jnp.bitwise_xor(s[0] >> 1, pair), x_first)
        refs[0][slot] = jnp.where(even, low, high)
        refs[1][slot] = jnp.where(even, high, low)


def weight_grad(meta, jobs, outs, rows, fast, mp, x_first, deps=()):
    features = jobs[0][0].shape[1]
    tokens = jobs[0][0].shape[0]
    steps = len(jobs)
    copies = 2 if fast else 1
    lefts, rights = [], []
    for left, right, _, _, _ in jobs:
        if all(left is not x for x in lefts):
            lefts.append(left)
        if all(right is not x for x in rights):
            rights.append(right)
    left_of = [next(i for i, x in enumerate(lefts) if x is job[0]) for job in jobs]
    right_of = [next(i for i, x in enumerate(rights) if x is job[1]) for job in jobs]

    def body(s, *refs):
        left_refs, refs = refs[: len(lefts)], refs[len(lefts) :]
        right_refs, refs = refs[: len(rights)], refs[len(rights) :]
        out_refs, scratch = refs[: copies * len(outs)], refs[-1]
        step = pl.program_id(0)
        for number in range(len(lefts)):

            @pl.when(step == left_of.index(number))
            def _(number=number):
                scratch[...] = transpose(left_refs[number][...])

        for number in range(len(rights)):
            for target in range(len(outs)):
                mine = [
                    i for i in range(steps) if right_of[i] == number and jobs[i][3] == target
                ]
                if not mine:
                    continue

                @pl.when(jnp.logical_and(step >= mine[0], step <= mine[-1]))
                def _(number=number, target=target):
                    product = nn(scratch[...], right_refs[number][...])
                    scatter_rows(
                        s, product, rows, fast, mp,
                        out_refs[copies * target : copies * (target + 1)],
                        x_first[target],
                    )

    def index_map(values, make):
        def pick(i, s):
            index = values[0]
            for number in range(1, steps):
                index = jnp.where(i >= number, values[number], index)
            return make(index)

        return pick

    def held(number, of, column):
        values, last = [], None
        for i in range(steps):
            if of[i] == number:
                last = jobs[i][column]
            values.append(last)
        first = next(v for v in values if v is not None)
        return [first if v is None else v for v in values]

    in_specs = [whole((tokens, features)) for _ in lefts]
    for number in range(len(rights)):
        in_specs.append(
            pl.BlockSpec(
                (tokens, features),
                index_map(held(number, right_of, 2), lambda index: (0, index)),
            )
        )
    out_of = [job[3] for job in jobs]
    out_specs, out_shape = [], []
    lead = mp // 2 if fast else mp
    for target, columns in enumerate(outs):
        spec = pl.BlockSpec(
            (lead, rows, features),
            index_map(held(target, out_of, 4), lambda index: (0, 0, index)),
        )
        for _ in range(copies):
            out_specs.append(spec)
            out_shape.append(sds((lead, rows, columns), bf16))
    results = call(
        body,
        out_shape,
        (steps,),
        in_specs,
        out_specs,
        [pltpu.VMEM((features, tokens), bf16)],
        2 * steps * tokens * features * features,
        (2 * steps + 1) * tokens * features * 2,
        deps,
    )(meta, *lefts, *rights)
    grouped = [results[copies * t : copies * (t + 1)] for t in range(len(outs))]
    if not fast:
        return grouped
    return [[x.reshape((2, 2) + x.shape[1:]) for x in pair] for pair in grouped]


def hidden_weight_grad(meta, cotangent, hidden, ids, all_videos, rows, mp, deps=()):
    n, patches, features = cotangent.shape
    tokens = n * ROWS
    count = features + all_videos
    wide = features + -(-all_videos // 128) * 128
    blocks = features // rows if rows % 128 == 0 else 0
    width = features

    def body(s, cot_ref, ids_ref, hidden_ref, *refs):
        left, scratch = refs[-2:]

        @pl.when(pl.program_id(0) == 0)
        def _():
            lane = lax.broadcasted_iota(jnp.int32, (patches, wide - features), 1)
            left[...] = jnp.zeros_like(left)
            for f in range(n):
                here = slice(f * ROWS, f * ROWS + patches)
                left[here, :features] = cot_ref[f].astype(f32)
                left[here, features:] = (lane == ids_ref[f : f + 1, :1]).astype(f32)
            scratch[...] = jnp.transpose(left[...]).astype(bf16)

        product = nn(scratch[...], hidden_ref[...]).astype(bf16)[:count]
        for d in range(blocks):
            refs[0][d] = product[:, d * rows : (d + 1) * rows]
        if not blocks:
            refs[0][...] = product

    if blocks:
        out_spec = pl.BlockSpec((blocks, count, rows), lambda i, s: (i, 0, 0))
        out_shape = sds((mp, count, rows), bf16)
    else:
        out_spec = pl.BlockSpec((count, width), lambda i, s: (0, i))
        out_shape = sds((count, hidden.shape[1]), bf16)
    results = call(
        body,
        [out_shape],
        (hidden.shape[1] // width,),
        [
            whole((n, patches, features)),
            whole((8, 128)),
            pl.BlockSpec((tokens, width), lambda i, s: (0, i)),
        ],
        [out_spec],
        [pltpu.VMEM((tokens, wide), f32), pltpu.VMEM((wide, tokens), bf16)],
        2 * tokens * features * hidden.shape[1],
        (hidden.shape[1] + features) * tokens * 2,
        deps,
    )(meta, cotangent, ids, hidden)
    if blocks:
        return results[0]
    return results[0].reshape(count, mp, rows).transpose(1, 0, 2)


def local(
    videos,
    mp,
    frames,
    cotangent,
    frame_video,
    group_ids,
    message_fc,
    message_gain,
    message_shift,
    message_qkv,
    message_out,
    pre_gain,
    pre_shift,
    attn_qkv,
    attn_out,
    mlp_gain,
    mlp_shift,
    fc_in,
    fc_out,
):
    n, patches, features = frames.shape
    rows = message_fc.shape[0]
    fast = (videos, mp) == (4, 8)
    z = lax.axis_index("videos")
    me = lax.axis_index("mp")
    group_videos = frame_video.shape[0] // FPV
    pad_videos = -(-group_videos // 8) * 8
    device_rows = 8 * (z * mp + me)
    meta = jnp.stack([me, z, device_rows // 256, lax.rem(device_rows, 256)]).astype(jnp.int32)

    own_video = lax.dynamic_slice_in_dim(frame_video, me * n, n)
    own_video = jnp.concatenate([own_video, jnp.full((8 - n,), -1, own_video.dtype)])
    onehot = (
        (own_video - z * group_videos)[None, :] == jnp.arange(pad_videos)[:, None]
    ).astype(f32)
    norms = jnp.concatenate(
        [message_gain, message_shift, pre_gain, pre_shift, mlp_gain, mlp_shift]
    )
    cls = jnp.concatenate(
        [
            jnp.concatenate(
                [
                    frames[:, 0, :],
                    jnp.pad(norms, (0, features - 6 * rows))[None, :],
                    jnp.zeros((7 - n, features), bf16),
                ]
            ),
            jnp.broadcast_to(own_video.astype(bf16)[:, None], (8, PACK)),
        ],
        axis=1,
    )
    qkv_w = gather_weights(attn_qkv, fast, mp)
    cls_steps = gather_small(tie(cls, *qkv_w.arrays[2:4]), fast, videos, mp)
    next(cls_steps)
    small = next(cls_steps)
    next(cls_steps)
    norms = next(cls_steps)[:, n, : 6 * rows].reshape(mp, 6, rows).transpose(1, 0, 2)
    params = jnp.pad(norms.reshape(6, features).astype(f32), ((0, 10), (0, 0)))
    pre_act, qkv = frame_projection(meta, frames, params, qkv_w)
    early = qkv_w.arrays[4:6] + [small] if fast else ()
    message_w = gather_weights(
        pack_columns(meta, [[attn_out, message_fc, message_qkv, message_out]])[0],
        fast, mp, first=early, relay=[qkv],
    )
    in_w = gather_whole(fc_in, mp, early)
    out_w = gather_whole(fc_out, mp, early)
    cls_steps.send([qkv])
    next(cls_steps)
    cls_all = next(cls_steps)
    msg_act, msg_proj, msg_mix, message, msg_total = message_forward(
        meta, cls_all, params, message_w
    )
    own_total = lax.dynamic_slice_in_dim(msg_total, device_rows, 8)
    attn_act, attn_proj, probs, mixed, residual = attention_forward(
        meta, frames, own_total, params, pre_act, qkv, qkv_w, message_w
    )
    pre_act, qkv = attn_act, attn_proj
    mlp_act, hidden_pre, hidden = mlp_in(meta, residual, params, in_w)
    all_videos = videos * pad_videos
    own_place = jnp.where(own_video < 0, -1, own_video - z * group_videos + z * pad_videos)
    out_parts = hidden_weight_grad(
        meta, cotangent, hidden.reshape(n * ROWS, -1),
        jnp.broadcast_to(own_place.astype(jnp.int32)[:, None], (8, 128)),
        all_videos, fc_out.shape[0], mp,
    )
    out_share = scatter_sum(out_parts)
    out_frames, video_part = mlp_out(
        meta, residual, hidden, onehot, out_w, patches, [out_parts]
    )
    pooled = gather_videos(sum_small(video_part, fast, mp), fast, videos)
    ids = jnp.pad(group_ids.reshape(videos, group_videos), ((0, 0), (0, pad_videos - group_videos)))
    ids = ids.reshape(-1)
    loss, frame_grad, video_grad = contrast(
        meta,
        pooled,
        jnp.broadcast_to(ids[:, None], (ids.shape[0], 128)),
        jnp.broadcast_to(ids[None, :], (8, ids.shape[0])),
        onehot,
        group_videos,
        patches,
    )
    pre_grad, residual_grad, low, mlp_norm = mlp_backward(
        meta, cotangent, frame_grad, hidden_pre, residual, params, in_w, out_w
    )
    flat = lambda a: a.reshape(n * ROWS, a.shape[-1])
    act_flat, pre_flat = flat(mlp_act), flat(pre_grad)
    halves = [2 * features, fc_in.shape[1] - 2 * features]
    in_parts = weight_grad(
        meta,
        [
            (act_flat, pre_flat, c, c // 2, c % 2)
            for c in range(fc_in.shape[1] // features)
        ],
        halves, rows, fast, mp, (True, False), [out_share],
    )
    in_reds = [Reduce(x, fast, videos, mp, i == 0) for i, x in enumerate(in_parts)]

    def in_step(*after):
        return [red.step(after) for red in in_reds]

    in_1 = in_step()
    out_along = Along([tie(out_share, pre_grad)], fast, videos)
    out_1 = out_along.step()
    mixed_grad, total_grad = message_token_backward(
        meta, low, mixed, qkv, probs, own_total, params, qkv_w, message_w, patches,
        [in_parts[0][0]] + out_1,
    )
    wide = -(-(1 << 20) // (mp * features * 2 * 8)) * 8
    grads_plane = lax.all_gather(
        jnp.pad(total_grad, ((0, wide - 8), (0, 0))), "mp", axis=0, tiled=False
    )
    out_2 = out_along.step()
    in_2 = in_step(mixed_grad)
    sent = [red.sent for red in in_reds] if fast else []
    qkv_grad = attention_backward(meta, mixed_grad, qkv, probs, in_1 + out_2 + sent)
    grads_plane = tie(grads_plane, qkv_grad)[:, :8].reshape(mp * 8, features)
    grads_all = gather_along(grads_plane, fast, videos)
    in_3 = in_step(qkv_grad)
    next(grads_all)
    grads_1 = next(grads_all)
    stacked_flat, qkv_flat, mixed_flat, low_flat = map(flat, (pre_act, qkv_grad, mixed, low))
    ((attn_parts,),) = weight_grad(
        meta,
        [(stacked_flat, qkv_flat, c, 0, c) for c in range(3)] + [(mixed_flat, low_flat, 0, 0, 3)],
        [4 * features], rows, False, mp, (True,), in_2,
    )
    attn_share = scatter_sum(attn_parts)
    in_4 = in_step(attn_parts)
    grads_2 = grads_all.send([attn_parts])
    frames_grad, first_token, pre_norm = stacked_backward(
        meta, qkv_grad, frames, own_total, residual_grad, params, qkv_w, [grads_1, attn_parts]
    )
    norms_all = sum_all(
        jnp.concatenate([pre_norm[:2], mlp_norm[:2], jnp.zeros((4, features), f32)], axis=0),
        fast, videos, mp,
    )
    norms_1, norms_2 = next(norms_all), next(norms_all)
    total_grads = grads_all.send([frames_grad])
    grad_message_fc, grad_message_qkv, grad_message_out, message_norm, class_grad = (
        message_backward(
            meta, total_grads, cls_all, msg_act, msg_proj, msg_mix, message, params, message_w,
            rows, in_3 + [norms_1],
        )
    )
    norms_all.send([class_grad])
    in_5 = in_step(frames_grad)
    norm_sums = next(norms_all)[:4]
    grad_fc_in = jnp.concatenate([red.result([class_grad]) for red in in_reds], axis=1)
    (grad_fc_out,) = out_along.result([class_grad])
    attn_share = tie(attn_share, class_grad)
    attn_along = Along([attn_share[:, : 2 * features], attn_share[:, 2 * features :]], fast, videos)
    attn_along.step(), attn_along.step()
    first_grad, second_grad = attn_along.result()
    grad_fc_out = grad_fc_out[:features] + lax.dot_general(
        video_grad, grad_fc_out[features:], (((0,), (0,)), ((), ())), precision=HIGH
    )
    tokens = (first_token + class_grad)[:n].astype(bf16)
    frames_grad = lax.dynamic_update_slice(frames_grad, tokens[:, None, :], (0, 0, 0))
    norm_all = jnp.concatenate([message_norm[:2], norm_sums], axis=0)
    norm_own = lax.dynamic_slice_in_dim(norm_all, me * rows, rows, 1).astype(bf16)
    return (
        out_frames,
        loss[0, 0],
        frames_grad,
        grad_message_fc,
        norm_own[0],
        norm_own[1],
        grad_message_qkv,
        grad_message_out,
        norm_own[2],
        norm_own[3],
        jnp.concatenate([first_grad, second_grad[:, :features]], axis=1).astype(bf16),
        second_grad[:, features:].astype(bf16),
        norm_own[4],
        norm_own[5],
        grad_fc_in.astype(bf16),
        grad_fc_out.T.astype(bf16),
    )


def solution(mesh):
    weight, norm = P("mp", None), P("mp")
    frame = P(("videos", "mp"), None, None)
    params = (
        weight, norm, norm, weight, weight, norm, norm, weight, weight, norm, norm, weight, weight,
    )
    return jax.shard_map(
        functools.partial(local, mesh.shape["videos"], mesh.shape["mp"]),
        mesh=mesh,
        in_specs=(frame, frame, P("videos"), P()) + params,
        out_specs=(frame, P(), frame) + params,
        check_vma=False,
    )
```

```python
import functools

import jax
import jax.numpy as jnp
from jax import lax
from jax.experimental import pallas as pl
from jax.experimental.pallas import tpu as pltpu
from jax.sharding import PartitionSpec as P

HEADS = 12
FPV = 16
EPS = 1e-05
LOGIT_SCALE = 50.0
ROWS = 208
PACK = 128
VMEM = 60 * 1024 * 1024

f32 = jnp.float32
bf16 = jnp.bfloat16
HIGH = lax.Precision.HIGHEST


def nn(a, b, precision=None):
    return jnp.dot(a, b, preferred_element_type=f32, precision=precision)


def nt(a, b, precision=None):
    return lax.dot_general(
        a, b, (((1,), (1,)), ((), ())), preferred_element_type=f32, precision=precision
    )


def norm_parts(x):
    mean = jnp.mean(x, axis=-1, keepdims=True)
    centred = x - mean
    var = jnp.mean(centred * centred, axis=-1, keepdims=True)
    rstd = lax.rsqrt(var + EPS)
    return centred * rstd, rstd


def norm_back(grad, xhat, rstd, gain):
    gy = grad * gain
    return rstd * (
        gy
        - jnp.mean(gy, axis=-1, keepdims=True)
        - xhat * jnp.mean(gy * xhat, axis=-1, keepdims=True)
    )


def sigmoid(x):
    return 0.5 * jnp.tanh(0.5 * x) + 0.5


def lane_masks(dtype):
    lane = lax.broadcasted_iota(jnp.int32, (1, 128), 1)
    low = (lane < 64).astype(f32)
    return low.astype(dtype), (1.0 - low).astype(dtype)


def transpose(x):
    return jnp.transpose(x.astype(f32)).astype(x.dtype)


def pair_probs(q2, k2, valid):
    m0, m1 = lane_masks(bf16)
    qs = q2 * jnp.asarray(0.125, bf16)
    keys = jnp.concatenate([k2 * m0, k2 * m1], axis=0)
    scores = nt(keys, qs)
    count = k2.shape[0]
    out = []
    for j in range(2):
        s = jnp.where(valid, scores[j * count : (j + 1) * count], -1e30)
        e = jnp.exp(s - jnp.max(s, axis=0, keepdims=True))
        out.append(e * (1.0 / jnp.sum(e, axis=0, keepdims=True)))
    return out


def pair_mix(v2, p0, p1):
    vt = transpose(v2)
    mixed = jnp.concatenate([nn(vt[:64], p0), nn(vt[64:], p1)], axis=0)
    return jnp.transpose(mixed)


def pair_back(q2, k2, v2, dm2, p0, p1):
    m0, m1 = lane_masks(bf16)
    count = k2.shape[0]
    lane = lax.broadcasted_iota(jnp.int32, (1, 128), 1) < 64
    eighth = jnp.asarray(0.125, bf16)
    dps = nt(jnp.concatenate([v2 * m0, v2 * m1], axis=0), dm2)
    lows, grads = [], []
    for j, p in enumerate((p0, p1)):
        dp = dps[j * count : (j + 1) * count]
        p_full = p.astype(f32)
        row = jnp.sum(dp * p_full, axis=0, keepdims=True)
        grads.append((p_full * (dp - row)).astype(bf16))
        lows.append(p.astype(bf16))
    dv = nn(jnp.concatenate(lows, axis=0), dm2)
    dk = nn(jnp.concatenate(grads, axis=0), q2 * eighth)
    kt = transpose(k2 * eighth)
    dq = jnp.transpose(
        jnp.concatenate([nn(kt[:64], grads[0]), nn(kt[64:], grads[1])], axis=0)
    )
    return dq, jnp.where(lane, dk[:count], dk[count:]), jnp.where(lane, dv[:count], dv[count:])


def call(body, out_shape, grid, in_specs, out_specs, scratch, flops, bytes_accessed, deps=()):
    count = 1 + len(in_specs)
    deps = tuple(deps)

    def run(*refs):
        return body(*refs[:count], *refs[count + len(deps) :])

    function = pl.pallas_call(
        run,
        out_shape=out_shape,
        grid_spec=pltpu.PrefetchScalarGridSpec(
            num_scalar_prefetch=1,
            grid=grid,
            in_specs=list(in_specs) + [ANY] * len(deps),
            out_specs=out_specs,
            scratch_shapes=scratch,
        ),
        compiler_params=pltpu.CompilerParams(
            dimension_semantics=("arbitrary",) * len(grid), vmem_limit_bytes=VMEM
        ),
        cost_estimate=pl.CostEstimate(
            flops=int(2 * flops), bytes_accessed=bytes_accessed, transcendentals=0
        ),
    )
    return lambda *arrays: function(*arrays, *deps)


ANY = pl.BlockSpec(memory_space=pl.ANY)


def whole(shape):
    return pl.BlockSpec(shape, lambda i, s: (0,) * len(shape))


def per_step(shape):
    return pl.BlockSpec((1,) + shape, lambda i, s: (i,) + (0,) * len(shape))


def sds(shape, dtype):
    return jax.ShapeDtypeStruct(shape, dtype)


def pack_columns(meta, groups):
    arrays = [x for group in groups for x in group]
    rows, count = arrays[0].shape[0], len(arrays)
    widths = [sum(x.shape[1] for x in group) for group in groups]

    def body(s, *refs):
        ins, outs = list(refs[:count]), refs[count:]
        for group, out in zip(groups, outs):
            first = 0
            for x in group:
                out[:, first : first + x.shape[1]] = ins.pop(0)[...]
                first += x.shape[1]

    return call(
        body,
        [sds((rows, width), bf16) for width in widths],
        (1,),
        [whole(x.shape) for x in arrays],
        [whole((rows, width)) for width in widths],
        [],
        0,
        4 * rows * sum(widths),
    )(meta, *arrays)


class Weights:
    def __init__(self, arrays, places, rows):
        self.arrays = arrays
        self.places = places
        self.rows = rows

    def copies(self, refs, me, sems, first, columns, dst):
        out = []
        for number, (ref, (slot, start, count)) in enumerate(zip(refs, self.places)):
            if slot is None:
                target = dst
            else:
                offset = jnp.bitwise_xor(me, slot) * self.rows + start
                target = dst.at[pl.ds(pl.multiple_of(offset, 16), count), :]
            out.append(
                pltpu.make_async_copy(
                    ref.at[:, pl.ds(first, columns)], target, sems.at[number]
                )
            )
        return out


def run_copies(copies):
    for copy in copies:
        copy.start()
    for copy in copies:
        copy.wait()


def swap(x, axis, size, bit):
    return lax.ppermute(x, axis, [(i, i ^ bit) for i in range(size)])


def tie(x, *arrays):
    return lax.optimization_barrier((x,) + arrays)[0]


def gather_weights(x, fast, mp, first=(), relay=(), swaps=(), late=()):
    rows = x.shape[0]
    if not fast:
        full = lax.all_gather(x, "mp", axis=0, tiled=True)
        return Weights([full], [(None, 0, rows * mp)], rows)
    half = rows // 2
    x = tie(x, *first)
    from_x = swap(x, "mp", mp, 2)
    from_y = swap(x, "mp", mp, 4)
    own_c = swap(tie(x, *swaps), "mp", mp, 1)
    arrays = [
        x,
        own_c,
        from_x,
        from_y,
        swap(tie(from_x, *relay)[:half], "mp", mp, 4),
        swap(tie(from_y, *relay)[half:], "mp", mp, 2),
    ]
    places = [(0, 0, rows), (1, 0, rows), (2, 0, rows), (4, 0, rows), (6, 0, half), (6, half, half)]
    for number in range(2, 6):
        slot, start, count = places[number]
        wait = late if number > 3 else swaps
        arrays.append(swap(tie(arrays[number], *wait), "mp", mp, 1))
        places.append((slot ^ 1, start, count))
    return Weights(arrays, places, rows)


def gather_whole(x, mp, first=()):
    rows = x.shape[0]
    full = lax.all_gather(tie(x, *first), "mp", axis=0, tiled=True)
    return Weights([full], [(None, 0, rows * mp)], rows)


def gather_small(x, fast, videos, mp):
    if not fast:
        for _ in range(3):
            yield x
        yield lax.all_gather(x, "mp", axis=0, tiled=False)
        whole_x = lax.all_gather(x, ("videos", "mp"), axis=0, tiled=True)
        while True:
            yield whole_x
    z = lax.axis_index("videos")
    me = lax.axis_index("mp")
    shape = x.shape
    x = x.reshape((1,) * 4 + shape)

    def ordered(own_first, own, other):
        return jnp.where(own_first, own, other), jnp.where(own_first, other, own)

    for bit, place in ((2, 2), (4, 1), (1, 3)):
        other = swap(x, "mp", mp, bit)
        yield other
        x = jnp.concatenate(ordered((me & bit) == 0, x, other), axis=place)
    after = yield x.reshape((-1,) + shape)
    x = tie(x, *after)
    other = swap(x, "videos", videos, 3)
    yield other
    x = jnp.concatenate(ordered(z < 2, x, other), axis=0)
    other = swap(x, "videos", videos, 1)
    yield other
    outer, inner = ordered(jnp.logical_or(z == 0, z == 3), x, other)
    x = jnp.concatenate([outer[:1], inner, outer[1:]], axis=0)
    yield x.reshape((videos * mp * shape[0],) + shape[1:])


def gather_along(x, fast, videos):
    if not fast:
        whole_x = lax.all_gather(x, "videos", axis=0, tiled=True)
        yield x
        while True:
            yield whole_x
    z = lax.axis_index("videos")
    yield x
    x = x[None]
    other = swap(x, "videos", videos, 3)
    after = yield other
    other = tie(other, *after)
    x = jnp.concatenate([jnp.where(z < 2, x, other), jnp.where(z < 2, other, x)])
    other = swap(x, "videos", videos, 1)
    after = yield other
    other = tie(other, *after)
    own_outer = jnp.logical_or(z == 0, z == 3)
    outer, inner = jnp.where(own_outer, x, other), jnp.where(own_outer, other, x)
    x = jnp.concatenate([outer[:1], inner, outer[1:]])
    yield x.reshape((-1,) + x.shape[2:])


def drain(steps, count=5):
    for _ in range(count):
        next(steps)
    return next(steps)


def sum_all(x, fast, videos, mp):
    if not fast:
        total = lax.psum(x, ("videos", "mp"))
        while True:
            yield total
    other = swap(x, "mp", mp, 1)
    yield other
    x = x + other
    others = plane_sum(x, mp)
    after = yield others[0]
    x = add_four(x, tuple(tie(y, *after) for y in others))
    others = along_all(x, videos)
    yield others[0]
    yield add_four(x, others)


def plane_sum(x, mp):
    return swap(x, "mp", mp, 2), swap(x, "mp", mp, 4), swap(x, "mp", mp, 6)


def add_four(x, others):
    return (x + others[0]) + (others[1] + others[2])


def along_all(x, videos):
    return tuple(swap(x, "videos", videos, bit) for bit in (1, 2, 3))


def sum_small(x, fast, mp):
    if not fast:
        return lax.psum(x, "mp")
    x = x + swap(x, "mp", mp, 1)
    return add_four(x, plane_sum(x, mp))


def gather_videos(x, fast, videos):
    if not fast:
        return lax.all_gather(x, "videos", axis=0, tiled=True)
    z = lax.axis_index("videos")
    parts = (x,) + along_all(x, videos)
    for bit in (1, 2):
        flip = (z & bit) != 0
        parts = tuple(jnp.where(flip, parts[i ^ bit], parts[i]) for i in range(4))
    return jnp.concatenate(parts, axis=0)


class Reduce:
    def __init__(self, parts, fast, videos, mp, x_first):
        self.parts, self.fast, self.videos, self.mp = parts, fast, videos, mp
        self.bits, self.zbits = ((2, 4), (1, 3)) if x_first else ((4, 2), (3, 1))
        self.number = 0
        if not fast:
            share = lax.psum_scatter(parts[0], "mp", scatter_dimension=0, tiled=False)
            self.total = lax.psum(share, "videos").astype(f32)

    def step(self, after=()):
        if not self.fast:
            return self.total
        number, self.number = self.number, self.number + 1
        if number == 0:
            self.keep, send = self.parts
            self.other = swap(tie(send, *after), "mp", self.mp, 1)
            return self.other
        other = tie(self.other, *after)
        if number == 1:
            self.first = other
            far = self.keep[1].astype(f32) + other[1].astype(f32)
            self.sent = far.astype(bf16)
            self.other = swap(self.sent, "mp", self.mp, self.bits[0])
        elif number == 2:
            near = self.keep[0].astype(f32) + self.first[0].astype(f32) + other.astype(f32)
            self.near = near[0]
            self.other = swap(near[1].astype(bf16), "mp", self.mp, self.bits[1])
        else:
            if number == 3:
                self.total = (self.near + other.astype(f32)).astype(bf16)
            else:
                self.total = (self.total.astype(f32) + other.astype(f32)).astype(bf16)
            self.other = swap(self.total, "videos", self.videos, self.zbits[number - 3])
        return self.other

    def result(self, after=()):
        if not self.fast:
            return self.total
        return self.total.astype(f32) + tie(self.other, *after).astype(f32)


def scatter_sum(x, after=()):
    return lax.psum_scatter(tie(x, *after), "mp", scatter_dimension=0, tiled=False)


class Along:
    def __init__(self, arrays, fast, videos):
        self.arrays, self.fast, self.videos = list(arrays), fast, videos
        self.number = 0
        if not fast:
            self.arrays = [lax.psum(x, "videos") for x in self.arrays]

    def add(self, after=()):
        self.arrays = [
            x.astype(f32) + tie(y, *after).astype(f32) for x, y in zip(self.arrays, self.others)
        ]

    def step(self, after=()):
        if not self.fast:
            return self.arrays
        if self.number:
            self.add(after)
        low = [x.astype(bf16) for x in self.arrays]
        order = ((3, 1), (1, 3))
        self.others = [
            swap(x, "videos", self.videos, order[i % 2][self.number]) for i, x in enumerate(low)
        ]
        self.arrays = low
        self.number += 1
        return self.others

    def result(self, after=()):
        if self.fast:
            self.add(after)
        return [x.astype(f32) for x in self.arrays]


def message_forward(meta, cls, params, weights, deps=()):
    rows = cls.shape[0]
    features = params.shape[1]
    chunk = min(rows, 256)
    count = len(weights.arrays)

    def body(s, cls_ref, params_ref, *rest):
        pieces, rest = rest[:count], rest[count:]
        act_ref, proj_ref, mix_ref, message_ref, total_ref = rest[:5]
        fc_w, qkv_w, out_w, sems = rest[5:]

        @pl.when(pl.program_id(0) == 0)
        def _():
            copies = []
            for number, (first, columns, dst) in enumerate(
                (
                    (features, features, fc_w),
                    (2 * features, 3 * features, qkv_w),
                    (5 * features, features, out_w),
                )
            ):
                copies += weights.copies(pieces, s[0], sems.at[number], first, columns, dst)
            run_copies(copies)

        ids = cls_ref[:, features:].astype(f32)
        same = ids[:, :1] == jnp.transpose(ids)[:1, :]
        message = nn(cls_ref[:, :features], fc_w[...])
        message_ref[...] = message
        xhat, _ = norm_parts(message)
        act_ref[...] = (xhat * params_ref[0:1] + params_ref[1:2]).astype(bf16)
        proj_ref[...] = nn(act_ref[...], qkv_w[...]).astype(bf16)
        for p in range(HEADS // 2):
            q2, k2, v2 = (
                proj_ref[:, part * features + p * 128 : part * features + (p + 1) * 128]
                for part in range(3)
            )
            p0, p1 = pair_probs(q2, k2, same)
            mix_ref[:, p * 128 : (p + 1) * 128] = pair_mix(
                v2, p0.astype(bf16), p1.astype(bf16)
            ).astype(bf16)
        total_ref[...] = message_ref[...] + nn(mix_ref[...], out_w[...])

    def block(columns):
        return pl.BlockSpec((chunk, columns), lambda i, s: (i, 0))

    return call(
        body,
        [
            sds((rows, features), bf16),
            sds((rows, 3 * features), bf16),
            sds((rows, features), bf16),
            sds((rows, features), f32),
            sds((rows, features), f32),
        ],
        (rows // chunk,),
        [block(features + PACK), whole((16, features))] + [ANY] * count,
        [
            block(features),
            block(3 * features),
            block(features),
            block(features),
            block(features),
        ],
        [
            pltpu.VMEM((features, features), bf16),
            pltpu.VMEM((features, 3 * features), bf16),
            pltpu.VMEM((features, features), bf16),
            pltpu.SemaphoreType.DMA((3, count)),
        ],
        2 * rows * 5 * features * features,
        12 * features * features,
        deps,
    )(meta, cls, params, *weights.arrays)


def frame_projection(meta, frames, params, weights, deps=()):
    n, patches, features = frames.shape
    count = len(weights.arrays)

    def body(s, frames_ref, params_ref, *rest):
        pieces, rest = rest[:count], rest[count:]
        act_ref, qkv_ref, qkv_w, stacked, sems = rest

        @pl.when(pl.program_id(0) == 0)
        def _():
            run_copies(weights.copies(pieces, s[0], sems, 0, 3 * features, qkv_w))
            stacked[...] = jnp.zeros_like(stacked)

        stacked[0:patches] = frames_ref[0].astype(f32)
        xhat, _ = norm_parts(stacked[...])
        act_ref[0] = (xhat * params_ref[2:3] + params_ref[3:4]).astype(bf16)
        qkv_ref[0] = nn(act_ref[0], qkv_w[...]).astype(bf16)

    return call(
        body,
        [
            sds((n, ROWS, features), bf16),
            sds((n, ROWS, 3 * features), bf16),
        ],
        (n,),
        [per_step((patches, features)), whole((16, features))] + [ANY] * count,
        [per_step((ROWS, features)), per_step((ROWS, 3 * features))],
        [
            pltpu.VMEM((features, 3 * features), bf16),
            pltpu.VMEM((ROWS, features), f32),
            pltpu.SemaphoreType.DMA((count,)),
        ],
        2 * n * ROWS * 3 * features * features,
        16 * 1024 * 1024,
        deps,
    )(meta, frames, params, *weights.arrays)


def attention_forward(meta, frames, total, params, act, qkv, weights, out_weights, deps=()):
    n, patches, features = frames.shape
    count, count_out = len(weights.arrays), len(out_weights.arrays)

    def body(s, frames_ref, total_ref, params_ref, act_in, qkv_in, *rest):
        pieces, rest = rest[:count], rest[count:]
        out_pieces, rest = rest[:count_out], rest[count_out:]
        act_ref, qkv_ref, probs_ref, mixed_ref, residual_ref = rest[:5]
        qkv_w, out_w, stacked, act_rows, qkv_rows, sems = rest[5:]
        f = pl.program_id(0)

        @pl.when(f == 0)
        def _():
            copies = weights.copies(pieces, s[0], sems.at[0], 0, 3 * features, qkv_w)
            copies += out_weights.copies(out_pieces, s[0], sems.at[1], 0, features, out_w)
            run_copies(copies)
            stacked[...] = jnp.zeros_like(stacked)
            xhat, _ = norm_parts(total_ref[...])
            rows = xhat * params_ref[2:3] + params_ref[3:4]
            act_rows[...] = rows
            qkv_rows[...] = nn(rows.astype(bf16), qkv_w[...])

        stacked[0:patches] = frames_ref[0].astype(f32)
        message_row = lax.broadcasted_iota(jnp.int32, (ROWS, 1), 0) == patches
        act_ref[0] = jnp.where(
            message_row, act_rows[pl.ds(f, 1), :], act_in[0].astype(f32)
        ).astype(bf16)
        qkv_ref[0] = jnp.where(
            message_row, qkv_rows[pl.ds(f, 1), :], qkv_in[0].astype(f32)
        ).astype(bf16)
        valid = lax.broadcasted_iota(jnp.int32, (ROWS, 1), 0) < patches + 1
        for p in range(HEADS // 2):
            q2, k2, v2 = (
                qkv_ref[0, :, part * features + p * 128 : part * features + (p + 1) * 128]
                for part in range(3)
            )
            p0, p1 = pair_probs(q2, k2, valid)
            p0, p1 = p0.astype(bf16), p1.astype(bf16)
            probs_ref[0, p, 0] = p0
            probs_ref[0, p, 1] = p1
            mixed_ref[0, :, p * 128 : (p + 1) * 128] = pair_mix(v2, p0, p1).astype(bf16)
        residual_ref[0] = stacked[...] + nn(mixed_ref[0], out_w[...])

    return call(
        body,
        [
            sds((n, ROWS, features), bf16),
            sds((n, ROWS, 3 * features), bf16),
            sds((n, HEADS // 2, 2, ROWS, ROWS), bf16),
            sds((n, ROWS, features), bf16),
            sds((n, ROWS, features), f32),
        ],
        (n,),
        [
            per_step((patches, features)),
            whole((8, features)),
            whole((16, features)),
            per_step((ROWS, features)),
            per_step((ROWS, 3 * features)),
        ]
        + [ANY] * (count + count_out),
        [
            per_step((ROWS, features)),
            per_step((ROWS, 3 * features)),
            per_step((HEADS // 2, 2, ROWS, ROWS)),
            per_step((ROWS, features)),
            per_step((ROWS, features)),
        ],
        [
            pltpu.VMEM((features, 3 * features), bf16),
            pltpu.VMEM((features, features), bf16),
            pltpu.VMEM((ROWS, features), f32),
            pltpu.VMEM((8, features), f32),
            pltpu.VMEM((8, 3 * features), f32),
            pltpu.SemaphoreType.DMA((2, count)),
        ],
        2 * n * ROWS * (features * features + 2 * ROWS * features),
        32 * 1024 * 1024,
        deps,
    )(meta, frames, total, params, act, qkv, *weights.arrays, *out_weights.arrays)


def mlp_in(meta, residual, params, win, deps=()):
    n, _, features = residual.shape
    hidden_units = win.arrays[0].shape[1]
    count = len(win.arrays)
    chunks = hidden_units // features

    def body(s, residual_ref, params_ref, *rest):
        pieces, rest = rest[:count], rest[count:]
        act_ref, pre_ref, hidden_ref, in_w, sems = rest

        @pl.when(pl.program_id(0) == 0)
        def _():
            run_copies(win.copies(pieces, s[0], sems, 0, hidden_units, in_w))

        xhat, _ = norm_parts(residual_ref[0])
        act_ref[0] = (xhat * params_ref[4:5] + params_ref[5:6]).astype(bf16)
        for c in range(chunks):
            columns = slice(c * features, (c + 1) * features)
            pre = nn(act_ref[0], in_w[:, columns])
            pre_ref[0, :, columns] = pre.astype(bf16)
            hidden_ref[0, :, columns] = (pre * sigmoid(1.702 * pre)).astype(bf16)

    return call(
        body,
        [
            sds((n, ROWS, features), bf16),
            sds((n, ROWS, hidden_units), bf16),
            sds((n, ROWS, hidden_units), bf16),
        ],
        (n,),
        [per_step((ROWS, features)), whole((16, features))] + [ANY] * count,
        [
            per_step((ROWS, features)),
            per_step((ROWS, hidden_units)),
            per_step((ROWS, hidden_units)),
        ],
        [pltpu.VMEM((features, hidden_units), bf16), pltpu.SemaphoreType.DMA((count,))],
        2 * n * ROWS * features * hidden_units,
        24 * 1024 * 1024,
        deps,
    )(meta, residual, params, *win.arrays)


def mlp_out(meta, residual, hidden, onehot, wout, patches, deps=()):
    n, _, features = residual.shape
    hidden_units = hidden.shape[2]
    count = len(wout.arrays)
    videos = onehot.shape[0]

    def body(s, residual_ref, hidden_ref, onehot_ref, *rest):
        pieces, rest = rest[:count], rest[count:]
        out_ref, sum_ref, out_w, means, sems = rest
        f = pl.program_id(0)

        @pl.when(f == 0)
        def _():
            run_copies(wout.copies(pieces, s[0], sems, 0, features, out_w))
            means[...] = jnp.zeros_like(means)

        output = residual_ref[0] + nn(hidden_ref[0], out_w[...])
        out_ref[0] = output[:patches].astype(bf16)
        valid = lax.broadcasted_iota(jnp.int32, (ROWS, 1), 0) < patches
        means[pl.ds(f, 1), :] = jnp.sum(
            jnp.where(valid, output, 0.0), axis=0, keepdims=True
        ) * (1.0 / patches)

        @pl.when(f == n - 1)
        def _():
            sum_ref[...] = nn(onehot_ref[...], means[...], HIGH) * (1.0 / FPV)

    return call(
        body,
        [sds((n, patches, features), bf16), sds((videos, features), f32)],
        (n,),
        [per_step((ROWS, features)), per_step((ROWS, hidden_units)), whole((videos, 8))]
        + [ANY] * count,
        [per_step((patches, features)), whole((videos, features))],
        [
            pltpu.VMEM((hidden_units, features), bf16),
            pltpu.VMEM((8, features), f32),
            pltpu.SemaphoreType.DMA((count,)),
        ],
        2 * n * ROWS * features * hidden_units,
        20 * 1024 * 1024,
        deps,
    )(meta, residual, hidden, onehot, *wout.arrays)


def contrast(meta, pooled, ids_column, ids_row, onehot, group_videos, patches, deps=()):
    total, features = pooled.shape
    pad = onehot.shape[0]
    videos = total // pad * group_videos
    weight = float(videos * FPV * patches)

    def body(s, pooled_ref, column_ref, row_ref, onehot_ref, loss_ref, grad_ref, all_ref, back):
        rows = lax.broadcasted_iota(jnp.int32, (total, 1), 0)
        lanes = lax.broadcasted_iota(jnp.int32, (1, total), 1)
        row_valid = lax.rem(rows, pad) < group_videos
        lane_valid = lax.rem(lanes, pad) < group_videos
        row_one = row_valid.astype(f32)
        values = jnp.where(row_valid, pooled_ref[...], 0.0)
        centred = (values - jnp.sum(values, axis=0, keepdims=True) / videos) * row_one
        scale = lax.rsqrt(jnp.sum(centred * centred, axis=1, keepdims=True) + 1e-06)
        embed = centred * scale
        logits = LOGIT_SCALE * nt(embed, embed, HIGH)
        other = jnp.logical_and(rows != lanes, jnp.logical_and(row_valid, lane_valid))
        masked = jnp.where(other, logits, -1e30)
        top = jnp.max(masked, axis=1, keepdims=True)
        e = jnp.where(other, jnp.exp(masked - top), 0.0)
        e_sum = jnp.sum(e, axis=1, keepdims=True)
        e_sum = jnp.where(row_valid, e_sum, 1.0)
        positive = jnp.logical_and(column_ref[:, :1] == row_ref[:1, :], other).astype(f32)
        counts = jnp.sum(positive, axis=1, keepdims=True)
        counts = jnp.where(row_valid, counts, 1.0)
        means = jnp.sum(positive * logits, axis=1, keepdims=True) / counts
        terms = jnp.where(row_valid, top + jnp.log(e_sum) - means, 0.0)
        loss_ref[...] = jnp.broadcast_to(
            jnp.sum(terms, axis=0, keepdims=True) / videos, loss_ref.shape
        )
        logit_grad = (e / e_sum - positive / counts) * (weight / videos)
        embed_grad = LOGIT_SCALE * (
            nn(logit_grad, embed, HIGH)
            + lax.dot_general(
                logit_grad, embed, (((0,), (0,)), ((), ())),
                preferred_element_type=f32, precision=HIGH,
            )
        )
        along = jnp.sum(embed_grad * embed, axis=1, keepdims=True)
        centred_grad = scale * (embed_grad - embed * along) * row_one
        back[...] = (
            centred_grad - jnp.sum(centred_grad, axis=0, keepdims=True) / videos
        ) * row_one
        own = back[pl.ds(pl.multiple_of(s[1] * pad, 8), pad), :]
        grad_ref[...] = lax.dot_general(
            onehot_ref[...], own, (((0,), (0,)), ((), ())),
            preferred_element_type=f32, precision=HIGH,
        ) * (1.0 / (FPV * patches))
        all_ref[...] = back[...] * (1.0 / (FPV * patches))

    return call(
        body,
        [sds((8, 128), f32), sds((8, features), f32), sds(pooled.shape, f32)],
        (1,),
        [whole(pooled.shape), whole(ids_column.shape), whole(ids_row.shape), whole(onehot.shape)],
        [whole((8, 128)), whole((8, features)), whole(pooled.shape)],
        [pltpu.VMEM(pooled.shape, f32)],
        10**6,
        10**6,
        deps,
    )(meta, pooled, ids_column, ids_row, onehot)


def mlp_backward(meta, cotangent, frame_grad, pre, residual, params, win, wout, deps=()):
    n, patches, features = cotangent.shape
    hidden_units = pre.shape[2]
    count_in, count_out = len(win.arrays), len(wout.arrays)
    chunks = hidden_units // features

    def body(s, cot_ref, fg_ref, pre_ref, residual_ref, params_ref, *rest):
        in_pieces, rest = rest[:count_in], rest[count_in:]
        out_pieces, rest = rest[:count_out], rest[count_out:]
        pre_grad_ref, residual_grad_ref, low_ref, norm_ref = rest[:4]
        in_w, out_w, output_grad, in_sems, out_sems = rest[4:]
        f = pl.program_id(0)

        @pl.when(f == 0)
        def _():
            first = wout.copies(out_pieces, s[0], out_sems, 0, features, out_w)
            for copy in first + win.copies(in_pieces, s[0], in_sems, 0, hidden_units, in_w):
                copy.start()
            for copy in first:
                copy.wait()
            output_grad[...] = jnp.zeros_like(output_grad)
            norm_ref[...] = jnp.zeros_like(norm_ref)

        output_grad[0:patches] = cot_ref[0].astype(f32) + fg_ref[pl.ds(f, 1), :]
        branch = output_grad[...].astype(bf16)
        normed = jnp.zeros((ROWS, features), f32)
        for c in range(chunks):
            columns = slice(c * features, (c + 1) * features)
            hidden_grad = nt(branch, out_w[columns, :])
            u = pre_ref[0, :, columns].astype(f32)
            sig = sigmoid(1.702 * u)
            slope = sig * (1.0 + 1.702 * u * (1.0 - sig))
            pre_grad = (hidden_grad * slope).astype(bf16)
            pre_grad_ref[0, :, columns] = pre_grad
            if c == 0:

                @pl.when(f == 0)
                def _():
                    for copy in win.copies(in_pieces, s[0], in_sems, 0, hidden_units, in_w):
                        copy.wait()

            normed = normed + nt(pre_grad, in_w[:, columns])
        xhat, rstd = norm_parts(residual_ref[0])
        norm_ref[0:1] += jnp.sum(normed * xhat, axis=0, keepdims=True)
        norm_ref[1:2] += jnp.sum(normed, axis=0, keepdims=True)
        residual_grad = output_grad[...] + norm_back(normed, xhat, rstd, params_ref[4:5])
        residual_grad_ref[0] = residual_grad
        low_ref[0] = residual_grad.astype(bf16)

    return call(
        body,
        [
            sds((n, ROWS, hidden_units), bf16),
            sds((n, ROWS, features), f32),
            sds((n, ROWS, features), bf16),
            sds((8, features), f32),
        ],
        (n,),
        [
            per_step((patches, features)),
            whole((8, features)),
            per_step((ROWS, hidden_units)),
            per_step((ROWS, features)),
            whole((16, features)),
        ]
        + [ANY] * (count_in + count_out),
        [
            per_step((ROWS, hidden_units)),
            per_step((ROWS, features)),
            per_step((ROWS, features)),
            whole((8, features)),
        ],
        [
            pltpu.VMEM((features, hidden_units), bf16),
            pltpu.VMEM((hidden_units, features), bf16),
            pltpu.VMEM((ROWS, features), f32),
            pltpu.SemaphoreType.DMA((count_in,)),
            pltpu.SemaphoreType.DMA((count_out,)),
        ],
        4 * n * ROWS * features * hidden_units,
        36 * 1024 * 1024,
        deps,
    )(meta, cotangent, frame_grad, pre, residual, params, *win.arrays, *wout.arrays)


def message_token_backward(
    meta, low, mixed, qkv, probs, total, params, weights, out_weights, patches, wide, deps=()
):
    n, _, features = low.shape
    count, count_out = len(weights.arrays), len(out_weights.arrays)
    base = patches // 16 * 16

    def body(s, low_ref, mixed_ref, qkv_ref, probs_ref, total_ref, params_ref, *rest):
        pieces, rest = rest[:count], rest[count:]
        out_pieces, rest = rest[:count_out], rest[count_out:]
        grad_ref, total_grad_ref, kv_w, out_w, heads, rows, table, sems = rest
        f = pl.program_id(0)

        @pl.when(f == 0)
        def _():
            run_copies(out_weights.copies(out_pieces, s[0], sems.at[0], 0, features, out_w))
            for copy in weights.copies(pieces, s[0], sems.at[1], features, 2 * features, kv_w):
                copy.start()
            rows[...] = jnp.zeros_like(rows)
            table[...] = jnp.zeros_like(table)
            head = lax.broadcasted_iota(jnp.int32, (features, 128), 0) // (features // HEADS)
            lane = lax.broadcasted_iota(jnp.int32, (features, 128), 1)
            heads[...] = (head == lane).astype(f32).astype(bf16)

        mixed_grad = nt(low_ref[0], out_w[...]).astype(bf16)
        grad_ref[0] = mixed_grad
        mixed_grad = mixed_grad.astype(f32)
        dots = nn((mixed_grad * mixed_ref[0].astype(f32)).astype(bf16), heads[...])
        here = slice(patches - base, patches - base + 1)
        value = qkv_ref[0, base : base + 16, 2 * features :].astype(f32)[here]
        prob_grad = nn((mixed_grad * value).astype(bf16), heads[...])
        for p in range(HEADS // 2):
            for j in range(2):
                table[2 * p + j : 2 * p + j + 1] = probs_ref[0, p, j].astype(f32)[here]
        probs = jnp.transpose(table[...])
        score_grad = (probs * (prob_grad - dots)).astype(bf16)
        queries = qkv_ref[0, :, :features].astype(f32) * 0.125
        key_grad = jnp.sum(nt(score_grad, heads[...]) * queries, axis=0, keepdims=True)
        value_grad = jnp.sum(
            nt(probs.astype(bf16), heads[...]) * mixed_grad, axis=0, keepdims=True
        )
        rows[pl.ds(f, 1), :] = jnp.concatenate([key_grad, value_grad], axis=1)

        @pl.when(f == n - 1)
        def _():
            for copy in weights.copies(pieces, s[0], sems.at[1], features, 2 * features, kv_w):
                copy.wait()
            pre_grad = nt(rows[...].astype(bf16), kv_w[...])
            xhat, rstd = norm_parts(total_ref[...])
            total_grad_ref[...] = jnp.zeros_like(total_grad_ref)
            total_grad_ref[0:8] = norm_back(pre_grad, xhat, rstd, params_ref[2:3]).astype(bf16)

    return call(
        body,
        [sds((n, ROWS, features), bf16), sds((wide, features), bf16)],
        (n,),
        [
            per_step((ROWS, features)),
            per_step((ROWS, features)),
            per_step((ROWS, 3 * features)),
            pl.BlockSpec(
                (1, HEADS // 2, 2, 16, ROWS), lambda i, s: (i, 0, 0, base // 16, 0)
            ),
            whole((8, features)),
            whole((16, features)),
        ]
        + [ANY] * (count + count_out),
        [per_step((ROWS, features)), whole((wide, features))],
        [
            pltpu.VMEM((features, 2 * features), bf16),
            pltpu.VMEM((features, features), bf16),
            pltpu.VMEM((features, 128), bf16),
            pltpu.VMEM((8, 2 * features), f32),
            pltpu.VMEM((128, ROWS), f32),
            pltpu.SemaphoreType.DMA((2, max(count, count_out))),
        ],
        2 * n * ROWS * features * (features + 512),
        16 * 1024 * 1024,
        deps,
    )(meta, low, mixed, qkv, probs, total, params, *weights.arrays, *out_weights.arrays)


def attention_backward(meta, mixed_grad, qkv, probs, deps=()):
    n, _, features = mixed_grad.shape

    def body(s, mixed_grad_ref, qkv_ref, probs_ref, grad_ref):
        for p in range(HEADS // 2):
            q2, k2, v2 = (
                qkv_ref[0, :, part * features + p * 128 : part * features + (p + 1) * 128]
                for part in range(3)
            )
            grads = pair_back(
                q2, k2, v2, mixed_grad_ref[0, :, p * 128 : (p + 1) * 128],
                probs_ref[0, p, 0], probs_ref[0, p, 1],
            )
            for part, grad in enumerate(grads):
                columns = slice(part * features + p * 128, part * features + (p + 1) * 128)
                grad_ref[0, :, columns] = grad.astype(bf16)

    return call(
        body,
        sds((n, ROWS, 3 * features), bf16),
        (n,),
        [
            per_step((ROWS, features)),
            per_step((ROWS, 3 * features)),
            per_step((HEADS // 2, 2, ROWS, ROWS)),
        ],
        per_step((ROWS, 3 * features)),
        [],
        2 * n * ROWS * 6 * ROWS * features,
        24 * 1024 * 1024,
        deps,
    )(meta, mixed_grad, qkv, probs)


def stacked_backward(meta, qkv_grad, frames, total, residual_grad, params, weights, deps=()):
    n, patches, features = frames.shape
    count = len(weights.arrays)

    def body(s, grad_ref, frames_ref, total_ref, residual_grad_ref, params_ref, *rest):
        pieces, rest = rest[:count], rest[count:]
        frames_grad_ref, first_ref, norm_ref, qkv_w, stacked, sems = rest
        f = pl.program_id(0)

        @pl.when(f == 0)
        def _():
            run_copies(weights.copies(pieces, s[0], sems, 0, 3 * features, qkv_w))
            stacked[...] = jnp.zeros_like(stacked)
            norm_ref[...] = jnp.zeros_like(norm_ref)
            first_ref[...] = jnp.zeros_like(first_ref)

        stacked[0:patches] = frames_ref[0].astype(f32)
        stacked[patches : patches + 1] = total_ref[pl.ds(f, 1), :]
        pre_grad = nt(grad_ref[0], qkv_w[...])
        xhat, rstd = norm_parts(stacked[...])
        norm_ref[0:1] += jnp.sum(pre_grad * xhat, axis=0, keepdims=True)
        norm_ref[1:2] += jnp.sum(pre_grad, axis=0, keepdims=True)
        stacked[...] = norm_back(pre_grad, xhat, rstd, params_ref[2:3]) + residual_grad_ref[0]
        frames_grad_ref[0] = stacked[0:patches].astype(bf16)
        first_ref[pl.ds(f, 1), :] = stacked[0:1]
        stacked[patches : patches + 1] = jnp.zeros((1, features), f32)
        stacked[patches + 1 :] = jnp.zeros((ROWS - patches - 1, features), f32)

    return call(
        body,
        [
            sds((n, patches, features), bf16),
            sds((8, features), f32),
            sds((8, features), f32),
        ],
        (n,),
        [
            per_step((ROWS, 3 * features)),
            per_step((patches, features)),
            whole((8, features)),
            per_step((ROWS, features)),
            whole((16, features)),
        ]
        + [ANY] * count,
        [
            per_step((patches, features)),
            whole((8, features)),
            whole((8, features)),
        ],
        [
            pltpu.VMEM((features, 3 * features), bf16),
            pltpu.VMEM((ROWS, features), f32),
            pltpu.SemaphoreType.DMA((count,)),
        ],
        1,
        1,
        deps,
    )(meta, qkv_grad, frames, total, residual_grad, params, *weights.arrays)


def message_backward(meta, total_grad, cls, act, proj, mix, message, params, weights, rows, deps=()):
    total, features = act.shape
    chunk = min(total, 256)
    steps = total // chunk
    count = len(weights.arrays)

    def body(s, tg_ref, cls_ref, act_ref, proj_ref, mix_ref, message_ref, params_ref, *rest):
        pieces, rest = rest[:count], rest[count:]
        fc_ref, qkv_ref, out_ref, norm_ref, class_ref = rest[:5]
        fc_w, qkv_w, out_w, grads, low, fc_sum, qkv_sum, out_sum, sems = rest[5:]
        step = pl.program_id(0)

        @pl.when(step == 0)
        def _():
            copies = []
            for number, (first, columns, dst) in enumerate(
                (
                    (5 * features, features, out_w),
                    (2 * features, 3 * features, qkv_w),
                    (features, features, fc_w),
                )
            ):
                copies += weights.copies(pieces, s[0], sems.at[number], first, columns, dst)
            run_copies(copies)
            norm_ref[...] = jnp.zeros_like(norm_ref)
            fc_sum[...] = jnp.zeros_like(fc_sum)
            qkv_sum[...] = jnp.zeros_like(qkv_sum)
            out_sum[...] = jnp.zeros_like(out_sum)

        pick = (
            lax.broadcasted_iota(jnp.int32, (features, 128), 0)
            == lax.broadcasted_iota(jnp.int32, (features, 128), 1) + s[0] * rows
        ).astype(f32).astype(bf16)

        def own_rows(values):
            return jnp.transpose(nn(values, pick)).astype(bf16)[:rows]

        ids = cls_ref[:, features:].astype(f32)
        same = ids[:, :1] == jnp.transpose(ids)[:1, :]
        tg = tg_ref[...]
        mix_grad = nt(tg, out_w[...]).astype(bf16)
        for p in range(HEADS // 2):
            q2, k2, v2 = (
                proj_ref[:, part * features + p * 128 : part * features + (p + 1) * 128]
                for part in range(3)
            )
            p0, p1 = pair_probs(q2, k2, same)
            parts = pair_back(q2, k2, v2, mix_grad[:, p * 128 : (p + 1) * 128], p0, p1)
            for part, grad in enumerate(parts):
                grads[:, part * features + p * 128 : part * features + (p + 1) * 128] = (
                    grad.astype(bf16)
                )
        out_sum[...] += nn(own_rows(mix_ref[...]), tg)
        qkv_sum[...] += nn(own_rows(act_ref[...]), grads[...])
        normed = nt(grads[...], qkv_w[...])
        xhat, rstd = norm_parts(message_ref[...])
        norm_ref[0:1] += jnp.sum(normed * xhat, axis=0, keepdims=True)
        norm_ref[1:2] += jnp.sum(normed, axis=0, keepdims=True)
        message_grad = tg.astype(f32) + norm_back(normed, xhat, rstd, params_ref[0:1])
        low[...] = message_grad
        fc_sum[...] += nn(own_rows(cls_ref[:, :features]), message_grad.astype(bf16))

        @pl.when(step == s[2])
        def _():
            own = low[pl.ds(pl.multiple_of(s[3], 8), 8), :].astype(bf16)
            class_ref[...] = nt(own, fc_w[...])

        @pl.when(step == steps - 1)
        def _():
            fc_ref[...] = fc_sum[...].astype(bf16)
            qkv_ref[...] = qkv_sum[...].astype(bf16)
            out_ref[...] = out_sum[...].astype(bf16)

    def block(columns):
        return pl.BlockSpec((chunk, columns), lambda i, s: (i, 0))

    return call(
        body,
        [
            sds((rows, features), bf16),
            sds((rows, 3 * features), bf16),
            sds((rows, features), bf16),
            sds((8, features), f32),
            sds((8, features), f32),
        ],
        (steps,),
        [
            block(features),
            block(features + PACK),
            block(features),
            block(3 * features),
            block(features),
            block(features),
            whole((16, features)),
        ]
        + [ANY] * count,
        [
            whole((rows, features)),
            whole((rows, 3 * features)),
            whole((rows, features)),
            whole((8, features)),
            whole((8, features)),
        ],
        [
            pltpu.VMEM((features, features), bf16),
            pltpu.VMEM((features, 3 * features), bf16),
            pltpu.VMEM((features, features), bf16),
            pltpu.VMEM((chunk, 3 * features), bf16),
            pltpu.VMEM((chunk, features), f32),
            pltpu.VMEM((rows, features), f32),
            pltpu.VMEM((rows, 3 * features), f32),
            pltpu.VMEM((rows, features), f32),
            pltpu.SemaphoreType.DMA((3, count)),
        ],
        1,
        1,
        deps,
    )(meta, total_grad, cls, act, proj, mix, message, params, *weights.arrays)


def chip_slot(chip, x_first):
    if not x_first:
        return chip
    return ((chip & 1) << 1) | (chip >> 1)


def scatter_rows(s, product, rows, fast, mp, refs, x_first):
    if not fast:
        for d in range(mp):
            refs[0][d] = product[d * rows : (d + 1) * rows].astype(bf16)
        return
    even = (s[0] & 1) == 0
    for pair in range(mp // 2):
        low = product[2 * pair * rows : (2 * pair + 1) * rows].astype(bf16)
        high = product[(2 * pair + 1) * rows : (2 * pair + 2) * rows].astype(bf16)
        slot = chip_slot(jnp.bitwise_xor(s[0] >> 1, pair), x_first)
        refs[0][slot] = jnp.where(even, low, high)
        refs[1][slot] = jnp.where(even, high, low)


def weight_grad(meta, jobs, outs, rows, fast, mp, x_first, deps=()):
    features = jobs[0][0].shape[1]
    tokens = jobs[0][0].shape[0]
    steps = len(jobs)
    copies = 2 if fast else 1
    lefts, rights = [], []
    for left, right, _, _, _ in jobs:
        if all(left is not x for x in lefts):
            lefts.append(left)
        if all(right is not x for x in rights):
            rights.append(right)
    left_of = [next(i for i, x in enumerate(lefts) if x is job[0]) for job in jobs]
    right_of = [next(i for i, x in enumerate(rights) if x is job[1]) for job in jobs]

    def body(s, *refs):
        left_refs, refs = refs[: len(lefts)], refs[len(lefts) :]
        right_refs, refs = refs[: len(rights)], refs[len(rights) :]
        out_refs, scratch = refs[: copies * len(outs)], refs[-1]
        step = pl.program_id(0)
        for number in range(len(lefts)):

            @pl.when(step == left_of.index(number))
            def _(number=number):
                scratch[...] = transpose(left_refs[number][...])

        for number in range(len(rights)):
            for target in range(len(outs)):
                mine = [
                    i for i in range(steps) if right_of[i] == number and jobs[i][3] == target
                ]
                if not mine:
                    continue

                @pl.when(jnp.logical_and(step >= mine[0], step <= mine[-1]))
                def _(number=number, target=target):
                    product = nn(scratch[...], right_refs[number][...])
                    scatter_rows(
                        s, product, rows, fast, mp,
                        out_refs[copies * target : copies * (target + 1)],
                        x_first[target],
                    )

    def index_map(values, make):
        def pick(i, s):
            index = values[0]
            for number in range(1, steps):
                index = jnp.where(i >= number, values[number], index)
            return make(index)

        return pick

    def held(number, of, column):
        values, last = [], None
        for i in range(steps):
            if of[i] == number:
                last = jobs[i][column]
            values.append(last)
        first = next(v for v in values if v is not None)
        return [first if v is None else v for v in values]

    in_specs = [whole((tokens, features)) for _ in lefts]
    for number in range(len(rights)):
        in_specs.append(
            pl.BlockSpec(
                (tokens, features),
                index_map(held(number, right_of, 2), lambda index: (0, index)),
            )
        )
    out_of = [job[3] for job in jobs]
    out_specs, out_shape = [], []
    lead = mp // 2 if fast else mp
    for target, columns in enumerate(outs):
        spec = pl.BlockSpec(
            (lead, rows, features),
            index_map(held(target, out_of, 4), lambda index: (0, 0, index)),
        )
        for _ in range(copies):
            out_specs.append(spec)
            out_shape.append(sds((lead, rows, columns), bf16))
    results = call(
        body,
        out_shape,
        (steps,),
        in_specs,
        out_specs,
        [pltpu.VMEM((features, tokens), bf16)],
        2 * steps * tokens * features * features,
        (2 * steps + 1) * tokens * features * 2,
        deps,
    )(meta, *lefts, *rights)
    grouped = [results[copies * t : copies * (t + 1)] for t in range(len(outs))]
    if not fast:
        return grouped
    return [[x.reshape((2, 2) + x.shape[1:]) for x in pair] for pair in grouped]


def hidden_weight_grad(meta, cotangent, hidden, ids, all_videos, rows, mp, deps=()):
    n, patches, features = cotangent.shape
    tokens = n * ROWS
    count = features + all_videos
    wide = features + -(-all_videos // 128) * 128
    blocks = features // rows if rows % 128 == 0 else 0
    width = features

    def body(s, cot_ref, ids_ref, hidden_ref, *refs):
        left, scratch = refs[-2:]

        @pl.when(pl.program_id(0) == 0)
        def _():
            lane = lax.broadcasted_iota(jnp.int32, (patches, wide - features), 1)
            left[...] = jnp.zeros_like(left)
            for f in range(n):
                here = slice(f * ROWS, f * ROWS + patches)
                left[here, :features] = cot_ref[f].astype(f32)
                left[here, features:] = (lane == ids_ref[f : f + 1, :1]).astype(f32)
            scratch[...] = jnp.transpose(left[...]).astype(bf16)

        product = nn(scratch[...], hidden_ref[...]).astype(bf16)[:count]
        for d in range(blocks):
            refs[0][d] = product[:, d * rows : (d + 1) * rows]
        if not blocks:
            refs[0][...] = product

    if blocks:
        out_spec = pl.BlockSpec((blocks, count, rows), lambda i, s: (i, 0, 0))
        out_shape = sds((mp, count, rows), bf16)
    else:
        out_spec = pl.BlockSpec((count, width), lambda i, s: (0, i))
        out_shape = sds((count, hidden.shape[1]), bf16)
    results = call(
        body,
        [out_shape],
        (hidden.shape[1] // width,),
        [
            whole((n, patches, features)),
            whole((8, 128)),
            pl.BlockSpec((tokens, width), lambda i, s: (0, i)),
        ],
        [out_spec],
        [pltpu.VMEM((tokens, wide), f32), pltpu.VMEM((wide, tokens), bf16)],
        2 * tokens * features * hidden.shape[1],
        (hidden.shape[1] + features) * tokens * 2,
        deps,
    )(meta, cotangent, ids, hidden)
    if blocks:
        return results[0]
    return results[0].reshape(count, mp, rows).transpose(1, 0, 2)


def local(
    videos,
    mp,
    frames,
    cotangent,
    frame_video,
    group_ids,
    message_fc,
    message_gain,
    message_shift,
    message_qkv,
    message_out,
    pre_gain,
    pre_shift,
    attn_qkv,
    attn_out,
    mlp_gain,
    mlp_shift,
    fc_in,
    fc_out,
):
    n, patches, features = frames.shape
    rows = message_fc.shape[0]
    fast = (videos, mp) == (4, 8)
    z = lax.axis_index("videos")
    me = lax.axis_index("mp")
    group_videos = frame_video.shape[0] // FPV
    pad_videos = -(-group_videos // 8) * 8
    device_rows = 8 * (z * mp + me)
    meta = jnp.stack([me, z, device_rows // 256, lax.rem(device_rows, 256)]).astype(jnp.int32)

    own_video = lax.dynamic_slice_in_dim(frame_video, me * n, n)
    own_video = jnp.concatenate([own_video, jnp.full((8 - n,), -1, own_video.dtype)])
    onehot = (
        (own_video - z * group_videos)[None, :] == jnp.arange(pad_videos)[:, None]
    ).astype(f32)
    norms = jnp.concatenate(
        [message_gain, message_shift, pre_gain, pre_shift, mlp_gain, mlp_shift]
    )
    cls = jnp.concatenate(
        [
            jnp.concatenate(
                [
                    frames[:, 0, :],
                    jnp.pad(norms, (0, features - 6 * rows))[None, :],
                    jnp.zeros((7 - n, features), bf16),
                ]
            ),
            jnp.broadcast_to(own_video.astype(bf16)[:, None], (8, PACK)),
        ],
        axis=1,
    )
    qkv_w = gather_weights(attn_qkv, fast, mp)
    cls_steps = gather_small(tie(cls, *qkv_w.arrays[2:4]), fast, videos, mp)
    next(cls_steps)
    small = next(cls_steps)
    next(cls_steps)
    norms = next(cls_steps)[:, n, : 6 * rows].reshape(mp, 6, rows).transpose(1, 0, 2)
    params = jnp.pad(norms.reshape(6, features).astype(f32), ((0, 10), (0, 0)))
    pre_act, qkv = frame_projection(meta, frames, params, qkv_w)
    early = qkv_w.arrays[4:6] + [small] if fast else ()
    message_w = gather_weights(
        pack_columns(meta, [[attn_out, message_fc, message_qkv, message_out]])[0],
        fast, mp, first=early, relay=[qkv],
    )
    in_w = gather_whole(fc_in, mp, early)
    out_w = gather_whole(fc_out, mp, early)
    cls_steps.send([qkv])
    next(cls_steps)
    cls_all = next(cls_steps)
    all_videos = videos * pad_videos
    own_place = jnp.where(own_video < 0, -1, own_video - z * group_videos + z * pad_videos)
    ids = jnp.pad(group_ids.reshape(videos, group_videos), ((0, 0), (0, pad_videos - group_videos)))
    ids = ids.reshape(-1)
    places = jnp.broadcast_to(own_place.astype(jnp.int32)[:, None], (8, 128))
    ids_column = jnp.broadcast_to(ids[:, None], (ids.shape[0], 128))
    ids_row = jnp.broadcast_to(ids[None, :], (8, ids.shape[0]))
    msg_act, msg_proj, msg_mix, message, msg_total = message_forward(
        meta, cls_all, params, message_w, [places, ids_column, ids_row, onehot]
    )
    own_total = lax.dynamic_slice_in_dim(msg_total, device_rows, 8)
    attn_act, attn_proj, probs, mixed, residual = attention_forward(
        meta, frames, own_total, params, pre_act, qkv, qkv_w, message_w
    )
    pre_act, qkv = attn_act, attn_proj
    mlp_act, hidden_pre, hidden = mlp_in(meta, residual, params, in_w)
    out_parts = hidden_weight_grad(
        meta, cotangent, hidden.reshape(n * ROWS, -1),
        places,
        all_videos, fc_out.shape[0], mp,
    )
    out_share = scatter_sum(out_parts)
    out_frames, video_part = mlp_out(
        meta, residual, hidden, onehot, out_w, patches, [out_parts]
    )
    pooled = gather_videos(sum_small(video_part, fast, mp), fast, videos)
    loss, frame_grad, video_grad = contrast(
        meta,
        pooled,
        ids_column,
        ids_row,
        onehot,
        group_videos,
        patches,
    )
    pre_grad, residual_grad, low, mlp_norm = mlp_backward(
        meta, cotangent, frame_grad, hidden_pre, residual, params, in_w, out_w
    )
    flat = lambda a: a.reshape(n * ROWS, a.shape[-1])
    act_flat, pre_flat = flat(mlp_act), flat(pre_grad)
    halves = [2 * features, fc_in.shape[1] - 2 * features]
    in_parts = weight_grad(
        meta,
        [
            (act_flat, pre_flat, c, c // 2, c % 2)
            for c in range(fc_in.shape[1] // features)
        ],
        halves, rows, fast, mp, (True, False), [out_share],
    )
    in_reds = [Reduce(x, fast, videos, mp, i == 0) for i, x in enumerate(in_parts)]

    def in_step(*after):
        return [red.step(after) for red in in_reds]

    in_1 = in_step()
    out_along = Along([tie(out_share, pre_grad)], fast, videos)
    out_1 = out_along.step()
    wide = -(-(1 << 20) // (mp * features * 2 * 8)) * 8
    mixed_grad, total_grad = message_token_backward(
        meta, low, mixed, qkv, probs, own_total, params, qkv_w, message_w, patches, wide,
        [in_parts[0][0]] + out_1,
    )
    grads_plane = lax.all_gather(
        total_grad, "mp", axis=0, tiled=False
    )
    out_2 = out_along.step()
    in_2 = in_step(mixed_grad)
    sent = [red.sent for red in in_reds] if fast else []
    qkv_grad = attention_backward(meta, mixed_grad, qkv, probs, in_1 + out_2 + sent)
    grads_plane = tie(grads_plane, qkv_grad)[:, :8].reshape(mp * 8, features)
    grads_all = gather_along(grads_plane, fast, videos)
    in_3 = in_step(qkv_grad)
    next(grads_all)
    grads_1 = next(grads_all)
    stacked_flat, qkv_flat, mixed_flat, low_flat = map(flat, (pre_act, qkv_grad, mixed, low))
    ((attn_parts,),) = weight_grad(
        meta,
        [(stacked_flat, qkv_flat, c, 0, c) for c in range(3)] + [(mixed_flat, low_flat, 0, 0, 3)],
        [4 * features], rows, False, mp, (True,), in_2,
    )
    attn_share = scatter_sum(attn_parts)
    in_4 = in_step(attn_parts)
    grads_2 = grads_all.send([attn_parts])
    frames_grad, first_token, pre_norm = stacked_backward(
        meta, qkv_grad, frames, own_total, residual_grad, params, qkv_w, [grads_1, attn_parts]
    )
    norms_all = sum_all(
        jnp.concatenate([pre_norm[:2], mlp_norm[:2], jnp.zeros((4, features), f32)], axis=0),
        fast, videos, mp,
    )
    norms_1, norms_2 = next(norms_all), next(norms_all)
    total_grads = grads_all.send([frames_grad])
    grad_message_fc, grad_message_qkv, grad_message_out, message_norm, class_grad = (
        message_backward(
            meta, total_grads, cls_all, msg_act, msg_proj, msg_mix, message, params, message_w,
            rows, in_3 + [norms_1],
        )
    )
    norms_all.send([class_grad])
    in_5 = in_step(frames_grad)
    norm_sums = next(norms_all)[:4]
    grad_fc_in = jnp.concatenate([red.result([class_grad]) for red in in_reds], axis=1)
    (grad_fc_out,) = out_along.result([class_grad])
    attn_share = tie(attn_share, class_grad)
    attn_along = Along([attn_share[:, : 2 * features], attn_share[:, 2 * features :]], fast, videos)
    attn_along.step(), attn_along.step()
    first_grad, second_grad = attn_along.result()
    grad_fc_out = grad_fc_out[:features] + lax.dot_general(
        video_grad, grad_fc_out[features:], (((0,), (0,)), ((), ())), precision=HIGH
    )
    tokens = (first_token + class_grad)[:n].astype(bf16)
    frames_grad = lax.dynamic_update_slice(frames_grad, tokens[:, None, :], (0, 0, 0))
    norm_all = jnp.concatenate([message_norm[:2], norm_sums], axis=0)
    norm_own = lax.dynamic_slice_in_dim(norm_all, me * rows, rows, 1).astype(bf16)
    return (
        out_frames,
        loss[0, 0],
        frames_grad,
        grad_message_fc,
        norm_own[0],
        norm_own[1],
        grad_message_qkv,
        grad_message_out,
        norm_own[2],
        norm_own[3],
        jnp.concatenate([first_grad, second_grad[:, :features]], axis=1).astype(bf16),
        second_grad[:, features:].astype(bf16),
        norm_own[4],
        norm_own[5],
        grad_fc_in.astype(bf16),
        grad_fc_out.T.astype(bf16),
    )


def solution(mesh):
    weight, norm = P("mp", None), P("mp")
    frame = P(("videos", "mp"), None, None)
    params = (
        weight, norm, norm, weight, weight, norm, norm, weight, weight, norm, norm, weight, weight,
    )
    return jax.shard_map(
        functools.partial(local, mesh.shape["videos"], mesh.shape["mp"]),
        mesh=mesh,
        in_specs=(frame, frame, P("videos"), P()) + params,
        out_specs=(frame, P(), frame) + params,
        check_vma=False,
    )
```
